32 devices in a mesh: seq: 8 (over z, x), tp: 4 (over y, core).
Axes of the slice: x: 2, y: 2, z: 4, core: 2. Of those that a mesh axis runs over, the one named last changes fastest.
Arguments:
- tokens: bfloat16 [4096, 768], P(('seq', 'tp')), may hold values from -6 to 6
- cotangent: bfloat16 [4096, 768], P(('seq', 'tp')), may hold values from -6 to 6
- prefix_length: int32 [1], replicated, may hold values from 0 to 2047
- mask_flags: int32 [4096], P(('seq', 'tp')), may hold values 0 or 1
- timestep: int32 [1], replicated, may hold values from 0 to 999
- mask_embed: bfloat16 [768], replicated, may hold values from -6 to 6
- ln1_gain: bfloat16 [768], replicated, may hold values from 0.099609375 to 1.8984375
- ln2_gain: bfloat16 [768], replicated, may hold values from 0.099609375 to 1.8984375
- ada_weight: bfloat16 [128, 4608], replicated, may hold values from -0.5 to 0.5
- ada_bias: bfloat16 [4608], replicated, may hold values from -3 to 3
- qkv_weight: bfloat16 [768, 2304], replicated, may hold values from -0.21875 to 0.21875
- out_weight: bfloat16 [768, 768], replicated, may hold values from -2 to 2
- up_weight: bfloat16 [768, 3072], P(None, 'tp'), may hold values from -0.21875 to 0.21875
- up_bias: bfloat16 [3072], P('tp'), may hold values from -3 to 3
- down_weight: bfloat16 [3072, 768], P('tp'), may hold values from -0.109375 to 0.109375
- down_bias: bfloat16 [768], replicated, may hold values from -3 to 3
Outputs:
- output: bfloat16 [4096, 768], P(('seq', 'tp'))
- input_grad: float32 [4096, 768], P(('seq', 'tp'))
- mask_embed_grad: float32 [768], replicated
- ln1_gain_grad: float32 [768], replicated
- ln2_gain_grad: float32 [768], replicated
- ada_weight_grad: float32 [128, 4608], replicated
- ada_bias_grad: float32 [4608], replicated
- qkv_weight_grad: float32 [768, 2304], replicated
- out_weight_grad: float32 [768, 768], replicated
- up_weight_grad: float32 [768, 3072], P(None, 'tp')
- up_bias_grad: float32 [3072], P('tp')
- down_weight_grad: float32 [3072, 768], P('tp')
- down_bias_grad: float32 [768], replicated
The draws below stay inside these ranges and needn't reach their ends.
All inputs are finite; a program needn't handle non-finite values. No bound on the sum of `mask_flags` on one device may be relied on, other than what follows from the above.
Results may differ from the reference program's by a relative error of at most 0.019.
Values may be sent and summed in bfloat16 or wider, within the bound.
A program may use at most 384 MiB of HBM per device.

```python
import math
import jax
import jax.numpy as jnp
from jax import lax

D = 768
HEADS = 12
HEAD_DIM = 64
FF = 3072
COND = 128
SEQ_LEN = 4096


def set_ends(entries, key, low, high):
    spot = [jax.random.randint(jax.random.fold_in(key, axis), (), 0, length) for axis, length in enumerate(entries.shape)]
    widest = entries.shape.index(max(entries.shape))
    next_to = spot[:widest] + [(spot[widest] + 1) % entries.shape[widest]] + spot[widest + 1:]
    return entries.at[tuple(spot)].set(low).at[tuple(next_to)].set(high)


def steps_of(key, shape, cuts, smallest, largest):
    level, own = 1.0, jax.random.fold_in(key, 6)
    for axis_at, parts in cuts:
        steps = jnp.exp(jax.random.uniform(jax.random.fold_in(own, axis_at), (parts,), jnp.float32, smallest / len(cuts), largest / len(cuts)))
        level = level * jnp.repeat(steps, shape[axis_at] // parts).reshape([-1 if axis == axis_at else 1 for axis in range(len(shape))])
    return level


def gaussian(rng, shape, spread, limit, pieces=(), kind=jnp.bfloat16):
    loudness = steps_of(rng, shape, pieces, -0.22, 0.18) if pieces else 1.0
    values = jax.random.normal(rng, shape, jnp.float32) * spread * loudness
    return jnp.minimum(jnp.maximum(values, -limit), limit).astype(kind)


def setup_inputs(seed: int = 0) -> dict:
    key_list = jax.random.split(jax.random.key(seed), 17)
    tokens = gaussian(key_list[0], (SEQ_LEN, D), 1.0, 6.0, ((0, 32),))
    cotangent = gaussian(key_list[1], (SEQ_LEN, D), 1.0, 6.0, ((0, 32),))
    prefix_length = jax.random.randint(key_list[2], (1,), 0, SEQ_LEN // 2).astype(jnp.int32)
    mask_flags = set_ends((jax.random.randint(key_list[3], (SEQ_LEN,), 0, 2) < 1).astype(jnp.int32), jax.random.fold_in(key_list[3], 1), 0, 1)
    timestep = jax.random.randint(key_list[4], (1,), 0, 1000).astype(jnp.int32)
    mask_embed = gaussian(key_list[5], (D,), 1.0, 6.0)
    ln1_gain = jnp.clip(1.0 + 0.18 * jax.random.normal(key_list[6], (D,), jnp.float32), 0.099609375, 1.8984375).astype(jnp.bfloat16)
    ln2_gain = jnp.clip(1.0 + 0.18 * jax.random.normal(key_list[7], (D,), jnp.float32), 0.099609375, 1.8984375).astype(jnp.bfloat16)
    ada_weight = gaussian(key_list[8], (COND, 6 * D), COND ** -0.5, 0.5)
    ada_bias = gaussian(key_list[9], (6 * D,), 0.5, 3.0)
    qkv_weight = gaussian(key_list[10], (D, 3 * D), D ** -0.5, 0.21875)
    out_weight = gaussian(key_list[11], (D, D), (max(1, D * D // (16 * SEQ_LEN))) ** -0.5, 2.0)
    up_weight = gaussian(key_list[12], (D, FF), D ** -0.5, 0.21875, ((1, 4),))
    up_bias = gaussian(key_list[13], (FF,), 0.5, 3.0, ((0, 4),))
    down_weight = gaussian(key_list[14], (FF, D), FF ** -0.5, 0.109375, ((0, 4),))
    down_bias = gaussian(key_list[15], (D,), 0.5, 3.0)
    return {"tokens": tokens, "cotangent": cotangent, "prefix_length": prefix_length, "mask_flags": mask_flags, "timestep": timestep, "mask_embed": mask_embed, "ln1_gain": ln1_gain, "ln2_gain": ln2_gain, "ada_weight": ada_weight, "ada_bias": ada_bias, "qkv_weight": qkv_weight, "out_weight": out_weight, "up_weight": up_weight, "up_bias": up_bias, "down_weight": down_weight, "down_bias": down_bias}


@jax.custom_vjp
def low(v):
    return lax.optimization_barrier(v.astype(jnp.bfloat16)).astype(jnp.float32)

@jax.custom_vjp
def low_back(v):
    return v

def low_keep(v):
    return (low(v), None)

def low_pass(kept, grad):
    return (grad,)

def back_keep(v):
    return (v, None)

def back_low(kept, grad):
    return (low(grad),)
low.defvjp(low_keep, low_pass)
low_back.defvjp(back_keep, back_low)
epsilon = 1e-05
highest = lax.Precision.HIGHEST

def layer_norm(inputs, norm_gain):
    centred = inputs - lax.optimization_barrier(jnp.mean(inputs, axis=-1, keepdims=True))
    variance = lax.optimization_barrier(jnp.mean(centred * centred, axis=-1, keepdims=True))
    return centred * lax.rsqrt(variance + epsilon) * norm_gain

def modulate(inputs, norm_gain, shift_vector, scale_vector):
    return layer_norm(inputs, norm_gain) * (1.0 + scale_vector) + shift_vector

def rotary_tables(positions, head_width):
    halfway = head_width // 2
    inverse = jnp.exp(-math.log(10000.0) * jnp.arange(halfway, dtype=jnp.float32) / halfway)
    angles = positions.astype(jnp.float32)[:, None] * inverse[None, :]
    angles = jnp.concatenate([angles, angles], axis=1)
    return (jnp.cos(angles), jnp.sin(angles))

def rotate(head_rows, cosine, sine):
    halfway = head_rows.shape[-1] // 2
    turned = jnp.concatenate([-head_rows[..., halfway:], head_rows[..., :halfway]], axis=-1)
    return head_rows * cosine[:, None, :] + turned * sine[:, None, :]

def time_embedding(timestep, embed_width):
    halfway = embed_width // 2
    rates = jnp.exp(-math.log(10000.0) * jnp.arange(halfway, dtype=jnp.float32) / halfway)
    angles = timestep[0].astype(jnp.float32) * rates
    return jnp.concatenate([jnp.cos(angles), jnp.sin(angles)])

def attention(queries, key_heads, value_heads):
    block_size = math.gcd(SEQ_LEN, 512)
    score_scale = HEAD_DIM ** (-0.5)
    blocks = queries.reshape(SEQ_LEN // block_size, block_size, HEADS, HEAD_DIM)

    @jax.checkpoint
    def one_block(query_block):
        scores = low_back(jnp.einsum('qhd,khd->hqk', query_block, key_heads, precision=highest) * score_scale)
        shifted = scores - lax.optimization_barrier(jnp.max(scores, axis=-1, keepdims=True))
        weights = jnp.exp(shifted)
        probs = low(weights / lax.optimization_barrier(jnp.sum(weights, axis=-1, keepdims=True)))
        return jnp.einsum('hqk,khd->qhd', probs, value_heads, precision=highest)
    return lax.map(one_block, blocks).reshape(SEQ_LEN, HEADS * HEAD_DIM)

def reference(tokens, cotangent, prefix_length, mask_flags, timestep, mask_embed, ln1_gain, ln2_gain, ada_weight, ada_bias, qkv_weight, out_weight, up_weight, up_bias, down_weight, down_bias):
    positions = jnp.arange(SEQ_LEN, dtype=jnp.int32)
    masked = ((positions >= prefix_length[0]) & (mask_flags == 1)).astype(jnp.float32)
    activation = jax.nn.silu(time_embedding(timestep, COND))
    cosine, sine = rotary_tables(positions, HEAD_DIM)

    def forward(params):
        inputs, embed_row, gain_one, gain_two, ada_matrix, ada_offset, qkv_matrix, out_matrix, up_matrix, up_offset, down_matrix, down_offset = params
        modulation = jnp.dot(activation, ada_matrix, precision=highest) + ada_offset
        shift_one, scale_one, gate_one, shift_two, scale_two, gate_two = jnp.split(modulation, 6)
        start = inputs + masked[:, None] * embed_row[None, :]
        normed = low(modulate(start, gain_one, shift_one, scale_one))
        projected = low_back(jnp.dot(normed, qkv_matrix, precision=highest))
        split_rows = projected.reshape(SEQ_LEN, 3, HEADS, HEAD_DIM)
        queries = low(rotate(split_rows[:, 0], cosine, sine))
        key_heads = low(rotate(split_rows[:, 1], cosine, sine))
        value_heads = low(split_rows[:, 2])
        mixed = low_back(low(attention(queries, key_heads, value_heads)))
        branch = low_back(jnp.dot(mixed, out_matrix, precision=highest))
        middle = start + gate_one * branch
        normed_two = low(modulate(middle, gain_two, shift_two, scale_two))
        hidden = low_back(jnp.dot(normed_two, up_matrix, precision=highest) + up_offset)
        active = low(jax.nn.gelu(hidden))
        result = low_back(jnp.dot(active, down_matrix, precision=highest) + down_offset)
        return middle + gate_two * result
    params = tuple((array.astype(jnp.float32) for array in (tokens, mask_embed, ln1_gain, ln2_gain, ada_weight, ada_bias, qkv_weight, out_weight, up_weight, up_bias, down_weight, down_bias)))
    output, pullback = jax.vjp(forward, params)
    grads, = pullback(cotangent.astype(jnp.float32))
    return (output.astype(jnp.bfloat16), grads[0], grads[1], grads[2], grads[3], grads[4], grads[5], grads[6], grads[7], grads[8], grads[9], grads[10], grads[11])
```

```python
import math

import jax
import jax.numpy as jnp
from jax import lax
from jax.sharding import PartitionSpec as P

HEADS = 12


epsilon = 1e-05
highest = lax.Precision.HIGHEST
floor_value = -1e30


def layer_norm(inputs, norm_gain):
    centred = inputs - jnp.mean(inputs, axis=-1, keepdims=True)
    variance = jnp.mean(centred * centred, axis=-1, keepdims=True)
    return centred * lax.rsqrt(variance + epsilon) * norm_gain


def modulate(inputs, norm_gain, shift_vector, scale_vector):
    return layer_norm(inputs, norm_gain) * (1.0 + scale_vector) + shift_vector


def rotary_tables(positions, head_width):
    halfway = head_width // 2
    inverse = jnp.exp(-math.log(10000.0) * jnp.arange(halfway, dtype=jnp.float32) / halfway)
    angles = positions.astype(jnp.float32)[:, None] * inverse[None, :]
    angles = jnp.concatenate([angles, angles], axis=1)
    return (jnp.cos(angles), jnp.sin(angles))


def rotate(head_rows, cosine, sine):
    halfway = head_rows.shape[-1] // 2
    turned = jnp.concatenate([-head_rows[..., halfway:], head_rows[..., :halfway]], axis=-1)
    return head_rows * cosine[:, None, :] + turned * sine[:, None, :]


def time_embedding(timestep, embed_width):
    halfway = embed_width // 2
    rates = jnp.exp(-math.log(10000.0) * jnp.arange(halfway, dtype=jnp.float32) / halfway)
    angles = timestep[0].astype(jnp.float32) * rates
    return jnp.concatenate([jnp.cos(angles), jnp.sin(angles)])


def block_length(total_rows, other_count):
    pieces = total_rows // other_count
    widest = 1 << max(0, (2048 // other_count).bit_length() - 1)
    size = other_count * math.gcd(pieces, widest)
    return size


def over_blocks(running, row_arrays, other_count, advance):
    total_rows = row_arrays[0].shape[0]
    block_size = block_length(total_rows, other_count)

    def one_turn(block_index, current):
        block_start = block_index * block_size
        blocks = tuple(
            (lax.dynamic_slice_in_dim(array, block_start, block_size, 0) for array in row_arrays)
        )
        return advance(current, blocks)

    return lax.fori_loop(0, total_rows // block_size, one_turn, running)


def forward_update(running, queries, key_block, value_block, score_scale):
    highest_seen, totals, weighted = running
    scores = (
        jnp.einsum("qhd,khd->hqk", queries, key_block, preferred_element_type=jnp.float32)
        * score_scale
    )
    new_highest = jnp.maximum(highest_seen, jnp.max(scores, axis=-1))
    factor = jnp.exp(highest_seen - new_highest)
    weights = jnp.exp(scores - new_highest[:, :, None])
    totals = totals * factor + jnp.sum(weights, axis=-1)
    weighted = weighted * factor.T[:, :, None] + jnp.einsum(
        "hqk,khd->qhd",
        weights.astype(jnp.bfloat16),
        value_block,
        preferred_element_type=jnp.float32,
    )
    return (new_highest, totals, weighted)


def query_update(
    query_grad, queries, mixed_grad, logsum, delta, key_block, value_block, score_scale
):
    scores = (
        jnp.einsum("qhd,khd->hqk", queries, key_block, preferred_element_type=jnp.float32)
        * score_scale
    )
    probs = jnp.exp(scores - logsum[:, :, None])
    prob_grad = jnp.einsum(
        "qhd,khd->hqk", mixed_grad, value_block, preferred_element_type=jnp.float32
    )
    score_grad = (probs * (prob_grad - delta[:, :, None])).astype(jnp.bfloat16)
    return query_grad + score_scale * jnp.einsum(
        "hqk,khd->qhd", score_grad, key_block, preferred_element_type=jnp.float32
    )


def key_update(
    running, query_block, grad_block, logsum_block, delta_block, own_keys, own_values, score_scale
):
    key_grad, value_grad = running
    scores = (
        jnp.einsum("qhd,khd->hqk", query_block, own_keys, preferred_element_type=jnp.float32)
        * score_scale
    )
    probs = jnp.exp(scores - logsum_block.T[:, :, None])
    value_grad = value_grad + jnp.einsum(
        "hqk,qhd->khd", probs.astype(jnp.bfloat16), grad_block, preferred_element_type=jnp.float32
    )
    prob_grad = jnp.einsum(
        "qhd,khd->hqk", grad_block, own_values, preferred_element_type=jnp.float32
    )
    score_grad = (probs * (prob_grad - delta_block.T[:, :, None])).astype(jnp.bfloat16)
    key_grad = key_grad + score_scale * jnp.einsum(
        "hqk,qhd->khd", score_grad, query_block, preferred_element_type=jnp.float32
    )
    return (key_grad, value_grad)


def to_heads(rows):
    return lax.all_to_all(rows, "tp", split_axis=1, concat_axis=0, tiled=True)


def to_rows(rows):
    return lax.all_to_all(rows, "tp", split_axis=0, concat_axis=1, tiled=True)


def per_device(
    tokens,
    cotangent,
    prefix_length,
    mask_flags,
    timestep,
    mask_embed,
    ln1_gain,
    ln2_gain,
    ada_weight,
    ada_bias,
    qkv_weight,
    out_weight,
    up_weight,
    up_bias,
    down_weight,
    down_bias,
):
    row_count = tokens.shape[0]
    model_width = tokens.shape[1]
    head_count = HEADS
    head_width = model_width // head_count
    score_scale = head_width ** (-0.5)
    positions = lax.axis_index(("seq", "tp")) * row_count + jnp.arange(row_count, dtype=jnp.int32)
    masked = ((positions >= prefix_length[0]) & (mask_flags == 1)).astype(jnp.float32)
    activation = jax.nn.silu(time_embedding(timestep, ada_weight.shape[0]))
    modulation = jnp.dot(
        activation, ada_weight.astype(jnp.float32), precision=highest
    ) + ada_bias.astype(jnp.float32)
    shift_one, scale_one, gate_one, shift_two, scale_two, gate_two = jnp.split(modulation, 6)
    cosine, sine = rotary_tables(positions, head_width)
    gain_one = ln1_gain.astype(jnp.float32)
    gain_two = ln2_gain.astype(jnp.float32)
    start = tokens.astype(jnp.float32) + masked[:, None] * mask_embed.astype(jnp.float32)[None, :]
    normed = modulate(start, gain_one, shift_one, scale_one).astype(jnp.bfloat16)
    projected = jnp.dot(normed, qkv_weight, preferred_element_type=jnp.float32)
    split_rows = projected.reshape(row_count, 3, head_count, head_width)
    queries, key_rows, value_rows = (
        to_heads(rows.reshape(row_count, model_width).astype(jnp.bfloat16))
        for rows in (
            rotate(split_rows[:, 0], cosine, sine),
            rotate(split_rows[:, 1], cosine, sine),
            split_rows[:, 2],
        )
    )
    group_size, group_width = queries.shape
    head_group = group_width // head_width
    queries = queries.reshape(group_size, head_group, head_width)
    every_key = lax.all_gather(key_rows, "seq", axis=0, tiled=True)
    every_value = lax.all_gather(value_rows, "seq", axis=0, tiled=True)
    initial = (
        jnp.full((head_group, group_size), floor_value, jnp.float32),
        jnp.zeros((head_group, group_size), jnp.float32),
        jnp.zeros((group_size, head_group, head_width), jnp.float32),
    )

    def advance(current, blocks):
        return forward_update(
            current,
            queries,
            blocks[0].reshape(-1, head_group, head_width),
            blocks[1].reshape(-1, head_group, head_width),
            score_scale,
        )

    running = over_blocks(
        initial,
        (every_key, every_value),
        group_size,
        advance,
    )
    highest_seen, totals, weighted = running
    logsum = highest_seen + jnp.log(totals)
    attended = weighted / totals.T[:, :, None]
    mixed = to_rows(attended.reshape(group_size, group_width).astype(jnp.bfloat16))
    branch = jnp.dot(mixed, out_weight, preferred_element_type=jnp.float32)
    middle = start + gate_one * branch
    normed_two = modulate(middle, gain_two, shift_two, scale_two).astype(jnp.bfloat16)
    group_rows = lax.all_gather(normed_two, "tp", axis=0, tiled=True)
    hidden = jnp.dot(group_rows, up_weight, preferred_element_type=jnp.float32) + up_bias.astype(
        jnp.float32
    )
    active = jax.nn.gelu(hidden).astype(jnp.bfloat16)
    result = lax.psum_scatter(
        jnp.dot(active, down_weight, preferred_element_type=jnp.float32).astype(jnp.bfloat16),
        "tp",
        scatter_dimension=0,
        tiled=True,
    ).astype(jnp.float32) + down_bias.astype(jnp.float32)
    output = (middle + gate_two * result).astype(jnp.bfloat16)
    upstream = cotangent.astype(jnp.float32)
    result_grad = (upstream * gate_two).astype(jnp.bfloat16)
    gate_two_grad = jnp.sum(upstream * result, axis=0)
    down_bias_grad = jnp.sum(result_grad.astype(jnp.float32), axis=0)
    group_grads = lax.all_gather(result_grad, "tp", axis=0, tiled=True)
    down_weight_grad = jnp.dot(active.T, group_grads, preferred_element_type=jnp.float32)
    active_grad = jnp.dot(group_grads, down_weight.T, preferred_element_type=jnp.float32)
    unused, gelu_back = jax.vjp(jax.nn.gelu, hidden)
    hidden_grad = gelu_back(active_grad)[0].astype(jnp.bfloat16)
    up_bias_grad = jnp.sum(hidden_grad.astype(jnp.float32), axis=0)
    up_weight_grad = jnp.dot(group_rows.T, hidden_grad, preferred_element_type=jnp.float32)
    normed_two_grad = lax.psum_scatter(
        jnp.dot(hidden_grad, up_weight.T, preferred_element_type=jnp.float32).astype(jnp.bfloat16),
        "tp",
        scatter_dimension=0,
        tiled=True,
    ).astype(jnp.float32)
    unused, second_back = jax.vjp(modulate, middle, gain_two, shift_two, scale_two)
    middle_part, gain_two_grad, shift_two_grad, scale_two_grad = second_back(normed_two_grad)
    middle_grad = middle_part + upstream
    gate_one_grad = jnp.sum(middle_grad * branch, axis=0)
    branch_grad = (middle_grad * gate_one).astype(jnp.bfloat16)
    out_weight_grad = jnp.dot(mixed.T, branch_grad, preferred_element_type=jnp.float32)
    mixed_grad = to_heads(
        jnp.dot(branch_grad, out_weight.T, preferred_element_type=jnp.float32).astype(jnp.bfloat16)
    ).reshape(group_size, head_group, head_width)
    delta_rows = jnp.sum(mixed_grad.astype(jnp.float32) * attended, axis=-1)
    delta = delta_rows.T
    initial_query = jnp.zeros((group_size, head_group, head_width), jnp.float32)

    def advance(grads_now, blocks):
        return query_update(
            grads_now,
            queries,
            mixed_grad,
            logsum,
            delta,
            blocks[0].reshape(-1, head_group, head_width),
            blocks[1].reshape(-1, head_group, head_width),
            score_scale,
        )

    query_grad = over_blocks(
        initial_query,
        (every_key, every_value),
        group_size,
        advance,
    )
    every_logsum, every_delta = (
        lax.all_gather(logsum.T, "seq", axis=0, tiled=True),
        lax.all_gather(delta_rows, "seq", axis=0, tiled=True),
    )
    own_keys = key_rows.reshape(group_size, head_group, head_width)
    own_values = value_rows.reshape(group_size, head_group, head_width)
    initial_keys = (
        jnp.zeros((group_size, head_group, head_width), jnp.float32),
        jnp.zeros((group_size, head_group, head_width), jnp.float32),
    )

    def advance(grads_now, blocks):
        return key_update(
            grads_now,
            blocks[0].reshape(-1, head_group, head_width),
            blocks[1].reshape(-1, head_group, head_width),
            blocks[2],
            blocks[3],
            own_keys,
            own_values,
            score_scale,
        )

    key_grad, value_grad = over_blocks(
        initial_keys,
        (
            lax.all_gather(queries.reshape(group_size, group_width), "seq", axis=0, tiled=True),
            lax.all_gather(mixed_grad.reshape(group_size, group_width), "seq", axis=0, tiled=True),
            every_logsum,
            every_delta,
        ),
        group_size,
        advance,
    )
    query_rows, key_part_rows, value_grad_rows = (
        to_rows(rows.reshape(group_size, group_width)).reshape(row_count, head_count, head_width)
        for rows in (query_grad, key_grad, value_grad)
    )
    unused, rotate_back = jax.vjp(lambda head_rows: rotate(head_rows, cosine, sine), query_rows)
    query_part = rotate_back(query_rows)[0].reshape(row_count, model_width)
    key_part = rotate_back(key_part_rows)[0].reshape(row_count, model_width)
    projected_grad = jnp.concatenate(
        [query_part, key_part, value_grad_rows.reshape(row_count, model_width)], axis=1
    ).astype(jnp.bfloat16)
    qkv_weight_grad = jnp.dot(normed.T, projected_grad, preferred_element_type=jnp.float32)
    normed_grad = jnp.dot(projected_grad, qkv_weight.T, preferred_element_type=jnp.float32)
    unused, first_back = jax.vjp(modulate, start, gain_one, shift_one, scale_one)
    start_part, gain_one_grad, shift_one_grad, scale_one_grad = first_back(normed_grad)
    start_grad = start_part + middle_grad
    embed_grad = jnp.sum(masked[:, None] * start_grad, axis=0)
    modulation_grad = jnp.concatenate(
        [
            shift_one_grad,
            scale_one_grad,
            gate_one_grad,
            shift_two_grad,
            scale_two_grad,
            gate_two_grad,
        ]
    )
    summed = lax.psum(
        (
            qkv_weight_grad,
            out_weight_grad,
            modulation_grad,
            gain_one_grad,
            gain_two_grad,
            down_bias_grad,
            embed_grad,
        ),
        ("seq", "tp"),
    )
    split_sums = lax.psum((up_weight_grad, up_bias_grad, down_weight_grad), "seq")
    return (
        output,
        start_grad,
        summed[6],
        summed[3],
        summed[4],
        activation[:, None] * summed[2][None, :],
        summed[2],
        summed[0],
        summed[1],
        split_sums[0],
        split_sums[1],
        split_sums[2],
        summed[5],
    )


def solution(mesh):
    in_specs = (
        P(("seq", "tp"), None),
        P(("seq", "tp"), None),
        P(),
        P(("seq", "tp")),
        P(),
        P(),
        P(),
        P(),
        P(),
        P(),
        P(),
        P(),
        P(None, "tp"),
        P("tp"),
        P("tp", None),
        P(),
    )
    out_specs = (
        P(("seq", "tp"), None),
        P(("seq", "tp"), None),
        P(),
        P(),
        P(),
        P(),
        P(),
        P(),
        P(),
        P(None, "tp"),
        P("tp"),
        P("tp", None),
        P(),
    )
    return jax.shard_map(
        per_device, mesh=mesh, in_specs=in_specs, out_specs=out_specs, check_vma=False
    )
```

```python
import functools
import math

import jax
import jax.numpy as jnp
import numpy as np
from jax import lax
from jax.experimental import pallas as pl
from jax.experimental.pallas import tpu as pltpu
from jax.sharding import PartitionSpec as P

HEADS = 12


epsilon = 1e-05
highest = lax.Precision.HIGHEST
floor_value = -1e30


def layer_norm(inputs, norm_gain):
    centred = inputs - jnp.mean(inputs, axis=-1, keepdims=True)
    variance = jnp.mean(centred * centred, axis=-1, keepdims=True)
    return centred * lax.rsqrt(variance + epsilon) * norm_gain


def modulate(inputs, norm_gain, shift_vector, scale_vector):
    return layer_norm(inputs, norm_gain) * (1.0 + scale_vector) + shift_vector


def rotary_tables(positions, head_width):
    halfway = head_width // 2
    inverse = jnp.exp(-math.log(10000.0) * jnp.arange(halfway, dtype=jnp.float32) / halfway)
    angles = positions.astype(jnp.float32)[:, None] * inverse[None, :]
    angles = jnp.concatenate([angles, angles], axis=1)
    return (jnp.cos(angles), jnp.sin(angles))


def rotate(head_rows, cosine, sine):
    halfway = head_rows.shape[-1] // 2
    turned = jnp.concatenate([-head_rows[..., halfway:], head_rows[..., :halfway]], axis=-1)
    return head_rows * cosine[:, None, :] + turned * sine[:, None, :]


def time_embedding(timestep, embed_width):
    halfway = embed_width // 2
    rates = jnp.exp(-math.log(10000.0) * jnp.arange(halfway, dtype=jnp.float32) / halfway)
    angles = timestep[0].astype(jnp.float32) * rates
    return jnp.concatenate([jnp.cos(angles), jnp.sin(angles)])


def block_length(total_rows, other_count):
    pieces = total_rows // other_count
    widest = 1 << max(0, (2048 // other_count).bit_length() - 1)
    size = other_count * math.gcd(pieces, widest)
    return size


def over_blocks(running, row_arrays, other_count, advance):
    total_rows = row_arrays[0].shape[0]
    block_size = block_length(total_rows, other_count)

    def one_turn(block_index, current):
        block_start = block_index * block_size
        blocks = tuple(
            (lax.dynamic_slice_in_dim(array, block_start, block_size, 0) for array in row_arrays)
        )
        return advance(current, blocks)

    return lax.fori_loop(0, total_rows // block_size, one_turn, running)


def forward_update(running, queries, key_block, value_block, score_scale):
    highest_seen, totals, weighted = running
    scores = (
        jnp.einsum("qhd,khd->hqk", queries, key_block, preferred_element_type=jnp.float32)
        * score_scale
    )
    new_highest = jnp.maximum(highest_seen, jnp.max(scores, axis=-1))
    factor = jnp.exp(highest_seen - new_highest)
    weights = jnp.exp(scores - new_highest[:, :, None])
    totals = totals * factor + jnp.sum(weights, axis=-1)
    weighted = weighted * factor.T[:, :, None] + jnp.einsum(
        "hqk,khd->qhd",
        weights.astype(jnp.bfloat16),
        value_block,
        preferred_element_type=jnp.float32,
    )
    return (new_highest, totals, weighted)


def query_update(
    query_grad, queries, mixed_grad, logsum, delta, key_block, value_block, score_scale
):
    scores = (
        jnp.einsum("qhd,khd->hqk", queries, key_block, preferred_element_type=jnp.float32)
        * score_scale
    )
    probs = jnp.exp(scores - logsum[:, :, None])
    prob_grad = jnp.einsum(
        "qhd,khd->hqk", mixed_grad, value_block, preferred_element_type=jnp.float32
    )
    score_grad = (probs * (prob_grad - delta[:, :, None])).astype(jnp.bfloat16)
    return query_grad + score_scale * jnp.einsum(
        "hqk,khd->qhd", score_grad, key_block, preferred_element_type=jnp.float32
    )


def key_update(
    running, query_block, grad_block, logsum_block, delta_block, own_keys, own_values, score_scale
):
    key_grad, value_grad = running
    scores = (
        jnp.einsum("qhd,khd->hqk", query_block, own_keys, preferred_element_type=jnp.float32)
        * score_scale
    )
    probs = jnp.exp(scores - logsum_block.T[:, :, None])
    value_grad = value_grad + jnp.einsum(
        "hqk,qhd->khd", probs.astype(jnp.bfloat16), grad_block, preferred_element_type=jnp.float32
    )
    prob_grad = jnp.einsum(
        "qhd,khd->hqk", grad_block, own_values, preferred_element_type=jnp.float32
    )
    score_grad = (probs * (prob_grad - delta_block.T[:, :, None])).astype(jnp.bfloat16)
    key_grad = key_grad + score_scale * jnp.einsum(
        "hqk,qhd->khd", score_grad, query_block, preferred_element_type=jnp.float32
    )
    return (key_grad, value_grad)


def to_heads(rows):
    return lax.all_to_all(rows, "tp", split_axis=1, concat_axis=0, tiled=True)


def to_rows(rows):
    return lax.all_to_all(rows, "tp", split_axis=0, concat_axis=1, tiled=True)


def per_device(
    tokens,
    cotangent,
    prefix_length,
    mask_flags,
    timestep,
    mask_embed,
    ln1_gain,
    ln2_gain,
    ada_weight,
    ada_bias,
    qkv_weight,
    out_weight,
    up_weight,
    up_bias,
    down_weight,
    down_bias,
):
    row_count = tokens.shape[0]
    model_width = tokens.shape[1]
    head_count = HEADS
    head_width = model_width // head_count
    score_scale = head_width ** (-0.5)
    positions = lax.axis_index(("seq", "tp")) * row_count + jnp.arange(row_count, dtype=jnp.int32)
    masked = ((positions >= prefix_length[0]) & (mask_flags == 1)).astype(jnp.float32)
    activation = jax.nn.silu(time_embedding(timestep, ada_weight.shape[0]))
    modulation = jnp.dot(
        activation, ada_weight.astype(jnp.float32), precision=highest
    ) + ada_bias.astype(jnp.float32)
    shift_one, scale_one, gate_one, shift_two, scale_two, gate_two = jnp.split(modulation, 6)
    cosine, sine = rotary_tables(positions, head_width)
    gain_one = ln1_gain.astype(jnp.float32)
    gain_two = ln2_gain.astype(jnp.float32)
    start = tokens.astype(jnp.float32) + masked[:, None] * mask_embed.astype(jnp.float32)[None, :]
    normed = modulate(start, gain_one, shift_one, scale_one).astype(jnp.bfloat16)
    projected = jnp.dot(normed, qkv_weight, preferred_element_type=jnp.float32)
    split_rows = projected.reshape(row_count, 3, head_count, head_width)
    queries, key_rows, value_rows = (
        to_heads(rows.reshape(row_count, model_width).astype(jnp.bfloat16))
        for rows in (
            rotate(split_rows[:, 0], cosine, sine),
            rotate(split_rows[:, 1], cosine, sine),
            split_rows[:, 2],
        )
    )
    group_size, group_width = queries.shape
    head_group = group_width // head_width
    queries = queries.reshape(group_size, head_group, head_width)
    every_key = lax.all_gather(key_rows, "seq", axis=0, tiled=True)
    every_value = lax.all_gather(value_rows, "seq", axis=0, tiled=True)
    initial = (
        jnp.full((head_group, group_size), floor_value, jnp.float32),
        jnp.zeros((head_group, group_size), jnp.float32),
        jnp.zeros((group_size, head_group, head_width), jnp.float32),
    )

    def advance(current, blocks):
        return forward_update(
            current,
            queries,
            blocks[0].reshape(-1, head_group, head_width),
            blocks[1].reshape(-1, head_group, head_width),
            score_scale,
        )

    running = over_blocks(
        initial,
        (every_key, every_value),
        group_size,
        advance,
    )
    highest_seen, totals, weighted = running
    logsum = highest_seen + jnp.log(totals)
    attended = weighted / totals.T[:, :, None]
    mixed = to_rows(attended.reshape(group_size, group_width).astype(jnp.bfloat16))
    branch = jnp.dot(mixed, out_weight, preferred_element_type=jnp.float32)
    middle = start + gate_one * branch
    normed_two = modulate(middle, gain_two, shift_two, scale_two).astype(jnp.bfloat16)
    group_rows = lax.all_gather(normed_two, "tp", axis=0, tiled=True)
    hidden = jnp.dot(group_rows, up_weight, preferred_element_type=jnp.float32) + up_bias.astype(
        jnp.float32
    )
    active = jax.nn.gelu(hidden).astype(jnp.bfloat16)
    result = lax.psum_scatter(
        jnp.dot(active, down_weight, preferred_element_type=jnp.float32).astype(jnp.bfloat16),
        "tp",
        scatter_dimension=0,
        tiled=True,
    ).astype(jnp.float32) + down_bias.astype(jnp.float32)
    output = (middle + gate_two * result).astype(jnp.bfloat16)
    upstream = cotangent.astype(jnp.float32)
    result_grad = (upstream * gate_two).astype(jnp.bfloat16)
    gate_two_grad = jnp.sum(upstream * result, axis=0)
    down_bias_grad = jnp.sum(result_grad.astype(jnp.float32), axis=0)
    group_grads = lax.all_gather(result_grad, "tp", axis=0, tiled=True)
    down_weight_grad = jnp.dot(active.T, group_grads, preferred_element_type=jnp.float32)
    active_grad = jnp.dot(group_grads, down_weight.T, preferred_element_type=jnp.float32)
    unused, gelu_back = jax.vjp(jax.nn.gelu, hidden)
    hidden_grad = gelu_back(active_grad)[0].astype(jnp.bfloat16)
    up_bias_grad = jnp.sum(hidden_grad.astype(jnp.float32), axis=0)
    up_weight_grad = jnp.dot(group_rows.T, hidden_grad, preferred_element_type=jnp.float32)
    normed_two_grad = lax.psum_scatter(
        jnp.dot(hidden_grad, up_weight.T, preferred_element_type=jnp.float32).astype(jnp.bfloat16),
        "tp",
        scatter_dimension=0,
        tiled=True,
    ).astype(jnp.float32)
    unused, second_back = jax.vjp(modulate, middle, gain_two, shift_two, scale_two)
    middle_part, gain_two_grad, shift_two_grad, scale_two_grad = second_back(normed_two_grad)
    middle_grad = middle_part + upstream
    gate_one_grad = jnp.sum(middle_grad * branch, axis=0)
    branch_grad = (middle_grad * gate_one).astype(jnp.bfloat16)
    out_weight_grad = jnp.dot(mixed.T, branch_grad, preferred_element_type=jnp.float32)
    mixed_grad = to_heads(
        jnp.dot(branch_grad, out_weight.T, preferred_element_type=jnp.float32).astype(jnp.bfloat16)
    ).reshape(group_size, head_group, head_width)
    delta_rows = jnp.sum(mixed_grad.astype(jnp.float32) * attended, axis=-1)
    delta = delta_rows.T
    initial_query = jnp.zeros((group_size, head_group, head_width), jnp.float32)

    def advance(grads_now, blocks):
        return query_update(
            grads_now,
            queries,
            mixed_grad,
            logsum,
            delta,
            blocks[0].reshape(-1, head_group, head_width),
            blocks[1].reshape(-1, head_group, head_width),
            score_scale,
        )

    query_grad = over_blocks(
        initial_query,
        (every_key, every_value),
        group_size,
        advance,
    )
    every_logsum, every_delta = (
        lax.all_gather(logsum.T, "seq", axis=0, tiled=True),
        lax.all_gather(delta_rows, "seq", axis=0, tiled=True),
    )
    own_keys = key_rows.reshape(group_size, head_group, head_width)
    own_values = value_rows.reshape(group_size, head_group, head_width)
    initial_keys = (
        jnp.zeros((group_size, head_group, head_width), jnp.float32),
        jnp.zeros((group_size, head_group, head_width), jnp.float32),
    )

    def advance(grads_now, blocks):
        return key_update(
            grads_now,
            blocks[0].reshape(-1, head_group, head_width),
            blocks[1].reshape(-1, head_group, head_width),
            blocks[2],
            blocks[3],
            own_keys,
            own_values,
            score_scale,
        )

    key_grad, value_grad = over_blocks(
        initial_keys,
        (
            lax.all_gather(queries.reshape(group_size, group_width), "seq", axis=0, tiled=True),
            lax.all_gather(mixed_grad.reshape(group_size, group_width), "seq", axis=0, tiled=True),
            every_logsum,
            every_delta,
        ),
        group_size,
        advance,
    )
    query_rows, key_part_rows, value_grad_rows = (
        to_rows(rows.reshape(group_size, group_width)).reshape(row_count, head_count, head_width)
        for rows in (query_grad, key_grad, value_grad)
    )
    unused, rotate_back = jax.vjp(lambda head_rows: rotate(head_rows, cosine, sine), query_rows)
    query_part = rotate_back(query_rows)[0].reshape(row_count, model_width)
    key_part = rotate_back(key_part_rows)[0].reshape(row_count, model_width)
    projected_grad = jnp.concatenate(
        [query_part, key_part, value_grad_rows.reshape(row_count, model_width)], axis=1
    ).astype(jnp.bfloat16)
    qkv_weight_grad = jnp.dot(normed.T, projected_grad, preferred_element_type=jnp.float32)
    normed_grad = jnp.dot(projected_grad, qkv_weight.T, preferred_element_type=jnp.float32)
    unused, first_back = jax.vjp(modulate, start, gain_one, shift_one, scale_one)
    start_part, gain_one_grad, shift_one_grad, scale_one_grad = first_back(normed_grad)
    start_grad = start_part + middle_grad
    embed_grad = jnp.sum(masked[:, None] * start_grad, axis=0)
    modulation_grad = jnp.concatenate(
        [
            shift_one_grad,
            scale_one_grad,
            gate_one_grad,
            shift_two_grad,
            scale_two_grad,
            gate_two_grad,
        ]
    )
    summed = lax.psum(
        (
            qkv_weight_grad,
            out_weight_grad,
            modulation_grad,
            gain_one_grad,
            gain_two_grad,
            down_bias_grad,
            embed_grad,
        ),
        ("seq", "tp"),
    )
    split_sums = lax.psum((up_weight_grad, up_bias_grad, down_weight_grad), "seq")
    return (
        output,
        start_grad,
        summed[6],
        summed[3],
        summed[4],
        activation[:, None] * summed[2][None, :],
        summed[2],
        summed[0],
        summed[1],
        split_sums[0],
        split_sums[1],
        split_sums[2],
        summed[5],
    )


VMEM_LIMIT = 63 * 2**20
GROUPS = 4
CHIPS = 4
MESH = pl.DeviceIdType.MESH
f32, bf16 = jnp.float32, jnp.bfloat16


def dot(left, right, left_dim, right_dim):
    return lax.dot_general(
        left, right, (((left_dim,), (right_dim,)), ((), ())), preferred_element_type=f32
    )


def normalise(rows):
    centred = rows - jnp.mean(rows, axis=-1, keepdims=True)
    variance = jnp.mean(centred * centred, axis=-1, keepdims=True)
    spread = lax.rsqrt(variance + epsilon)
    return centred * spread, spread


def normalise_back(upstream, normal, spread):
    along = jnp.mean(upstream * normal, axis=-1, keepdims=True)
    return spread * (upstream - jnp.mean(upstream, axis=-1, keepdims=True) - normal * along)


def column_sum(rows):
    return jnp.sum(rows, axis=0, keepdims=True)


def row_of(ref, i, width):
    return ref[i * width : (i + 1) * width].astype(f32).reshape(1, width)


def activation_of(step, first, count, cond):
    halfway = cond // 2
    place = first + lax.broadcasted_iota(jnp.int32, (count, 1), 0)
    which = jnp.where(place < halfway, place, place - halfway).astype(f32)
    angles = step.astype(f32) * jnp.exp(-math.log(10000.0) * which / halfway)
    wave = jnp.where(place < halfway, jnp.cos(angles), jnp.sin(angles))
    return wave / (1.0 + jnp.exp(-wave))


def finish_kernel(
    per,
    head,
    timestep_ref,
    sums,
    output,
    input_grad,
    first,
    second,
    out_parts,
    up_parts,
    down_parts,
    o_out,
    o_in,
    o_embed,
    o_gain1,
    o_gain2,
    o_ada,
    o_ada_b,
    o_qkv,
    o_ow,
    o_up,
    o_up_b,
    o_down,
    o_down_b,
):
    n = pl.program_id(0)
    width = sums.shape[1]
    o_out[...] = output[...]
    o_in[...] = input_grad[...]
    o_up[...] = up_parts[...].astype(f32)
    o_down[...] = down_parts[...].astype(f32)
    wide = out_parts.shape[3]
    for m in range(2):
        o_ow[:, m * wide : (m + 1) * wide] = out_parts[0, m].astype(f32)
    count = o_ada.shape[0]
    act = activation_of(timestep_ref[0], n * count, count, count * 8)
    for i in range(6):
        o_ada[:, i * width : (i + 1) * width] = act * sums[8 + i : 9 + i, :]

    def piece(third, j):
        g, h = j // per, j % per
        source = first if h < 2 else second
        a = (4 + h % 2) * head if third == 0 else h % 2 * 2 * head + (third - 1) * head
        if h == 2 and third == 0:
            a = 2 * head
        return source[g, 0, :, a : a + head].astype(f32)

    for third in range(3):
        for j in range(0, GROUPS * per, 2):
            a = third * width + j * head
            o_qkv[:, a : a + 2 * head] = jnp.concatenate(
                [piece(third, j), piece(third, j + 1)], axis=1
            )

    @pl.when(n == 0)
    def _():
        for ref, i in ((o_embed, 0), (o_gain1, 1), (o_gain2, 2), (o_down_b, 3), (o_up_b, 4)):
            ref[...] = sums[i : i + 1, :].reshape(width)
        for i in range(6):
            o_ada_b[i * width : (i + 1) * width] = sums[8 + i : 9 + i, :].reshape(width)


def fused_kernel(
    tp_size,
    prefix_ref,
    timestep_ref,
    flags_ref,
    embed_ref,
    gain1_ref,
    gain2_ref,
    up_b_ref,
    down_b_ref,
    ada_b_ref,
    tokens_ref,
    cot_ref,
    cos_hbm,
    sin_hbm,
    ada_hbm,
    qkv_hbm,
    out_w,
    up_w,
    down_w,
    o_out,
    o_in,
    o_vec,
    o_qkv1,
    o_qkv2,
    o_ow,
    o_mlp,
    mod,
    start,
    normal1,
    spread1,
    normal2,
    spread2,
    branch,
    middle_grad,
    mcol,
    nl,
    nt,
    whm,
    cosb,
    sinb,
    kvall,
    qd,
    expd,
    tops,
    mrun,
    lrun,
    ot,
    lse,
    delta,
    mtb,
    mi,
    rg,
    ng,
    acts,
    hgs,
    ag,
    pn_own,
    pn_so,
    pn_si,
    pn_yo,
    pn_yi,
    bgg,
    mig,
    dob,
    doi,
    dos,
    sbo,
    sbi,
    rso,
    rsi,
    dkv,
    pg1,
    pgi1,
    pg2,
    pgi2,
    dwb1,
    dws1,
    dwc1,
    dwr1,
    wg1,
    dwb2,
    dws2,
    dwc2,
    dwr2,
    wg2,
    wbuf,
    wsi,
    wz,
    wgt,
    og,
    mbuf,
    msi,
    mz,
    mgat,
    vec,
    vpl,
    vzs,
    vco,
    ss,
    rr,
    ls,
):
    rows, width = tokens_ref.shape
    head = width // HEADS
    per = HEADS // GROUPS
    gw = per * head
    line = GROUPS * rows
    shard = width // (2 * CHIPS)
    kv_at = [0, 2 * head, 6 * head]
    q_at = [4 * head, 8 * head]
    split = 6 * head
    s, t = lax.axis_index("seq"), lax.axis_index("tp")
    z, x, y, c = s // 2, s % 2, t // 2, t % 2
    sib = (s, t + 1 - 2 * c)
    chip = x * 2 + y
    p = chip * 2 + c

    def chip_of(k):
        return ((x + k // 2) % 2) * 2 + (y + k % 2) % 2

    def dev(k):
        return (z * 2 + (x + k // 2) % 2, ((y + k % 2) % 2) * 2 + c)

    def zdev(k):
        return (((z + k) % 4) * 2 + x, t)

    def zfrom(k):
        return (z + 4 - k) % 4

    names = {}

    def ids(name, count):
        if name not in names:
            names[name] = sum(n for _, n in names.values()), count
        return names[name][0]

    def remote(src, dst, i, to):
        return pltpu.make_async_remote_copy(
            src_ref=src,
            dst_ref=dst,
            send_sem=ss.at[i],
            recv_sem=rr.at[i],
            device_id=to,
            device_id_type=MESH,
        )

    pending = []

    def send(src, dst, i, to):
        copy = remote(src, dst, i, to)
        copy.start()
        pending.append(copy)
        return copy

    barrier = pltpu.get_barrier_semaphore()
    t_sib, t_y = y * 2 + 1 - c, (1 - y) * 2 + c
    t_ysib = (1 - y) * 2 + 1 - c
    ysib = (s, t_ysib)
    peers = [sib, ysib] + [dev(k) for k in (1, 2, 3)] + [zdev(k) for k in (1, 2, 3)]
    for peer in peers:
        pl.semaphore_signal(barrier, inc=1, device_id=peer, device_id_type=MESH)

    locals_ = []

    def local(src, dst, i):
        copy = pltpu.make_async_copy(src, dst, ls.at[i])
        copy.start()
        locals_.append(copy)
        return copy

    cond = ada_hbm.shape[0]
    ada = [
        local(ada_hbm.at[:, i * width : (i + 1) * width], msi.at[i * cond : (i + 1) * cond], 11 + i)
        for i in range(6)
    ]
    stage = [mbuf.at[0:width], mbuf.at[width : 2 * width], mgat.at[0:width]]
    raw = [local(qkv_hbm.at[:, i * width : (i + 1) * width], stage[i], i) for i in range(3)]
    for zb in range(GROUPS):
        block = (zb * 2 + x) * tp_size + t
        raw.append(local(cos_hbm.at[block], cosb.at[zb], 3 + zb))
        raw.append(local(sin_hbm.at[block], sinb.at[zb], 7 + zb))

    act = activation_of(timestep_ref[0], 0, cond, cond)
    for i in range(6):
        ada[i].wait()
        part = msi[i * cond : (i + 1) * cond, :].astype(f32)
        mod[i : i + 1, :] = column_sum(part * act) + row_of(ada_b_ref, i, width)
    shift1, scale1, gate1 = mod[0:1, :], mod[1:2, :], mod[2:3, :]
    shift2, scale2, gate2 = mod[3:4, :], mod[4:5, :], mod[5:6, :]
    embed, gain1, gain2, up_b, down_b = (
        row_of(ref, 0, width) for ref in (embed_ref, gain1_ref, gain2_ref, up_b_ref, down_b_ref)
    )
    place = (s * tp_size + t) * rows + lax.broadcasted_iota(jnp.int32, (1, rows), 1)
    chosen = jnp.where((place >= prefix_ref[0]) & (flags_ref[...].reshape(1, rows) == 1), 1.0, 0.0).astype(f32)
    mcol[...] = jnp.broadcast_to(chosen, (rows, rows)).T[:, 0:1]
    start[...] = tokens_ref[...].astype(f32) + mcol[...] * embed
    normal, spread = normalise(start[...])
    normal1[...] = normal
    spread1[...] = spread
    nl[z] = (normal * (gain1 * (1.0 + scale1)) + shift1).astype(bf16)
    rg[t] = (cot_ref[...].astype(f32) * gate2).astype(bf16)

    pl.semaphore_wait(barrier, len(peers))
    zi = ids("nl", 3)
    got_nl = [send(nl.at[z], nl.at[z], zi + k - 1, zdev(k)) for k in (1, 2, 3)]

    def group_start(buffer, name):
        i = ids(name, 3)
        one = send(buffer.at[t], buffer.at[t], i, sib)
        two = send(buffer.at[t], buffer.at[t], i + 1, dev(1))
        return one, two, i + 2

    def group_pass(buffer, two, i):
        two.wait_recv()
        other = (1 - y) * 2 + c
        return send(buffer.at[other], buffer.at[other], i, sib)

    rg1, rg2, rgi = group_start(rg, "rg")

    for copy in raw:
        copy.wait()
    for g in range(GROUPS):
        for h in range(per):
            a = g * gw + h * head
            tile = [mbuf[width : 2 * width, a : a + head], mgat[0:width, a : a + head]]
            whm[g, :, kv_at[h] : kv_at[h] + 2 * head] = jnp.concatenate(tile, axis=1)
        a = g * gw
        whm[g, :, q_at[0] : q_at[0] + 2 * head] = mbuf[0:width, a : a + 2 * head]
        tile = [mbuf[0:width, a + 2 * head : a + 3 * head], jnp.zeros((width, head), bf16)]
        whm[g, :, q_at[1] : q_at[1] + 2 * head] = jnp.concatenate(tile, axis=1)

    lane = lax.broadcasted_iota(jnp.int32, (rows, 2 * head), 1)
    low_half = lane < head
    first = (lane % head) < head // 2
    half = head // 2

    def turn(tile, cosine, sine):
        ahead = jnp.where(first, -pltpu.roll(tile, 2 * head - half, 1), pltpu.roll(tile, half, 1))
        return tile * cosine + ahead * sine

    def turn_back(tile, cosine, sine):
        moved = tile * sine
        behind = jnp.where(first, pltpu.roll(moved, 2 * head - half, 1), -pltpu.roll(moved, half, 1))
        return tile * cosine + behind

    kvi = ids("kv", 12)
    scale = head ** (-0.5)
    for k in range(GROUPS):
        zb = zfrom(k)
        if k:
            got_nl[k - 1].wait_recv()
        proj = dot(nl[zb], whm[z], 1, 0)
        cosine, sine = cosb[zb], sinb[zb]
        here = pl.ds(zb * rows, rows)
        for h in range(per):
            tile = proj[:, kv_at[h] : kv_at[h] + 2 * head]
            kvall[h, p, here, :] = jnp.where(low_half, turn(tile, cosine, sine), tile).astype(bf16)
        for kk in (1, 2, 3):
            src = kvall.at[:, p, here, :]
            send(src, src, kvi + (kk - 1) * 4 + k, dev(kk))
        for i in range(2):
            tile = turn(proj[:, q_at[i] : q_at[i] + 2 * head], cosine, sine) * scale
            qd[2 * i, here, :] = jnp.where(low_half, tile, 0.0).astype(bf16)
            if i == 0:
                qd[1, here, :] = jnp.where(low_half, pltpu.roll(tile, head, 1), 0.0).astype(bf16)
    kdi = ids("kvd", 4)
    remote(kvall.at[:, p], kvall.at[:, p], kdi, sib).start()

    mrun[...] = jnp.full_like(mrun, floor_value)
    lrun[...] = jnp.zeros_like(lrun)
    ot[...] = jnp.zeros_like(ot)

    def forward(i, carry):
        k, r = i // (2 * per), i % (2 * per)
        h, away = r % per, r // per
        chunk = chip_of(k) * 2 + (c + away) % 2

        @pl.when((r == 0) & (k > 0))
        def _():
            for q in range(GROUPS):
                block = kvall.at[:, chunk, pl.ds(q * rows, rows), :]
                remote(block, block, kvi + (k - 1) * 4 + q, sib).wait_recv()
            remote(kvall.at[:, chunk], kvall.at[:, chunk], kdi + k, sib).start()

        @pl.when(r == per)
        def _():
            remote(kvall.at[:, chunk], kvall.at[:, chunk], kdi + k, sib).wait_recv()

        keys = kvall[h, chunk]
        scores = dot(keys, qd[h], 1, 1)
        before = mrun[h]
        top = jnp.maximum(before, jnp.max(scores, axis=0, keepdims=True))
        weights = jnp.exp(scores - top)
        factor = jnp.exp(before - top)
        rounded = weights.astype(bf16)
        expd[h, chunk] = rounded
        lrun[h] = lrun[h] * factor + column_sum(weights)
        mrun[h] = top
        tops[h, chunk] = top
        ot[h] = ot[h] * factor + dot(keys, rounded, 0, 0)
        return carry

    lax.fori_loop(0, 2 * CHIPS * per, forward, 0)

    for h in range(per):
        ot[h] = ot[h] / lrun[h]
        lse[h] = mrun[h] + jnp.log(lrun[h])
        for zb in range(GROUPS):
            mtb[zb, h * head : (h + 1) * head, :] = ot[
                h, head : 2 * head, zb * rows : (zb + 1) * rows
            ].astype(bf16)
    i = ids("mix", 3)
    got_mix = [send(mtb.at[(z + k) % 4], mi.at[z], i + k - 1, zdev(k)) for k in (1, 2, 3)]
    mi[z] = mtb[z]
    rg3 = group_pass(rg, rg2, rgi)
    nt[...] = nl[...].reshape(line, width).T
    rg1.wait_recv()
    rg3.wait_recv()
    for tb in range(tp_size):
        ag[tb] = dot(rg[tb], down_w[...], 1, 1)
    for copy in got_mix:
        copy.wait_recv()
    total = dot(mi[0], out_w[0:gw, :], 0, 0)
    for g in range(1, GROUPS):
        total = total + dot(mi[g], out_w[g * gw : (g + 1) * gw, :], 0, 0)
    i = ids("mig", 3)
    to = ((t_sib, sib), (t_y, dev(1)), (t_ysib, ysib))
    got_mig = [send(mi.at[at], mig.at[t], i + n, where) for n, (at, where) in enumerate(to)]
    mig[t] = mi[t]
    branch[...] = total
    start[...] = start[...] + gate1 * total
    normal, spread = normalise(start[...])
    normal2[...] = normal
    spread2[...] = spread
    ng[t] = (normal * (gain2 * (1.0 + scale2)) + shift2).astype(bf16)
    ng1, ng2, ngi = group_start(ng, "ng")

    inner, cubic = 0.7978845608028654, 0.044715

    def feed(tb):
        hidden = dot(ng[tb], up_w[...], 1, 0) + up_b
        square = hidden * hidden
        bent = jnp.tanh(inner * hidden * (1.0 + cubic * square))
        share = 0.5 * (1.0 + bent)
        acts[tb] = (hidden * share).astype(bf16)
        slope = share + 0.5 * hidden * (1.0 - bent * bent) * (
            inner * (1.0 + 3.0 * cubic * square)
        )
        hgs[tb] = (ag[tb] * slope).astype(bf16)
        return dot(hgs[tb], up_w[...], 1, 1)

    def group_sum(n, term, name, own_first, sib_first, y_first, ysib_first):
        i = ids(name, 3)
        if own_first is not None:
            own_first()
        pn_own[n] = term(t)
        if sib_first is not None:
            sib_first()
        pn_so[n, 0] = term(t_sib).astype(bf16)
        one = send(pn_so.at[n, 0], pn_si.at[n, 0], i, sib)
        if ysib_first is not None:
            y_first()
            ysib_first()
        pn_so[n, 1] = term(t_ysib).astype(bf16)
        two = send(pn_so.at[n, 1], pn_si.at[n, 1], i + 1, sib)
        mine = term(t_y)
        two.wait_recv()
        pn_yo[n] = (mine + pn_si[n, 1].astype(f32)).astype(bf16)
        three = send(pn_yo.at[n], pn_yi.at[n], i + 2, dev(1))

        def finish():
            one.wait_recv()
            three.wait_recv()
            return pn_own[n] + pn_si[n, 0].astype(f32) + pn_yi[n].astype(f32)

        return finish

    ng3 = []
    finish_grad = group_sum(
        0,
        feed,
        "pn",
        None,
        ng1.wait_recv,
        lambda: ng3.append(group_pass(ng, ng2, ngi)),
        lambda: ng3[0].wait_recv(),
    )
    half_rows = width // 2

    def exchange(part, buffer, incoming, parts, gathered, base, count, name):
        near, own = count // 2, count // 2 // GROUPS
        i = ids(name, 8)
        src = buffer.at[pl.ds(base + (1 - x) * near, near)]
        got = send(src, incoming, i, dev(2))
        yield
        got.wait_recv()
        mine = buffer[pl.ds(base + x * near, near), :].astype(f32) + incoming[...].astype(f32)
        incoming[...] = mine.astype(bf16)
        got = []
        for k in (1, 2, 3):
            src = incoming.at[pl.ds(((z + k) % 4) * own, own)]
            got.append(send(src, parts.at[k - 1], i + k, zdev(k)))
        yield
        for copy in got:
            copy.wait_recv()
        mine = incoming[pl.ds(z * own, own), :].astype(f32)
        for k in range(3):
            mine = mine + parts[k].astype(f32)
        src = gathered.at[pl.ds(base + x * near + z * own, own)]
        src[...] = mine.astype(bf16)
        got = [send(src, src, i + 3 + k, zdev(k)) for k in (1, 2, 3)]
        yield
        for copy in got:
            copy.wait_recv()
        src = gathered.at[pl.ds(base + x * near, near)]
        got = send(src, src, i + 7, dev(2))
        yield
        got.wait_recv()
        yield

    def exchange_of(m):
        side = pl.ds(m * half_rows, half_rows)
        return exchange(m, mbuf, msi.at[side], mz.at[m], mgat, m * width, width, f"m{m}")

    def matrix(left, right):
        return dot(left[...].reshape(line, width), right[...].reshape(line, width), 0, 0)

    mbuf[width : 2 * width, :] = matrix(acts, rg).astype(bf16)
    down_path = exchange_of(1)
    next(down_path)

    upstream = cot_ref[...].astype(f32)
    n2g = finish_grad()
    normal = normal2[...]
    middle = normalise_back(n2g * (gain2 * (1.0 + scale2)), normal, spread2[...]) + upstream
    bgg[t] = (middle * gate1).astype(bf16)
    for g in range(GROUPS):
        dob[g] = dot(out_w[g * gw : (g + 1) * gw, :], bgg[t], 1, 1).astype(bf16)
    i = ids("do", 3)
    got_do = [send(dob.at[(z + k) % 4], doi.at[z], i + k - 1, zdev(k)) for k in (1, 2, 3)]
    bg1, bg2, bgi = group_start(bgg, "bg")
    doi[z] = dob[z]
    middle_grad[...] = middle
    vec[3:4, :] = column_sum(middle * branch[...])
    vec[4:5, :] = column_sum(n2g)
    vec[5:6, :] = column_sum(n2g * normal)
    mbuf[0:width, :] = matrix(ng, hgs).astype(bf16)
    up_path = exchange_of(0)
    next(up_path)
    finish_result = group_sum(
        1, lambda tb: dot(acts[tb], down_w[...], 1, 0), "res", None, None, None, None
    )
    bg3 = group_pass(bgg, bg2, bgi)
    vec[8:9, :] = column_sum(hgs[...].reshape(line, width).astype(f32))
    vec[9:16, :] = jnp.zeros((7, width), f32)
    vec[7:8, :] = column_sum(rg[t].astype(f32))

    for copy in got_do:
        copy.wait_recv()
    for h in range(per):
        dos[h, 0:head, :] = jnp.zeros((head, line), bf16)
        for zb in range(GROUPS):
            dos[h, head : 2 * head, zb * rows : (zb + 1) * rows] = doi[
                zb, h * head : (h + 1) * head, :
            ]
        delta[h] = column_sum(dos[h, head : 2 * head, :].astype(f32) * ot[h, head : 2 * head, :])
    dq = ot
    dq[...] = jnp.zeros_like(dq)
    sbx = ids("sb", 12)
    rsx = ids("rs", 9)

    def backward(i, carry):
        h, r = i // (2 * CHIPS), i % (2 * CHIPS)
        away, k = 1 - r // CHIPS, CHIPS - 1 - r % CHIPS
        chunk = chip_of(k) * 2 + (c + away) % 2
        keys = kvall[h, chunk]
        factor = jnp.exp(tops[h, chunk] - lse[h])
        scaled = (dos[h].astype(f32) * factor).astype(bf16)
        prob_grad = dot(keys, scaled, 1, 0)
        rounded = expd[h, chunk]
        score_grad = (rounded.astype(f32) * (prob_grad - delta[h] * factor)).astype(bf16)
        dq[h] = dq[h] + dot(keys, score_grad, 0, 0)
        part = dot(score_grad, qd[h], 1, 0) + dot(rounded, scaled, 1, 1)
        over = remote(sbo.at[k], sbi.at[h, k], sbx + h * CHIPS + k, sib)

        @pl.when((away == 1) & (h > 0))
        def _():
            remote(sbo.at[k], sbi.at[h, k], sbx + (h - 1) * CHIPS + k, sib).wait_send()

        @pl.when(away == 1)
        def _():
            sbo[k] = part.astype(bf16)
            over.start()

        @pl.when(away == 0)
        def _():
            over.wait_recv()
            both = part + sbi[h, k].astype(f32)

            @pl.when(k == 0)
            def _():
                dkv[h] = both

            @pl.when((k > 0) & (h > 0))
            def _():
                remote(rso.at[k - 1], rsi.at[h, k - 1], rsx + (h - 1) * 3 + k - 1, sib).wait_send()

            @pl.when(k > 0)
            def _():
                rso[k - 1] = both.astype(bf16)
                remote(rso.at[k - 1], rsi.at[h, k - 1], rsx + h * 3 + k - 1, dev(k)).start()

        return carry

    def backward_from(first, last):
        lax.fori_loop(first, last, backward, 0)

    def keys_back(h, out, b):
        total = dkv[h]
        for k in range(3):
            remote(rso.at[k], rsi.at[h, k], rsx + h * 3 + k, sib).wait_recv()
            total = total + rsi[h, k].astype(f32)
        for zb in range(GROUPS):
            tile = total[zb * rows : (zb + 1) * rows, :]
            back = jnp.where(low_half, turn_back(tile, cosb[zb], sinb[zb]), tile)
            out[zb, :, b : b + 2 * head] = back.astype(bf16)

    def queries_back(one, two, out, b):
        flat = jnp.concatenate([one, two], axis=0).T * scale
        for zb in range(GROUPS):
            tile = flat[zb * rows : (zb + 1) * rows, :]
            out[zb, :, b : b + 2 * head] = turn_back(tile, cosb[zb], sinb[zb]).astype(bf16)

    def scatter_rows(out, into, name):
        i = ids(name, 3)
        got = [send(out.at[(z + k) % 4], into.at[z], i + k - 1, zdev(k)) for k in (1, 2, 3)]
        into[z] = out[z]
        return got

    def projection(out, mine, other, summed, incoming, gathered, name):
        grad = dot(nt[...], out[...].reshape(line, out.shape[2]), 1, 0)
        for n in range(2 * CHIPS):
            mine[n % 2, n // 2] = grad[n * shard : (n + 1) * shard, :].astype(bf16)
        i = ids(name, 13)
        got = send(mine.at[1 - c], other, i, sib)
        yield
        got.wait_recv()
        summed[...] = (mine[c].astype(f32) + other[...].astype(f32)).astype(bf16)
        got = [send(summed.at[chip_of(k)], incoming.at[k - 1], i + k, dev(k)) for k in (1, 2, 3)]
        yield
        for copy in got:
            copy.wait_recv()
        whole = summed[chip].astype(f32)
        for k in range(3):
            whole = whole + incoming[k].astype(f32)
        gathered[z, chip, c] = whole.astype(bf16)
        src = gathered.at[z, chip, c]
        got = [send(src, src, i + 3 + k, zdev(k)) for k in (1, 2, 3)]
        yield
        for copy in got:
            copy.wait_recv()
        src = gathered.at[:, chip, c]
        over_y = send(src, src, i + 7, dev(1))
        over_x = send(src, src, i + 8, dev(2))
        last = [send(src, src, i + 9, sib)]
        yield
        over_x.wait_recv()
        src = gathered.at[:, chip_of(2), c]
        both = send(src, src, i + 10, dev(1))
        last.append(send(src, src, i + 11, sib))
        yield
        over_y.wait_recv()
        src = gathered.at[:, chip_of(1), c]
        last.append(send(src, src, i + 12, sib))
        both.wait_recv()
        src = gathered.at[:, chip_of(3), c]
        last.append(send(src, src, ids(name + "x", 1), sib))
        yield
        for copy in last:
            copy.wait_recv()
        yield

    next(down_path)
    backward_from(0, 8)
    bg1.wait_recv()
    bg3.wait_recv()
    for copy in got_mig:
        copy.wait_recv()
    grad = dot(mig[0], bgg[0], 1, 0)
    for n in range(1, tp_size):
        grad = grad + dot(mig[n], bgg[n], 1, 0)
    wide = width // 2
    wbuf[0:gw, :] = grad[:, 0:wide].astype(bf16)
    wbuf[gw : 2 * gw, :] = grad[:, wide:width].astype(bf16)
    out_path = exchange(2, wbuf, wsi, wz, wgt, 0, 2 * gw, "wo")
    next(out_path)
    result = finish_result() + down_b
    o_out[...] = (start[...] + gate2 * result).astype(bf16)
    vec[6:7, :] = column_sum(cot_ref[...].astype(f32) * result)
    backward_from(8, 16)
    next(up_path)
    backward_from(16, 20)
    keys_back(0, pg1, kv_at[0])
    keys_back(1, pg1, kv_at[1])
    queries_back(dq[0, 0:head, :], dq[1, 0:head, :], pg1, q_at[0])
    got_pg1 = scatter_rows(pg1, pgi1, "pg1")
    first_path = projection(pg1, dwb1, dws1, dwc1, dwr1, wg1, "w1")
    next(first_path)
    next(down_path)
    backward_from(20, 24)
    next(first_path)
    next(out_path)
    keys_back(2, pg2, kv_at[2] - split)
    queries_back(dq[2, 0:head, :], jnp.zeros((head, line), f32), pg2, q_at[1] - split)
    got_pg2 = scatter_rows(pg2, pgi2, "pg2")
    second_path = projection(pg2, dwb2, dws2, dwc2, dwr2, wg2, "w2")
    next(second_path)
    next(first_path)
    for copy in got_pg1:
        copy.wait_recv()
    n1g = dot(pgi1[0], whm[0, :, 0:split], 1, 1)
    for g in range(1, GROUPS):
        n1g = n1g + dot(pgi1[g], whm[g, :, 0:split], 1, 1)
    next(second_path)
    next(up_path)
    next(out_path)
    for copy in got_pg2:
        copy.wait_recv()
    for g in range(GROUPS):
        n1g = n1g + dot(pgi2[g], whm[g, :, split : split + 4 * head], 1, 1)
    normal = normal1[...]
    vec[1:2, :] = column_sum(n1g)
    vec[2:3, :] = column_sum(n1g * normal)
    grad = normalise_back(n1g * (gain1 * (1.0 + scale1)), normal, spread1[...]) + middle_grad[...]
    o_in[...] = grad
    vec[0:1, :] = column_sum(grad * mcol[...])
    vpl[chip] = vec[...]
    i = ids("vp", 3)
    got_vp = [send(vec, vpl.at[chip], i + k - 1, dev(k)) for k in (1, 2, 3)]
    next(second_path)
    next(first_path)
    next(down_path)
    for copy in got_vp:
        copy.wait_recv()
    vzs[z, 0:8] = (vpl[0, 0:8] + vpl[1, 0:8]) + (vpl[2, 0:8] + vpl[3, 0:8])
    vzs[z, 8:16] = vpl[y, 8:16] + vpl[2 + y, 8:16]
    iv = ids("vz", 3)
    got_vz = [send(vzs.at[z], vzs.at[z], iv + k - 1, zdev(k)) for k in (1, 2, 3)]
    next(first_path)
    next(second_path)
    next(out_path)
    next(up_path)
    for copy in got_vz:
        copy.wait_recv()
    vco[c] = (vzs[0] + vzs[1]) + (vzs[2] + vzs[3])
    got_vc = send(vco.at[c], vco.at[c], ids("vc", 1), sib)
    next(first_path)
    next(out_path)
    og[t] = wgt[...]
    og1, og2, ogi = group_start(og, "og")
    next(second_path)
    got_vc.wait_recv()
    sums = vco[0] + vco[1]
    o_vec[0:1, :] = sums[0:1, :]
    o_vec[1:2, :] = sums[2:3, :] * (1.0 + scale1)
    o_vec[2:3, :] = sums[5:6, :] * (1.0 + scale2)
    o_vec[3:4, :] = sums[7:8, :]
    o_vec[4:5, :] = vco[c, 8:9, :]
    o_vec[5:8, :] = jnp.zeros((3, width), f32)
    o_vec[8:9, :] = sums[1:2, :]
    o_vec[9:10, :] = sums[2:3, :] * gain1
    o_vec[10:11, :] = sums[3:4, :]
    o_vec[11:12, :] = sums[4:5, :]
    o_vec[12:13, :] = sums[5:6, :] * gain2
    o_vec[13:14, :] = sums[6:7, :]
    o_vec[14:16, :] = jnp.zeros((2, width), f32)
    next(down_path)
    copies = [pltpu.make_async_copy(mgat.at[width : 2 * width], o_mlp.at[width : 2 * width], ls.at[0])]
    copies[-1].start()
    next(first_path)
    copies.append(pltpu.make_async_copy(wg1, o_qkv1, ls.at[1]))
    copies[-1].start()
    og3 = group_pass(og, og2, ogi)
    next(second_path)
    next(up_path)
    copies.append(pltpu.make_async_copy(mgat.at[0:width], o_mlp.at[0:width], ls.at[2]))
    copies[-1].start()
    next(second_path)
    copies.append(pltpu.make_async_copy(wg2, o_qkv2, ls.at[3]))
    copies[-1].start()
    og1.wait_recv()
    og3.wait_recv()
    copies.append(pltpu.make_async_copy(og, o_ow, ls.at[4]))
    copies[-1].start()
    for copy in pending:
        copy.wait_send()
    for k in range(CHIPS):
        remote(kvall.at[:, 0], kvall.at[:, 0], kdi + k, sib).wait_send()

    def drain(i, carry):
        remote(sbo.at[i], sbi.at[0, 0], sbx + (per - 1) * CHIPS + i, sib).wait_send()
        return carry

    lax.fori_loop(0, CHIPS, drain, 0)

    def drain(i, carry):
        remote(rso.at[i], rsi.at[0, 0], rsx + (per - 1) * 3 + i, sib).wait_send()
        return carry

    lax.fori_loop(0, 3, drain, 0)
    for copy in copies:
        copy.wait()


def rope_constants(length, rows, head):
    half = head // 2
    inverse = np.exp(np.float32(-math.log(10000.0)) * np.arange(half, dtype=np.float32) / half)
    angles = np.arange(length, dtype=np.float32)[:, None] * inverse.astype(np.float32)[None, :]
    angles = np.tile(angles, (1, 4)).astype(np.float64)
    shape = (length // rows, rows, 2 * head)
    return (
        jnp.asarray(np.cos(angles).astype(np.float32).reshape(shape)),
        jnp.asarray(np.sin(angles).astype(np.float32).reshape(shape)),
    )


def fused_device(
    seq_size,
    tp_size,
    tokens,
    cotangent,
    prefix_length,
    mask_flags,
    timestep,
    mask_embed,
    ln1_gain,
    ln2_gain,
    ada_weight,
    ada_bias,
    qkv_weight,
    out_weight,
    up_weight,
    up_bias,
    down_weight,
    down_bias,
):
    rows, width = tokens.shape
    head = width // HEADS
    per = HEADS // GROUPS
    gw = per * head
    line = GROUPS * rows
    packed = (per * 2 + 4) * head
    shard = width // (2 * CHIPS)
    cond = ada_weight.shape[0]
    cosine, sine = rope_constants(rows * seq_size * tp_size, rows, head)
    V = pltpu.VMEM
    vmem = pl.BlockSpec(memory_space=pltpu.VMEM)
    hbm = pl.BlockSpec(memory_space=pl.ANY)
    parts = (6 * head, 4 * head)
    outs = pl.pallas_call(
        functools.partial(fused_kernel, tp_size),
        out_shape=[
            jax.ShapeDtypeStruct((rows, width), bf16),
            jax.ShapeDtypeStruct((rows, width), f32),
            jax.ShapeDtypeStruct((16, width), f32),
            jax.ShapeDtypeStruct((GROUPS, CHIPS, 2, shard, parts[0]), bf16),
            jax.ShapeDtypeStruct((GROUPS, CHIPS, 2, shard, parts[1]), bf16),
            jax.ShapeDtypeStruct((tp_size, 2 * gw, width // 2), bf16),
            jax.ShapeDtypeStruct((2 * width, width), bf16),
        ],
        in_specs=[pl.BlockSpec(memory_space=pltpu.SMEM)] * 2
        + [vmem] * 9
        + [hbm] * 4
        + [vmem] * 3,
        out_specs=[vmem] * 3 + [hbm] * 4,
        scratch_shapes=[
            V((8, width), f32),
            V((rows, width), f32),
            V((rows, width), f32),
            V((rows, 1), f32),
            V((rows, width), f32),
            V((rows, 1), f32),
            V((rows, width), f32),
            V((rows, width), f32),
            V((rows, 1), f32),
            V((GROUPS, rows, width), bf16),
            V((width, line), bf16),
            V((GROUPS, width, packed), bf16),
            V((GROUPS, rows, 2 * head), f32),
            V((GROUPS, rows, 2 * head), f32),
            V((per, 2 * CHIPS, line, 2 * head), bf16),
            V((per, line, 2 * head), bf16),
            V((per, 2 * CHIPS, line, line), bf16),
            V((per, 2 * CHIPS, 1, line), f32),
            V((per, 1, line), f32),
            V((per, 1, line), f32),
            V((per, 2 * head, line), f32),
            V((per, 1, line), f32),
            V((per, 1, line), f32),
            V((GROUPS, gw, rows), bf16),
            V((GROUPS, gw, rows), bf16),
            V((tp_size, rows, width), bf16),
            V((tp_size, rows, width), bf16),
            V((tp_size, rows, width), bf16),
            V((tp_size, rows, width), bf16),
            V((tp_size, rows, width), f32),
            V((2, rows, width), f32),
            V((2, 2, rows, width), bf16),
            V((2, 2, rows, width), bf16),
            V((2, rows, width), bf16),
            V((2, rows, width), bf16),
            V((tp_size, rows, width), bf16),
            V((tp_size, gw, rows), bf16),
            V((GROUPS, gw, rows), bf16),
            V((GROUPS, gw, rows), bf16),
            V((per, 2 * head, line), bf16),
            V((CHIPS, line, 2 * head), bf16),
            V((per, CHIPS, line, 2 * head), bf16),
            V((3, line, 2 * head), bf16),
            V((per, 3, line, 2 * head), bf16),
            V((per, line, 2 * head), f32),
        ]
        + [V((GROUPS, rows, n), bf16) for n in parts for _ in range(2)]
        + [
            V(shape, bf16)
            for n in parts
            for shape in (
                (2, CHIPS, shard, n),
                (CHIPS, shard, n),
                (CHIPS, shard, n),
                (3, shard, n),
                (GROUPS, CHIPS, 2, shard, n),
            )
        ]
        + [
            V((2 * gw, width // 2), bf16),
            V((gw, width // 2), bf16),
            V((3, gw // GROUPS, width // 2), bf16),
            V((2 * gw, width // 2), bf16),
            V((tp_size, 2 * gw, width // 2), bf16),
            V((2 * width, width), bf16),
            V((width, width), bf16),
            V((2, 3, shard, width), bf16),
            V((2 * width, width), bf16),
            V((16, width), f32),
            V((CHIPS, 16, width), f32),
            V((GROUPS, 16, width), f32),
            V((2, 16, width), f32),
            pltpu.SemaphoreType.DMA((160,)),
            pltpu.SemaphoreType.DMA((160,)),
            pltpu.SemaphoreType.DMA((17,)),
        ],
        compiler_params=pltpu.CompilerParams(
            collective_id=0, has_side_effects=True, vmem_limit_bytes=VMEM_LIMIT
        ),
    )(
        prefix_length,
        timestep,
        mask_flags,
        mask_embed,
        ln1_gain,
        ln2_gain,
        up_bias,
        down_bias,
        ada_bias,
        tokens,
        cotangent,
        cosine,
        sine,
        ada_weight,
        qkv_weight,
        out_weight,
        up_weight,
        down_weight,
    )
    output, input_grad, sums, first, second, out_parts, mlp_parts = outs
    steps = 2 * CHIPS
    vector = jax.ShapeDtypeStruct((width,), f32)
    whole = pl.BlockSpec((width,), lambda n: (0,))

    def some(*shape):
        return jax.ShapeDtypeStruct(shape, f32)

    def rows_of(count, columns, skip=0):
        return pl.BlockSpec((count, columns), lambda n: (n + skip, 0))

    return pl.pallas_call(
        functools.partial(finish_kernel, per, head),
        grid=(steps,),
        out_shape=[
            jax.ShapeDtypeStruct((rows, width), bf16),
            some(rows, width),
            vector,
            vector,
            vector,
            some(cond, 6 * width),
            some(6 * width),
            some(width, 3 * width),
            some(width, width),
            some(width, width),
            vector,
            some(width, width),
            vector,
        ],
        in_specs=[
            pl.BlockSpec(memory_space=pltpu.SMEM),
            pl.BlockSpec((16, width), lambda n: (0, 0)),
            rows_of(rows // steps, width),
            rows_of(rows // steps, width),
            pl.BlockSpec((GROUPS, 1, shard, parts[0]), lambda n: (0, n, 0, 0)),
            pl.BlockSpec((GROUPS, 1, shard, parts[1]), lambda n: (0, n, 0, 0)),
            pl.BlockSpec((1, 2, shard, width // 2), lambda n: (n // 2, 0, n % 2, 0)),
            rows_of(shard, width),
            rows_of(shard, width, steps),
        ],
        out_specs=[
            rows_of(rows // steps, width),
            rows_of(rows // steps, width),
            whole,
            whole,
            whole,
            rows_of(cond // steps, 6 * width),
            pl.BlockSpec((6 * width,), lambda n: (0,)),
            rows_of(shard, 3 * width),
            rows_of(shard, width),
            rows_of(shard, width),
            whole,
            rows_of(shard, width),
            whole,
        ],
    )(
        timestep,
        sums,
        output,
        input_grad,
        first.reshape(GROUPS, steps, shard, parts[0]),
        second.reshape(GROUPS, steps, shard, parts[1]),
        out_parts.reshape(tp_size, 2, gw, width // 2),
        mlp_parts,
        mlp_parts,
    )


def solution(mesh):
    seq_size, tp_size = mesh.shape["seq"], mesh.shape["tp"]
    small = seq_size == 2 * GROUPS and tp_size == CHIPS
    in_specs = (
        P(("seq", "tp"), None),
        P(("seq", "tp"), None),
        P(),
        P(("seq", "tp")),
        P(),
        P(),
        P(),
        P(),
        P(),
        P(),
        P(),
        P(),
        P(None, "tp"),
        P("tp"),
        P("tp", None),
        P(),
    )
    out_specs = (
        P(("seq", "tp"), None),
        P(("seq", "tp"), None),
        P(),
        P(),
        P(),
        P(),
        P(),
        P(),
        P(),
        P(None, "tp"),
        P("tp"),
        P("tp", None),
        P(),
    )
    return jax.shard_map(
        functools.partial(fused_device, seq_size, tp_size) if small else per_device,
        mesh=mesh, in_specs=in_specs, out_specs=out_specs, check_vma=False
    )
```

```python
import functools
import math

import jax
import jax.numpy as jnp
import numpy as np
from jax import lax
from jax.experimental import pallas as pl
from jax.experimental.pallas import tpu as pltpu
from jax.sharding import PartitionSpec as P

HEADS = 12


epsilon = 1e-05
highest = lax.Precision.HIGHEST
floor_value = -1e30


def layer_norm(inputs, norm_gain):
    centred = inputs - jnp.mean(inputs, axis=-1, keepdims=True)
    variance = jnp.mean(centred * centred, axis=-1, keepdims=True)
    return centred * lax.rsqrt(variance + epsilon) * norm_gain


def modulate(inputs, norm_gain, shift_vector, scale_vector):
    return layer_norm(inputs, norm_gain) * (1.0 + scale_vector) + shift_vector


def rotary_tables(positions, head_width):
    halfway = head_width // 2
    inverse = jnp.exp(-math.log(10000.0) * jnp.arange(halfway, dtype=jnp.float32) / halfway)
    angles = positions.astype(jnp.float32)[:, None] * inverse[None, :]
    angles = jnp.concatenate([angles, angles], axis=1)
    return (jnp.cos(angles), jnp.sin(angles))


def rotate(head_rows, cosine, sine):
    halfway = head_rows.shape[-1] // 2
    turned = jnp.concatenate([-head_rows[..., halfway:], head_rows[..., :halfway]], axis=-1)
    return head_rows * cosine[:, None, :] + turned * sine[:, None, :]


def time_embedding(timestep, embed_width):
    halfway = embed_width // 2
    rates = jnp.exp(-math.log(10000.0) * jnp.arange(halfway, dtype=jnp.float32) / halfway)
    angles = timestep[0].astype(jnp.float32) * rates
    return jnp.concatenate([jnp.cos(angles), jnp.sin(angles)])


def block_length(total_rows, other_count):
    pieces = total_rows // other_count
    widest = 1 << max(0, (2048 // other_count).bit_length() - 1)
    size = other_count * math.gcd(pieces, widest)
    return size


def over_blocks(running, row_arrays, other_count, advance):
    total_rows = row_arrays[0].shape[0]
    block_size = block_length(total_rows, other_count)

    def one_turn(block_index, current):
        block_start = block_index * block_size
        blocks = tuple(
            (lax.dynamic_slice_in_dim(array, block_start, block_size, 0) for array in row_arrays)
        )
        return advance(current, blocks)

    return lax.fori_loop(0, total_rows // block_size, one_turn, running)


def forward_update(running, queries, key_block, value_block, score_scale):
    highest_seen, totals, weighted = running
    scores = (
        jnp.einsum("qhd,khd->hqk", queries, key_block, preferred_element_type=jnp.float32)
        * score_scale
    )
    new_highest = jnp.maximum(highest_seen, jnp.max(scores, axis=-1))
    factor = jnp.exp(highest_seen - new_highest)
    weights = jnp.exp(scores - new_highest[:, :, None])
    totals = totals * factor + jnp.sum(weights, axis=-1)
    weighted = weighted * factor.T[:, :, None] + jnp.einsum(
        "hqk,khd->qhd",
        weights.astype(jnp.bfloat16),
        value_block,
        preferred_element_type=jnp.float32,
    )
    return (new_highest, totals, weighted)


def query_update(
    query_grad, queries, mixed_grad, logsum, delta, key_block, value_block, score_scale
):
    scores = (
        jnp.einsum("qhd,khd->hqk", queries, key_block, preferred_element_type=jnp.float32)
        * score_scale
    )
    probs = jnp.exp(scores - logsum[:, :, None])
    prob_grad = jnp.einsum(
        "qhd,khd->hqk", mixed_grad, value_block, preferred_element_type=jnp.float32
    )
    score_grad = (probs * (prob_grad - delta[:, :, None])).astype(jnp.bfloat16)
    return query_grad + score_scale * jnp.einsum(
        "hqk,khd->qhd", score_grad, key_block, preferred_element_type=jnp.float32
    )


def key_update(
    running, query_block, grad_block, logsum_block, delta_block, own_keys, own_values, score_scale
):
    key_grad, value_grad = running
    scores = (
        jnp.einsum("qhd,khd->hqk", query_block, own_keys, preferred_element_type=jnp.float32)
        * score_scale
    )
    probs = jnp.exp(scores - logsum_block.T[:, :, None])
    value_grad = value_grad + jnp.einsum(
        "hqk,qhd->khd", probs.astype(jnp.bfloat16), grad_block, preferred_element_type=jnp.float32
    )
    prob_grad = jnp.einsum(
        "qhd,khd->hqk", grad_block, own_values, preferred_element_type=jnp.float32
    )
    score_grad = (probs * (prob_grad - delta_block.T[:, :, None])).astype(jnp.bfloat16)
    key_grad = key_grad + score_scale * jnp.einsum(
        "hqk,qhd->khd", score_grad, query_block, preferred_element_type=jnp.float32
    )
    return (key_grad, value_grad)


def to_heads(rows):
    return lax.all_to_all(rows, "tp", split_axis=1, concat_axis=0, tiled=True)


def to_rows(rows):
    return lax.all_to_all(rows, "tp", split_axis=0, concat_axis=1, tiled=True)


def per_device(
    tokens,
    cotangent,
    prefix_length,
    mask_flags,
    timestep,
    mask_embed,
    ln1_gain,
    ln2_gain,
    ada_weight,
    ada_bias,
    qkv_weight,
    out_weight,
    up_weight,
    up_bias,
    down_weight,
    down_bias,
):
    row_count = tokens.shape[0]
    model_width = tokens.shape[1]
    head_count = HEADS
    head_width = model_width // head_count
    score_scale = head_width ** (-0.5)
    positions = lax.axis_index(("seq", "tp")) * row_count + jnp.arange(row_count, dtype=jnp.int32)
    masked = ((positions >= prefix_length[0]) & (mask_flags == 1)).astype(jnp.float32)
    activation = jax.nn.silu(time_embedding(timestep, ada_weight.shape[0]))
    modulation = jnp.dot(
        activation, ada_weight.astype(jnp.float32), precision=highest
    ) + ada_bias.astype(jnp.float32)
    shift_one, scale_one, gate_one, shift_two, scale_two, gate_two = jnp.split(modulation, 6)
    cosine, sine = rotary_tables(positions, head_width)
    gain_one = ln1_gain.astype(jnp.float32)
    gain_two = ln2_gain.astype(jnp.float32)
    start = tokens.astype(jnp.float32) + masked[:, None] * mask_embed.astype(jnp.float32)[None, :]
    normed = modulate(start, gain_one, shift_one, scale_one).astype(jnp.bfloat16)
    projected = jnp.dot(normed, qkv_weight, preferred_element_type=jnp.float32)
    split_rows = projected.reshape(row_count, 3, head_count, head_width)
    queries, key_rows, value_rows = (
        to_heads(rows.reshape(row_count, model_width).astype(jnp.bfloat16))
        for rows in (
            rotate(split_rows[:, 0], cosine, sine),
            rotate(split_rows[:, 1], cosine, sine),
            split_rows[:, 2],
        )
    )
    group_size, group_width = queries.shape
    head_group = group_width // head_width
    queries = queries.reshape(group_size, head_group, head_width)
    every_key = lax.all_gather(key_rows, "seq", axis=0, tiled=True)
    every_value = lax.all_gather(value_rows, "seq", axis=0, tiled=True)
    initial = (
        jnp.full((head_group, group_size), floor_value, jnp.float32),
        jnp.zeros((head_group, group_size), jnp.float32),
        jnp.zeros((group_size, head_group, head_width), jnp.float32),
    )

    def advance(current, blocks):
        return forward_update(
            current,
            queries,
            blocks[0].reshape(-1, head_group, head_width),
            blocks[1].reshape(-1, head_group, head_width),
            score_scale,
        )

    running = over_blocks(
        initial,
        (every_key, every_value),
        group_size,
        advance,
    )
    highest_seen, totals, weighted = running
    logsum = highest_seen + jnp.log(totals)
    attended = weighted / totals.T[:, :, None]
    mixed = to_rows(attended.reshape(group_size, group_width).astype(jnp.bfloat16))
    branch = jnp.dot(mixed, out_weight, preferred_element_type=jnp.float32)
    middle = start + gate_one * branch
    normed_two = modulate(middle, gain_two, shift_two, scale_two).astype(jnp.bfloat16)
    group_rows = lax.all_gather(normed_two, "tp", axis=0, tiled=True)
    hidden = jnp.dot(group_rows, up_weight, preferred_element_type=jnp.float32) + up_bias.astype(
        jnp.float32
    )
    active = jax.nn.gelu(hidden).astype(jnp.bfloat16)
    result = lax.psum_scatter(
        jnp.dot(active, down_weight, preferred_element_type=jnp.float32).astype(jnp.bfloat16),
        "tp",
        scatter_dimension=0,
        tiled=True,
    ).astype(jnp.float32) + down_bias.astype(jnp.float32)
    output = (middle + gate_two * result).astype(jnp.bfloat16)
    upstream = cotangent.astype(jnp.float32)
    result_grad = (upstream * gate_two).astype(jnp.bfloat16)
    gate_two_grad = jnp.sum(upstream * result, axis=0)
    down_bias_grad = jnp.sum(result_grad.astype(jnp.float32), axis=0)
    group_grads = lax.all_gather(result_grad, "tp", axis=0, tiled=True)
    down_weight_grad = jnp.dot(active.T, group_grads, preferred_element_type=jnp.float32)
    active_grad = jnp.dot(group_grads, down_weight.T, preferred_element_type=jnp.float32)
    unused, gelu_back = jax.vjp(jax.nn.gelu, hidden)
    hidden_grad = gelu_back(active_grad)[0].astype(jnp.bfloat16)
    up_bias_grad = jnp.sum(hidden_grad.astype(jnp.float32), axis=0)
    up_weight_grad = jnp.dot(group_rows.T, hidden_grad, preferred_element_type=jnp.float32)
    normed_two_grad = lax.psum_scatter(
        jnp.dot(hidden_grad, up_weight.T, preferred_element_type=jnp.float32).astype(jnp.bfloat16),
        "tp",
        scatter_dimension=0,
        tiled=True,
    ).astype(jnp.float32)
    unused, second_back = jax.vjp(modulate, middle, gain_two, shift_two, scale_two)
    middle_part, gain_two_grad, shift_two_grad, scale_two_grad = second_back(normed_two_grad)
    middle_grad = middle_part + upstream
    gate_one_grad = jnp.sum(middle_grad * branch, axis=0)
    branch_grad = (middle_grad * gate_one).astype(jnp.bfloat16)
    out_weight_grad = jnp.dot(mixed.T, branch_grad, preferred_element_type=jnp.float32)
    mixed_grad = to_heads(
        jnp.dot(branch_grad, out_weight.T, preferred_element_type=jnp.float32).astype(jnp.bfloat16)
    ).reshape(group_size, head_group, head_width)
    delta_rows = jnp.sum(mixed_grad.astype(jnp.float32) * attended, axis=-1)
    delta = delta_rows.T
    initial_query = jnp.zeros((group_size, head_group, head_width), jnp.float32)

    def advance(grads_now, blocks):
        return query_update(
            grads_now,
            queries,
            mixed_grad,
            logsum,
            delta,
            blocks[0].reshape(-1, head_group, head_width),
            blocks[1].reshape(-1, head_group, head_width),
            score_scale,
        )

    query_grad = over_blocks(
        initial_query,
        (every_key, every_value),
        group_size,
        advance,
    )
    every_logsum, every_delta = (
        lax.all_gather(logsum.T, "seq", axis=0, tiled=True),
        lax.all_gather(delta_rows, "seq", axis=0, tiled=True),
    )
    own_keys = key_rows.reshape(group_size, head_group, head_width)
    own_values = value_rows.reshape(group_size, head_group, head_width)
    initial_keys = (
        jnp.zeros((group_size, head_group, head_width), jnp.float32),
        jnp.zeros((group_size, head_group, head_width), jnp.float32),
    )

    def advance(grads_now, blocks):
        return key_update(
            grads_now,
            blocks[0].reshape(-1, head_group, head_width),
            blocks[1].reshape(-1, head_group, head_width),
            blocks[2],
            blocks[3],
            own_keys,
            own_values,
            score_scale,
        )

    key_grad, value_grad = over_blocks(
        initial_keys,
        (
            lax.all_gather(queries.reshape(group_size, group_width), "seq", axis=0, tiled=True),
            lax.all_gather(mixed_grad.reshape(group_size, group_width), "seq", axis=0, tiled=True),
            every_logsum,
            every_delta,
        ),
        group_size,
        advance,
    )
    query_rows, key_part_rows, value_grad_rows = (
        to_rows(rows.reshape(group_size, group_width)).reshape(row_count, head_count, head_width)
        for rows in (query_grad, key_grad, value_grad)
    )
    unused, rotate_back = jax.vjp(lambda head_rows: rotate(head_rows, cosine, sine), query_rows)
    query_part = rotate_back(query_rows)[0].reshape(row_count, model_width)
    key_part = rotate_back(key_part_rows)[0].reshape(row_count, model_width)
    projected_grad = jnp.concatenate(
        [query_part, key_part, value_grad_rows.reshape(row_count, model_width)], axis=1
    ).astype(jnp.bfloat16)
    qkv_weight_grad = jnp.dot(normed.T, projected_grad, preferred_element_type=jnp.float32)
    normed_grad = jnp.dot(projected_grad, qkv_weight.T, preferred_element_type=jnp.float32)
    unused, first_back = jax.vjp(modulate, start, gain_one, shift_one, scale_one)
    start_part, gain_one_grad, shift_one_grad, scale_one_grad = first_back(normed_grad)
    start_grad = start_part + middle_grad
    embed_grad = jnp.sum(masked[:, None] * start_grad, axis=0)
    modulation_grad = jnp.concatenate(
        [
            shift_one_grad,
            scale_one_grad,
            gate_one_grad,
            shift_two_grad,
            scale_two_grad,
            gate_two_grad,
        ]
    )
    summed = lax.psum(
        (
            qkv_weight_grad,
            out_weight_grad,
            modulation_grad,
            gain_one_grad,
            gain_two_grad,
            down_bias_grad,
            embed_grad,
        ),
        ("seq", "tp"),
    )
    split_sums = lax.psum((up_weight_grad, up_bias_grad, down_weight_grad), "seq")
    return (
        output,
        start_grad,
        summed[6],
        summed[3],
        summed[4],
        activation[:, None] * summed[2][None, :],
        summed[2],
        summed[0],
        summed[1],
        split_sums[0],
        split_sums[1],
        split_sums[2],
        summed[5],
    )


VMEM_LIMIT = 63 * 2**20
GROUPS = 4
CHIPS = 4
MESH = pl.DeviceIdType.MESH
f32, bf16 = jnp.float32, jnp.bfloat16


def dot(left, right, left_dim, right_dim):
    return lax.dot_general(
        left, right, (((left_dim,), (right_dim,)), ((), ())), preferred_element_type=f32
    )


def normalise(rows):
    centred = rows - jnp.mean(rows, axis=-1, keepdims=True)
    variance = jnp.mean(centred * centred, axis=-1, keepdims=True)
    spread = lax.rsqrt(variance + epsilon)
    return centred * spread, spread


def normalise_back(upstream, normal, spread):
    along = jnp.mean(upstream * normal, axis=-1, keepdims=True)
    return spread * (upstream - jnp.mean(upstream, axis=-1, keepdims=True) - normal * along)


def column_sum(rows):
    return jnp.sum(rows, axis=0, keepdims=True)


def row_of(ref, i, width):
    return ref[i * width : (i + 1) * width].astype(f32).reshape(1, width)


def activation_of(step, first, count, cond):
    halfway = cond // 2
    place = first + lax.broadcasted_iota(jnp.int32, (count, 1), 0)
    which = jnp.where(place < halfway, place, place - halfway).astype(f32)
    angles = step.astype(f32) * jnp.exp(-math.log(10000.0) * which / halfway)
    wave = jnp.where(place < halfway, jnp.cos(angles), jnp.sin(angles))
    return wave / (1.0 + jnp.exp(-wave))


def finish_kernel(
    per,
    head,
    timestep_ref,
    sums,
    output,
    input_grad,
    first,
    second,
    out_parts,
    up_parts,
    down_parts,
    o_out,
    o_in,
    o_embed,
    o_gain1,
    o_gain2,
    o_ada,
    o_ada_b,
    o_qkv,
    o_ow,
    o_up,
    o_up_b,
    o_down,
    o_down_b,
):
    n = pl.program_id(0)
    width = sums.shape[1]
    o_out[...] = output[...]
    o_in[...] = input_grad[...]
    o_up[...] = up_parts[...].astype(f32)
    o_down[...] = down_parts[...].astype(f32)
    wide = out_parts.shape[3]
    for m in range(2):
        o_ow[:, m * wide : (m + 1) * wide] = out_parts[0, m].astype(f32)
    count = o_ada.shape[0]
    act = activation_of(timestep_ref[0], n * count, count, count * 8)
    for i in range(6):
        o_ada[:, i * width : (i + 1) * width] = act * sums[8 + i : 9 + i, :]

    def piece(third, j):
        g, h = j // per, j % per
        source = first if h < 2 else second
        a = (4 + h % 2) * head if third == 0 else h % 2 * 2 * head + (third - 1) * head
        if h == 2 and third == 0:
            a = 2 * head
        return source[g, 0, :, a : a + head].astype(f32)

    for third in range(3):
        for j in range(0, GROUPS * per, 2):
            a = third * width + j * head
            o_qkv[:, a : a + 2 * head] = jnp.concatenate(
                [piece(third, j), piece(third, j + 1)], axis=1
            )

    @pl.when(n == 0)
    def _():
        for ref, i in ((o_embed, 0), (o_gain1, 1), (o_gain2, 2), (o_down_b, 3), (o_up_b, 4)):
            ref[...] = sums[i : i + 1, :].reshape(width)
        for i in range(6):
            o_ada_b[i * width : (i + 1) * width] = sums[8 + i : 9 + i, :].reshape(width)


def fused_kernel(
    tp_size,
    prefix_ref,
    timestep_ref,
    flags_ref,
    embed_ref,
    gain1_ref,
    gain2_ref,
    up_b_ref,
    down_b_ref,
    ada_b_ref,
    tokens_ref,
    cot_ref,
    cos_hbm,
    sin_hbm,
    ada_hbm,
    qkv_hbm,
    out_hbm,
    up_hbm,
    down_hbm,
    o_out,
    o_in,
    o_vec,
    o_qkv1,
    o_qkv2,
    o_ow,
    o_mlp,
    out_w,
    up_w,
    down_w,
    mod,
    start,
    normal1,
    spread1,
    normal2,
    spread2,
    branch,
    middle_grad,
    mcol,
    nl,
    kvo,
    qo,
    qi,
    whm,
    cosb,
    sinb,
    kvall,
    qd,
    expd,
    tops,
    mrun,
    lrun,
    ot,
    lse,
    delta,
    mtb,
    mi,
    rg,
    ng,
    acts,
    hgs,
    ag,
    pn_own,
    pn_so,
    pn_si,
    pn_yo,
    pn_yi,
    bgg,
    mig,
    dob,
    doi,
    dos,
    sbo,
    sbi,
    rso,
    rsi,
    rsx_out,
    rsx_in,
    dkv,
    pg1,
    pgi1,
    pg2,
    pgi2,
    dwb1,
    dws1,
    dwc1,
    dwr1,
    wg1,
    dwb2,
    dws2,
    dwc2,
    dwr2,
    wg2,
    wbuf,
    wsi,
    wz,
    wgt,
    og,
    mbuf,
    msi,
    mz,
    mgat,
    vec,
    vpl,
    vzs,
    vco,
    ss,
    rr,
    ls,
):
    rows, width = tokens_ref.shape
    head = width // HEADS
    per = HEADS // GROUPS
    gw = per * head
    line = GROUPS * rows
    shard = width // (2 * CHIPS)
    kv_at = [0, 2 * head, 6 * head]
    q_at = [4 * head, 8 * head]
    split = 6 * head
    s, t = lax.axis_index("seq"), lax.axis_index("tp")
    z, x, y, c = s // 2, s % 2, t // 2, t % 2
    sib = (s, t + 1 - 2 * c)
    chip = x * 2 + y
    p = chip * 2 + c

    def chip_of(k):
        return ((x + k // 2) % 2) * 2 + (y + k % 2) % 2

    def dev(k):
        return (z * 2 + (x + k // 2) % 2, ((y + k % 2) % 2) * 2 + c)

    def zdev(k):
        return (((z + k) % 4) * 2 + x, t)

    def zfrom(k):
        return (z + 4 - k) % 4

    names = {}

    def ids(name, count):
        if name not in names:
            names[name] = sum(n for _, n in names.values()), count
        return names[name][0]

    def remote(src, dst, i, to):
        return pltpu.make_async_remote_copy(
            src_ref=src,
            dst_ref=dst,
            send_sem=ss.at[i],
            recv_sem=rr.at[i],
            device_id=to,
            device_id_type=MESH,
        )

    pending = []

    def send(src, dst, i, to):
        copy = remote(src, dst, i, to)
        copy.start()
        pending.append(copy)
        return copy

    barrier = pltpu.get_barrier_semaphore()
    t_sib, t_y = y * 2 + 1 - c, (1 - y) * 2 + c
    t_ysib = (1 - y) * 2 + 1 - c
    ysib = (s, t_ysib)
    peers = [sib, ysib] + [dev(k) for k in (1, 2, 3)] + [zdev(k) for k in (1, 2, 3)]
    for peer in peers:
        pl.semaphore_signal(barrier, inc=1, device_id=peer, device_id_type=MESH)

    locals_ = []

    def local(src, dst, i):
        copy = pltpu.make_async_copy(src, dst, ls.at[i])
        copy.start()
        locals_.append(copy)
        return copy

    cond = ada_hbm.shape[0]
    ada = [
        local(ada_hbm.at[:, i * width : (i + 1) * width], msi.at[i * cond : (i + 1) * cond], 11 + i)
        for i in range(6)
    ]
    stage = [mbuf.at[0:width], mbuf.at[width : 2 * width], mgat.at[0:width]]
    raw = []
    for zb in range(GROUPS):
        block = (zb * 2 + x) * tp_size + t
        raw.append(local(cos_hbm.at[block], cosb.at[zb], zb))
        raw.append(local(sin_hbm.at[block], sinb.at[zb], 4 + zb))
    raw += [local(qkv_hbm.at[:, i * width : (i + 1) * width], stage[i], 8 + i) for i in range(3)]
    loads = zip((down_hbm, out_hbm, up_hbm), (down_w, out_w, up_w))
    weights = [local(src, dst, 17 + i) for i, (src, dst) in enumerate(loads)]
    act = activation_of(timestep_ref[0], 0, cond, cond)
    def modulate_rows(first, last):
        for i in range(first, last):
            ada[i].wait()
            part = msi[i * cond : (i + 1) * cond, :].astype(f32)
            mod[i : i + 1, :] = column_sum(part * act) + row_of(ada_b_ref, i, width)

    modulate_rows(0, 2)
    shift1, scale1 = mod[0:1, :], mod[1:2, :]
    embed, gain1, gain2, up_b, down_b = (
        row_of(ref, 0, width) for ref in (embed_ref, gain1_ref, gain2_ref, up_b_ref, down_b_ref)
    )
    place = (s * tp_size + t) * rows + lax.broadcasted_iota(jnp.int32, (1, rows), 1)
    chosen = jnp.where((place >= prefix_ref[0]) & (flags_ref[...].reshape(1, rows) == 1), 1.0, 0.0).astype(f32)
    mcol[...] = jnp.broadcast_to(chosen, (rows, rows)).T[:, 0:1]
    start[...] = tokens_ref[...].astype(f32) + mcol[...] * embed
    normal, spread = normalise(start[...])
    normal1[...] = normal
    spread1[...] = spread
    nl[z] = (normal * (gain1 * (1.0 + scale1)) + shift1).astype(bf16)

    pl.semaphore_wait(barrier, len(peers))

    def group_start(buffer, name):
        i = ids(name, 3)
        one = send(buffer.at[t], buffer.at[t], i, sib)
        two = send(buffer.at[t], buffer.at[t], i + 1, dev(1))
        return one, two, i + 2

    def group_pass(buffer, two, i):
        two.wait_recv()
        other = (1 - y) * 2 + c
        return send(buffer.at[other], buffer.at[other], i, sib)


    for copy in raw:
        copy.wait()
    lane = lax.broadcasted_iota(jnp.int32, (rows, 2 * head), 1)
    low_half = lane < head
    first = (lane % head) < head // 2
    half = head // 2

    def turn(tile, cosine, sine):
        ahead = jnp.where(first, -pltpu.roll(tile, 2 * head - half, 1), pltpu.roll(tile, half, 1))
        return tile * cosine + ahead * sine

    def turn_back(tile, cosine, sine):
        moved = tile * sine
        behind = jnp.where(first, pltpu.roll(moved, 2 * head - half, 1), -pltpu.roll(moved, half, 1))
        return tile * cosine + behind

    kvi = ids("kv", 12)
    scale = head ** (-0.5)
    cosine, sine = cosb[z], sinb[z]
    thirds = [dot(nl[z], ref[...], 1, 0) for ref in stage]

    def of_head(third, n):
        return thirds[third][:, n * head : (n + 1) * head]

    for g in range(GROUPS):
        for h in range(per):
            n = g * per + h
            tile = jnp.concatenate([of_head(1, n), of_head(2, n)], axis=1)
            kvo[g, h] = jnp.where(low_half, turn(tile, cosine, sine), tile).astype(bf16)
    here = pl.ds(z * rows, rows)
    zi = ids("kvz", 3)
    got_kv = []
    for k in (1, 2, 3):
        there = kvall.at[:, p, here, :]
        got_kv.append(send(kvo.at[(z + k) % 4], there, zi + k - 1, zdev(k)))
    kvall[:, p, here, :] = kvo[z]

    def over_plane(k):
        src = kvall.at[:, p, pl.ds(zfrom(k) * rows, rows), :]
        for kk in (1, 2, 3):
            send(src, src, kvi + (kk - 1) * 4 + k, dev(kk))

    over_plane(0)
    for g in range(GROUPS):
        n = g * per
        tile = turn(thirds[0][:, n * head : (n + 2) * head], cosine, sine) * scale
        qo[g, 0] = tile.astype(bf16)
        tile = jnp.concatenate([of_head(0, n + 2), jnp.zeros((rows, head), f32)], axis=1)
        qo[g, 1] = (turn(tile, cosine, sine) * scale).astype(bf16)
    i = ids("q", 3)
    got_q = [send(qo.at[(z + k) % 4], qi.at[z], i + k - 1, zdev(k)) for k in (1, 2, 3)]
    qi[z] = qo[z]
    for g in range(GROUPS):
        for h in range(per):
            a = g * gw + h * head
            tile = [mbuf[width : 2 * width, a : a + head], mgat[0:width, a : a + head]]
            whm[g, :, kv_at[h] : kv_at[h] + 2 * head] = jnp.concatenate(tile, axis=1)
        a = g * gw
        whm[g, :, q_at[0] : q_at[0] + 2 * head] = mbuf[0:width, a : a + 2 * head]
        tile = [mbuf[0:width, a + 2 * head : a + 3 * head], jnp.zeros((width, head), bf16)]
        whm[g, :, q_at[1] : q_at[1] + 2 * head] = jnp.concatenate(tile, axis=1)

    modulate_rows(2, 6)
    gate1, shift2 = mod[2:3, :], mod[3:4, :]
    scale2, gate2 = mod[4:5, :], mod[5:6, :]
    rg[t] = (cot_ref[...].astype(f32) * gate2).astype(bf16)
    rg1, rg2, rgi = group_start(rg, "rg")
    for k in (1, 2, 3):
        got_kv[k - 1].wait_recv()
        over_plane(k)
    i = ids("nl", 3)
    got_nl = [send(nl.at[z], nl.at[z], i + k - 1, zdev(k)) for k in (1, 2, 3)]
    kdi = ids("kvd", 4)
    remote(kvall.at[:, p], kvall.at[:, p], kdi, sib).start()
    for copy in got_q:
        copy.wait_recv()
    for zb in range(GROUPS):
        at = slice(zb * rows, (zb + 1) * rows)
        pair, last = qi[zb, 0].astype(f32), qi[zb, 1].astype(f32)
        qd[0, at, :] = jnp.where(low_half, pair, 0.0).astype(bf16)
        qd[1, at, :] = jnp.where(low_half, pltpu.roll(pair, head, 1), 0.0).astype(bf16)
        qd[2, at, :] = jnp.where(low_half, last, 0.0).astype(bf16)

    mrun[...] = jnp.full_like(mrun, floor_value)
    lrun[...] = jnp.zeros_like(lrun)
    ot[...] = jnp.zeros_like(ot)

    def forward(i, carry):
        k, r = i // (2 * per), i % (2 * per)
        h, away = r % per, r // per
        chunk = chip_of(k) * 2 + (c + away) % 2

        @pl.when((r == 0) & (k > 0))
        def _():
            for q in range(GROUPS):
                block = kvall.at[:, chunk, pl.ds(q * rows, rows), :]
                remote(block, block, kvi + (k - 1) * 4 + q, sib).wait_recv()
            remote(kvall.at[:, chunk], kvall.at[:, chunk], kdi + k, sib).start()

        @pl.when(r == per)
        def _():
            remote(kvall.at[:, chunk], kvall.at[:, chunk], kdi + k, sib).wait_recv()

        keys = kvall[h, chunk]
        scores = dot(keys, qd[h], 1, 1)
        before = mrun[h]
        top = jnp.maximum(before, jnp.max(scores, axis=0, keepdims=True))
        weights = jnp.exp(scores - top)
        factor = jnp.exp(before - top)
        rounded = weights.astype(bf16)
        expd[h, chunk] = rounded
        lrun[h] = lrun[h] * factor + column_sum(weights)
        mrun[h] = top
        tops[h, chunk] = top
        ot[h] = ot[h] * factor + dot(keys, rounded, 0, 0)
        return carry

    lax.fori_loop(0, 2 * CHIPS * per, forward, 0)

    for h in range(per):
        ot[h] = ot[h] / lrun[h]
        lse[h] = mrun[h] + jnp.log(lrun[h])
        for zb in range(GROUPS):
            mtb[zb, h * head : (h + 1) * head, :] = ot[
                h, head : 2 * head, zb * rows : (zb + 1) * rows
            ].astype(bf16)
    i = ids("mix", 3)
    got_mix = [send(mtb.at[(z + k) % 4], mi.at[z], i + k - 1, zdev(k)) for k in (1, 2, 3)]
    mi[z] = mtb[z]
    rg3 = group_pass(rg, rg2, rgi)
    rg1.wait_recv()
    rg3.wait_recv()
    weights[0].wait()
    for tb in range(tp_size):
        ag[tb] = dot(rg[tb], down_w[...], 1, 1)
    for copy in got_mix:
        copy.wait_recv()
    weights[1].wait()
    weights[2].wait()
    total = dot(mi[0], out_w[0:gw, :], 0, 0)
    for g in range(1, GROUPS):
        total = total + dot(mi[g], out_w[g * gw : (g + 1) * gw, :], 0, 0)
    i = ids("mig", 3)
    to = ((t_sib, sib), (t_y, dev(1)), (t_ysib, ysib))
    got_mig = [send(mi.at[at], mig.at[t], i + n, where) for n, (at, where) in enumerate(to)]
    mig[t] = mi[t]
    branch[...] = total
    start[...] = start[...] + gate1 * total
    normal, spread = normalise(start[...])
    normal2[...] = normal
    spread2[...] = spread
    ng[t] = (normal * (gain2 * (1.0 + scale2)) + shift2).astype(bf16)
    ng1, ng2, ngi = group_start(ng, "ng")

    inner, cubic = 0.7978845608028654, 0.044715

    def feed(tb):
        hidden = dot(ng[tb], up_w[...], 1, 0) + up_b
        square = hidden * hidden
        bent = jnp.tanh(inner * hidden * (1.0 + cubic * square))
        share = 0.5 * (1.0 + bent)
        acts[tb] = (hidden * share).astype(bf16)
        slope = share + 0.5 * hidden * (1.0 - bent * bent) * (
            inner * (1.0 + 3.0 * cubic * square)
        )
        hgs[tb] = (ag[tb] * slope).astype(bf16)
        return dot(hgs[tb], up_w[...], 1, 1)

    def group_sum(n, term, name, own_first, sib_first, y_first, ysib_first):
        i = ids(name, 3)
        if own_first is not None:
            own_first()
        pn_own[n] = term(t)
        if sib_first is not None:
            sib_first()
        pn_so[n, 0] = term(t_sib).astype(bf16)
        one = send(pn_so.at[n, 0], pn_si.at[n, 0], i, sib)
        if ysib_first is not None:
            y_first()
            ysib_first()
        pn_so[n, 1] = term(t_ysib).astype(bf16)
        two = send(pn_so.at[n, 1], pn_si.at[n, 1], i + 1, sib)
        mine = term(t_y)
        two.wait_recv()
        pn_yo[n] = (mine + pn_si[n, 1].astype(f32)).astype(bf16)
        three = send(pn_yo.at[n], pn_yi.at[n], i + 2, dev(1))

        def finish():
            one.wait_recv()
            three.wait_recv()
            return pn_own[n] + pn_si[n, 0].astype(f32) + pn_yi[n].astype(f32)

        return finish

    ng3 = []
    finish_grad = group_sum(
        0,
        feed,
        "pn",
        None,
        ng1.wait_recv,
        lambda: ng3.append(group_pass(ng, ng2, ngi)),
        lambda: ng3[0].wait_recv(),
    )
    half_rows = width // 2

    def exchange(buffer, incoming, parts, gathered, base, count, name):
        near, own = count // 2, count // 2 // GROUPS
        i = ids(name, 8)
        src = buffer.at[pl.ds(base + (1 - x) * near, near)]
        got = send(src, incoming, i, dev(2))
        yield
        got.wait_recv()
        mine = buffer[pl.ds(base + x * near, near), :].astype(f32) + incoming[...].astype(f32)
        incoming[...] = mine.astype(bf16)
        beside = ((z + 1 - 2 * (z % 2)) * 2 + x, t)
        got = []
        for n in range(2):
            src = incoming.at[pl.ds((n * 2 + 1 - z % 2) * own, own)]
            got.append(send(src, parts.at[n], i + 1 + n, beside))
        yield
        for n in range(2):
            got[n].wait_recv()
            src = incoming.at[pl.ds((n * 2 + z % 2) * own, own)]
            src[...] = (src[...].astype(f32) + parts[n].astype(f32)).astype(bf16)
        src = incoming.at[pl.ds(((z + 2) % 4) * own, own)]
        got = send(src, parts.at[2], i + 3, zdev(2))
        yield
        got.wait_recv()
        mine = incoming[pl.ds(z * own, own), :].astype(f32) + parts[2].astype(f32)

        def place(d):
            return gathered.at[pl.ds(base + x * near + d * own, own)]

        src = place(z)
        src[...] = mine.astype(bf16)
        got = send(src, src, i + 4, zdev(2))
        yield
        got.wait_recv()
        got = [send(place(d), place(d), i + 5 + n, beside) for n, d in enumerate((z, (z + 2) % 4))]
        yield
        for copy in got:
            copy.wait_recv()
        src = gathered.at[pl.ds(base + x * near, near)]
        got = send(src, src, i + 7, dev(2))
        yield
        got.wait_recv()
        yield

    def exchange_of(m):
        side = pl.ds(m * half_rows, half_rows)
        return exchange(mbuf, msi.at[side], mz.at[m], mgat, m * width, width, f"m{m}")

    def matrix(left, right):
        return dot(left[...].reshape(line, width), right[...].reshape(line, width), 0, 0)

    mbuf[width : 2 * width, :] = matrix(acts, rg).astype(bf16)
    down_path = exchange_of(1)
    next(down_path)

    upstream = cot_ref[...].astype(f32)
    n2g = finish_grad()
    normal = normal2[...]
    middle = normalise_back(n2g * (gain2 * (1.0 + scale2)), normal, spread2[...]) + upstream
    bgg[t] = (middle * gate1).astype(bf16)
    for g in range(GROUPS):
        dob[g] = dot(out_w[g * gw : (g + 1) * gw, :], bgg[t], 1, 1).astype(bf16)
    i = ids("do", 3)
    got_do = [send(dob.at[(z + k) % 4], doi.at[z], i + k - 1, zdev(k)) for k in (1, 2, 3)]
    bg1, bg2, bgi = group_start(bgg, "bg")
    doi[z] = dob[z]
    middle_grad[...] = middle
    vec[3:4, :] = column_sum(middle * branch[...])
    vec[4:5, :] = column_sum(n2g)
    vec[5:6, :] = column_sum(n2g * normal)
    mbuf[0:width, :] = matrix(ng, hgs).astype(bf16)
    up_path = exchange_of(0)
    next(up_path)
    finish_result = group_sum(
        1, lambda tb: dot(acts[tb], down_w[...], 1, 0), "res", None, None, None, None
    )
    bg3 = group_pass(bgg, bg2, bgi)
    vec[8:9, :] = column_sum(hgs[...].reshape(line, width).astype(f32))
    vec[9:16, :] = jnp.zeros((7, width), f32)
    vec[7:8, :] = column_sum(rg[t].astype(f32))

    for copy in got_do:
        copy.wait_recv()
    for h in range(per):
        dos[h, 0:head, :] = jnp.zeros((head, line), bf16)
        for zb in range(GROUPS):
            dos[h, head : 2 * head, zb * rows : (zb + 1) * rows] = doi[
                zb, h * head : (h + 1) * head, :
            ]
        delta[h] = column_sum(dos[h, head : 2 * head, :].astype(f32) * ot[h, head : 2 * head, :])
    dq = ot
    dq[...] = jnp.zeros_like(dq)
    sbx = ids("sb", 12)
    rsi_at = ids("rs", 9)

    def backward(i, carry):
        h, r = i // (2 * CHIPS), i % (2 * CHIPS)
        away, k = 1 - r // CHIPS, CHIPS - 1 - r % CHIPS
        chunk = chip_of(k) * 2 + (c + away) % 2
        keys = kvall[h, chunk]
        factor = jnp.exp(tops[h, chunk] - lse[h])
        scaled = (dos[h].astype(f32) * factor).astype(bf16)
        prob_grad = dot(keys, scaled, 1, 0)
        rounded = expd[h, chunk]
        score_grad = (rounded.astype(f32) * (prob_grad - delta[h] * factor)).astype(bf16)
        dq[h] = dq[h] + dot(keys, score_grad, 0, 0)
        part = dot(score_grad, qd[h], 1, 0) + dot(rounded, scaled, 1, 1)
        over = remote(sbo.at[k], sbi.at[h, k], sbx + h * CHIPS + k, sib)

        @pl.when((away == 1) & (h > 0))
        def _():
            remote(sbo.at[k], sbi.at[h, k], sbx + (h - 1) * CHIPS + k, sib).wait_send()

        @pl.when(away == 1)
        def _():
            sbo[k] = part.astype(bf16)
            over.start()

        @pl.when(away == 0)
        def _():
            over.wait_recv()
            both = part + sbi[h, k].astype(f32)

            @pl.when(k == 0)
            def _():
                dkv[h] = both

            final = h // (per - 1)

            @pl.when(k == 2)
            def _():
                rsx_out[h] = both.astype(bf16)

            @pl.when((k == 2) & (final == 1))
            def _():
                remote(rsx_out.at[h], rsx_in.at[h], rsi_at + h * 3 + 2, dev(2)).start()

            odd = k // 2

            @pl.when((k % 2 == 1) & (h > 0))
            def _():
                remote(rso.at[odd], rsi.at[h, odd], rsi_at + (h - 1) * 3 + odd, sib).wait_send()

            @pl.when(k % 2 == 1)
            def _():
                rso[odd] = both.astype(bf16)
                remote(rso.at[odd], rsi.at[h, odd], rsi_at + h * 3 + odd, dev(1 + 2 * odd * final)).start()

        return carry

    def backward_from(first, last):
        lax.fori_loop(first, last, backward, 0)

    def relay(h):
        remote(rso.at[1], rsi.at[h, 1], rsi_at + h * 3 + 1, sib).wait_recv()
        rsx_out[h] = (rsx_out[h].astype(f32) + rsi[h, 1].astype(f32)).astype(bf16)
        return send(rsx_out.at[h], rsx_in.at[h], rsi_at + h * 3 + 2, dev(2))

    def keys_back(h, out, b):
        remote(rso.at[0], rsi.at[h, 0], rsi_at + h * 3, sib).wait_recv()
        across[h].wait_recv()
        total = dkv[h] + (rsi[h, 0].astype(f32) + rsx_in[h].astype(f32))
        if h == per - 1:
            remote(rso.at[1], rsi.at[h, 1], rsi_at + h * 3 + 1, sib).wait_recv()
            total = total + rsi[h, 1].astype(f32)
        for zb in range(GROUPS):
            tile = total[zb * rows : (zb + 1) * rows, :]
            back = jnp.where(low_half, turn_back(tile, cosb[zb], sinb[zb]), tile)
            out[zb, :, b : b + 2 * head] = back.astype(bf16)

    def queries_back(one, two, out, b):
        flat = jnp.concatenate([one, two], axis=0).T * scale
        for zb in range(GROUPS):
            tile = flat[zb * rows : (zb + 1) * rows, :]
            out[zb, :, b : b + 2 * head] = turn_back(tile, cosb[zb], sinb[zb]).astype(bf16)

    def scatter_rows(out, into, name):
        i = ids(name, 3)
        got = [send(out.at[(z + k) % 4], into.at[z], i + k - 1, zdev(k)) for k in (1, 2, 3)]
        into[z] = out[z]
        return got

    def projection(out, mine, other, summed, incoming, gathered, name):
        grad = dot(nl[...].reshape(line, width), out[...].reshape(line, out.shape[2]), 0, 0)
        for n in range(2 * CHIPS):
            mine[n % 2, n // 2] = grad[n * shard : (n + 1) * shard, :].astype(bf16)
        i = ids(name, 13)
        got = send(mine.at[1 - c], other, i, sib)
        yield
        got.wait_recv()
        summed[...] = (mine[c].astype(f32) + other[...].astype(f32)).astype(bf16)
        got = [send(summed.at[chip_of(k)], incoming.at[k - 1], i + k, dev(k)) for k in (1, 2, 3)]
        yield
        for copy in got:
            copy.wait_recv()
        whole = summed[chip].astype(f32)
        for k in range(3):
            whole = whole + incoming[k].astype(f32)
        gathered[z, chip, c] = whole.astype(bf16)
        src = gathered.at[z, chip, c]
        got = [send(src, src, i + 3 + k, zdev(k)) for k in (1, 2, 3)]
        yield
        for copy in got:
            copy.wait_recv()
        src = gathered.at[:, chip, c]
        over_y = send(src, src, i + 7, dev(1))
        over_x = send(src, src, i + 8, dev(2))
        last = [send(src, src, i + 9, sib)]
        yield
        over_x.wait_recv()
        src = gathered.at[:, chip_of(2), c]
        both = send(src, src, i + 10, dev(1))
        last.append(send(src, src, i + 11, sib))
        yield
        over_y.wait_recv()
        src = gathered.at[:, chip_of(1), c]
        last.append(send(src, src, i + 12, sib))
        both.wait_recv()
        src = gathered.at[:, chip_of(3), c]
        last.append(send(src, src, ids(name + "x", 1), sib))
        yield
        for copy in last:
            copy.wait_recv()
        yield

    across = {}
    backward_from(0, 8)
    next(down_path)
    bg1.wait_recv()
    bg3.wait_recv()
    for copy in got_mig:
        copy.wait_recv()
    grad = dot(mig[0], bgg[0], 1, 0)
    for n in range(1, tp_size):
        grad = grad + dot(mig[n], bgg[n], 1, 0)
    wide = width // 2
    wbuf[0:gw, :] = grad[:, 0:wide].astype(bf16)
    wbuf[gw : 2 * gw, :] = grad[:, wide:width].astype(bf16)
    out_path = exchange(wbuf, wsi, wz, wgt, 0, 2 * gw, "wo")
    next(out_path)
    result = finish_result() + down_b
    o_out[...] = (start[...] + gate2 * result).astype(bf16)
    vec[6:7, :] = column_sum(cot_ref[...].astype(f32) * result)
    backward_from(8, 16)
    across[0] = relay(0)
    next(down_path)
    next(up_path)
    backward_from(16, 20)
    across[1] = relay(1)
    backward_from(20, 24)
    across[2] = remote(rsx_out.at[per - 1], rsx_in.at[per - 1], rsi_at + per * 3 - 1, dev(2))
    pending.append(across[2])
    next(out_path)
    next(down_path)
    for copy in got_nl:
        copy.wait_recv()
    keys_back(0, pg1, kv_at[0])
    keys_back(1, pg1, kv_at[1])
    queries_back(dq[0, 0:head, :], dq[1, 0:head, :], pg1, q_at[0])
    got_pg1 = scatter_rows(pg1, pgi1, "pg1")
    first_path = projection(pg1, dwb1, dws1, dwc1, dwr1, wg1, "w1")
    next(first_path)
    keys_back(2, pg2, kv_at[2] - split)
    queries_back(dq[2, 0:head, :], jnp.zeros((head, line), f32), pg2, q_at[1] - split)
    got_pg2 = scatter_rows(pg2, pgi2, "pg2")
    second_path = projection(pg2, dwb2, dws2, dwc2, dwr2, wg2, "w2")
    next(second_path)
    next(first_path)
    next(up_path)
    next(out_path)
    next(second_path)
    next(first_path)
    next(down_path)
    next(second_path)
    next(up_path)
    next(out_path)
    for copy in got_pg1:
        copy.wait_recv()
    n1g = dot(pgi1[0], whm[0, :, 0:split], 1, 1)
    for g in range(1, GROUPS):
        n1g = n1g + dot(pgi1[g], whm[g, :, 0:split], 1, 1)
    for copy in got_pg2:
        copy.wait_recv()
    for g in range(GROUPS):
        n1g = n1g + dot(pgi2[g], whm[g, :, split : split + 4 * head], 1, 1)
    normal = normal1[...]
    vec[1:2, :] = column_sum(n1g)
    vec[2:3, :] = column_sum(n1g * normal)
    grad = normalise_back(n1g * (gain1 * (1.0 + scale1)), normal, spread1[...]) + middle_grad[...]
    o_in[...] = grad
    vec[0:1, :] = column_sum(grad * mcol[...])
    vpl[chip] = vec[...]
    i = ids("vp", 3)
    got_vp = [send(vec, vpl.at[chip], i + k - 1, dev(k)) for k in (1, 2, 3)]
    next(first_path)
    next(down_path)
    next(out_path)
    next(second_path)
    for copy in got_vp:
        copy.wait_recv()
    vzs[z, 0:8] = (vpl[0, 0:8] + vpl[1, 0:8]) + (vpl[2, 0:8] + vpl[3, 0:8])
    vzs[z, 8:16] = vpl[y, 8:16] + vpl[2 + y, 8:16]
    iv = ids("vz", 3)
    got_vz = [send(vzs.at[z], vzs.at[z], iv + k - 1, zdev(k)) for k in (1, 2, 3)]
    next(up_path)
    next(out_path)
    next(first_path)
    next(second_path)
    for copy in got_vz:
        copy.wait_recv()
    vco[c] = (vzs[0] + vzs[1]) + (vzs[2] + vzs[3])
    got_vc = send(vco.at[c], vco.at[c], ids("vc", 1), sib)
    next(out_path)
    og[t] = wgt[...]
    og1, og2, ogi = group_start(og, "og")
    next(up_path)
    next(first_path)
    next(second_path)
    got_vc.wait_recv()
    sums = vco[0] + vco[1]
    o_vec[0:1, :] = sums[0:1, :]
    o_vec[1:2, :] = sums[2:3, :] * (1.0 + scale1)
    o_vec[2:3, :] = sums[5:6, :] * (1.0 + scale2)
    o_vec[3:4, :] = sums[7:8, :]
    o_vec[4:5, :] = vco[c, 8:9, :]
    o_vec[5:8, :] = jnp.zeros((3, width), f32)
    o_vec[8:9, :] = sums[1:2, :]
    o_vec[9:10, :] = sums[2:3, :] * gain1
    o_vec[10:11, :] = sums[3:4, :]
    o_vec[11:12, :] = sums[4:5, :]
    o_vec[12:13, :] = sums[5:6, :] * gain2
    o_vec[13:14, :] = sums[6:7, :]
    o_vec[14:16, :] = jnp.zeros((2, width), f32)
    og3 = group_pass(og, og2, ogi)
    copies = []

    def write(src, dst):
        copies.append(pltpu.make_async_copy(src, dst, ls.at[len(copies)]))
        copies[-1].start()

    next(down_path)
    write(mgat.at[width : 2 * width], o_mlp.at[width : 2 * width])
    next(first_path)
    write(wg1, o_qkv1)
    next(second_path)
    write(wg2, o_qkv2)
    og1.wait_recv()
    og3.wait_recv()
    write(og, o_ow)
    next(up_path)
    write(mgat.at[0:width], o_mlp.at[0:width])
    for copy in pending:
        copy.wait_send()
    for k in range(CHIPS):
        remote(kvall.at[:, 0], kvall.at[:, 0], kdi + k, sib).wait_send()

    def drain(i, carry):
        remote(sbo.at[i], sbi.at[0, 0], sbx + (per - 1) * CHIPS + i, sib).wait_send()
        return carry

    lax.fori_loop(0, CHIPS, drain, 0)

    def drain(i, carry):
        remote(rso.at[i], rsi.at[0, 0], rsi_at + (per - 1) * 3 + i, sib).wait_send()
        return carry

    lax.fori_loop(0, 2, drain, 0)
    for copy in copies:
        copy.wait()


def rope_constants(length, rows, head):
    half = head // 2
    inverse = np.exp(np.float32(-math.log(10000.0)) * np.arange(half, dtype=np.float32) / half)
    angles = np.arange(length, dtype=np.float32)[:, None] * inverse.astype(np.float32)[None, :]
    angles = np.tile(angles, (1, 4)).astype(np.float64)
    shape = (length // rows, rows, 2 * head)
    return (
        jnp.asarray(np.cos(angles).astype(np.float32).reshape(shape)),
        jnp.asarray(np.sin(angles).astype(np.float32).reshape(shape)),
    )


def fused_device(
    seq_size,
    tp_size,
    tokens,
    cotangent,
    prefix_length,
    mask_flags,
    timestep,
    mask_embed,
    ln1_gain,
    ln2_gain,
    ada_weight,
    ada_bias,
    qkv_weight,
    out_weight,
    up_weight,
    up_bias,
    down_weight,
    down_bias,
):
    rows, width = tokens.shape
    head = width // HEADS
    per = HEADS // GROUPS
    gw = per * head
    line = GROUPS * rows
    packed = (per * 2 + 4) * head
    shard = width // (2 * CHIPS)
    cond = ada_weight.shape[0]
    cosine, sine = rope_constants(rows * seq_size * tp_size, rows, head)
    V = pltpu.VMEM
    vmem = pl.BlockSpec(memory_space=pltpu.VMEM)
    hbm = pl.BlockSpec(memory_space=pl.ANY)
    parts = (6 * head, 4 * head)
    outs = pl.pallas_call(
        functools.partial(fused_kernel, tp_size),
        out_shape=[
            jax.ShapeDtypeStruct((rows, width), bf16),
            jax.ShapeDtypeStruct((rows, width), f32),
            jax.ShapeDtypeStruct((16, width), f32),
            jax.ShapeDtypeStruct((GROUPS, CHIPS, 2, shard, parts[0]), bf16),
            jax.ShapeDtypeStruct((GROUPS, CHIPS, 2, shard, parts[1]), bf16),
            jax.ShapeDtypeStruct((tp_size, 2 * gw, width // 2), bf16),
            jax.ShapeDtypeStruct((2 * width, width), bf16),
        ],
        in_specs=[pl.BlockSpec(memory_space=pltpu.SMEM)] * 2
        + [vmem] * 9
        + [hbm] * 7,
        out_specs=[vmem] * 3 + [hbm] * 4,
        scratch_shapes=[
            V((width, width), bf16),
            V((width, width), bf16),
            V((width, width), bf16),
            V((8, width), f32),
            V((rows, width), f32),
            V((rows, width), f32),
            V((rows, 1), f32),
            V((rows, width), f32),
            V((rows, 1), f32),
            V((rows, width), f32),
            V((rows, width), f32),
            V((rows, 1), f32),
            V((GROUPS, rows, width), bf16),
            V((GROUPS, per, rows, 2 * head), bf16),
            V((GROUPS, 2, rows, 2 * head), bf16),
            V((GROUPS, 2, rows, 2 * head), bf16),
            V((GROUPS, width, packed), bf16),
            V((GROUPS, rows, 2 * head), f32),
            V((GROUPS, rows, 2 * head), f32),
            V((per, 2 * CHIPS, line, 2 * head), bf16),
            V((per, line, 2 * head), bf16),
            V((per, 2 * CHIPS, line, line), bf16),
            V((per, 2 * CHIPS, 1, line), f32),
            V((per, 1, line), f32),
            V((per, 1, line), f32),
            V((per, 2 * head, line), f32),
            V((per, 1, line), f32),
            V((per, 1, line), f32),
            V((GROUPS, gw, rows), bf16),
            V((GROUPS, gw, rows), bf16),
            V((tp_size, rows, width), bf16),
            V((tp_size, rows, width), bf16),
            V((tp_size, rows, width), bf16),
            V((tp_size, rows, width), bf16),
            V((tp_size, rows, width), f32),
            V((2, rows, width), f32),
            V((2, 2, rows, width), bf16),
            V((2, 2, rows, width), bf16),
            V((2, rows, width), bf16),
            V((2, rows, width), bf16),
            V((tp_size, rows, width), bf16),
            V((tp_size, gw, rows), bf16),
            V((GROUPS, gw, rows), bf16),
            V((GROUPS, gw, rows), bf16),
            V((per, 2 * head, line), bf16),
            V((CHIPS, line, 2 * head), bf16),
            V((per, CHIPS, line, 2 * head), bf16),
            V((2, line, 2 * head), bf16),
            V((per, 2, line, 2 * head), bf16),
            V((per, line, 2 * head), bf16),
            V((per, line, 2 * head), bf16),
            V((per, line, 2 * head), f32),
        ]
        + [V((GROUPS, rows, n), bf16) for n in parts for _ in range(2)]
        + [
            V(shape, bf16)
            for n in parts
            for shape in (
                (2, CHIPS, shard, n),
                (CHIPS, shard, n),
                (CHIPS, shard, n),
                (3, shard, n),
                (GROUPS, CHIPS, 2, shard, n),
            )
        ]
        + [
            V((2 * gw, width // 2), bf16),
            V((gw, width // 2), bf16),
            V((3, gw // GROUPS, width // 2), bf16),
            V((2 * gw, width // 2), bf16),
            V((tp_size, 2 * gw, width // 2), bf16),
            V((2 * width, width), bf16),
            V((width, width), bf16),
            V((2, 3, shard, width), bf16),
            V((2 * width, width), bf16),
            V((16, width), f32),
            V((CHIPS, 16, width), f32),
            V((GROUPS, 16, width), f32),
            V((2, 16, width), f32),
            pltpu.SemaphoreType.DMA((160,)),
            pltpu.SemaphoreType.DMA((160,)),
            pltpu.SemaphoreType.DMA((20,)),
        ],
        compiler_params=pltpu.CompilerParams(
            collective_id=0, has_side_effects=True, vmem_limit_bytes=VMEM_LIMIT
        ),
    )(
        prefix_length,
        timestep,
        mask_flags,
        mask_embed,
        ln1_gain,
        ln2_gain,
        up_bias,
        down_bias,
        ada_bias,
        tokens,
        cotangent,
        cosine,
        sine,
        ada_weight,
        qkv_weight,
        out_weight,
        up_weight,
        down_weight,
    )
    output, input_grad, sums, first, second, out_parts, mlp_parts = outs
    steps = 2 * CHIPS
    vector = jax.ShapeDtypeStruct((width,), f32)
    whole = pl.BlockSpec((width,), lambda n: (0,))

    def some(*shape):
        return jax.ShapeDtypeStruct(shape, f32)

    def rows_of(count, columns, skip=0):
        return pl.BlockSpec((count, columns), lambda n: (n + skip, 0))

    return pl.pallas_call(
        functools.partial(finish_kernel, per, head),
        grid=(steps,),
        out_shape=[
            jax.ShapeDtypeStruct((rows, width), bf16),
            some(rows, width),
            vector,
            vector,
            vector,
            some(cond, 6 * width),
            some(6 * width),
            some(width, 3 * width),
            some(width, width),
            some(width, width),
            vector,
            some(width, width),
            vector,
        ],
        in_specs=[
            pl.BlockSpec(memory_space=pltpu.SMEM),
            pl.BlockSpec((16, width), lambda n: (0, 0)),
            rows_of(rows // steps, width),
            rows_of(rows // steps, width),
            pl.BlockSpec((GROUPS, 1, shard, parts[0]), lambda n: (0, n, 0, 0)),
            pl.BlockSpec((GROUPS, 1, shard, parts[1]), lambda n: (0, n, 0, 0)),
            pl.BlockSpec((1, 2, shard, width // 2), lambda n: (n // 2, 0, n % 2, 0)),
            rows_of(shard, width),
            rows_of(shard, width, steps),
        ],
        out_specs=[
            rows_of(rows // steps, width),
            rows_of(rows // steps, width),
            whole,
            whole,
            whole,
            rows_of(cond // steps, 6 * width),
            pl.BlockSpec((6 * width,), lambda n: (0,)),
            rows_of(shard, 3 * width),
            rows_of(shard, width),
            rows_of(shard, width),
            whole,
            rows_of(shard, width),
            whole,
        ],
    )(
        timestep,
        sums,
        output,
        input_grad,
        first.reshape(GROUPS, steps, shard, parts[0]),
        second.reshape(GROUPS, steps, shard, parts[1]),
        out_parts.reshape(tp_size, 2, gw, width // 2),
        mlp_parts,
        mlp_parts,
    )


def solution(mesh):
    seq_size, tp_size = mesh.shape["seq"], mesh.shape["tp"]
    small = seq_size == 2 * GROUPS and tp_size == CHIPS
    in_specs = (
        P(("seq", "tp"), None),
        P(("seq", "tp"), None),
        P(),
        P(("seq", "tp")),
        P(),
        P(),
        P(),
        P(),
        P(),
        P(),
        P(),
        P(),
        P(None, "tp"),
        P("tp"),
        P("tp", None),
        P(),
    )
    out_specs = (
        P(("seq", "tp"), None),
        P(("seq", "tp"), None),
        P(),
        P(),
        P(),
        P(),
        P(),
        P(),
        P(),
        P(None, "tp"),
        P("tp"),
        P("tp", None),
        P(),
    )
    return jax.shard_map(
        functools.partial(fused_device, seq_size, tp_size) if small else per_device,
        mesh=mesh, in_specs=in_specs, out_specs=out_specs, check_vma=False
    )
```

```python
import functools
import math

import jax
import jax.numpy as jnp
import numpy as np
from jax import lax
from jax.experimental import pallas as pl
from jax.experimental.pallas import tpu as pltpu
from jax.sharding import PartitionSpec as P

HEADS = 12


epsilon = 1e-05
highest = lax.Precision.HIGHEST
floor_value = -1e30


def layer_norm(inputs, norm_gain):
    centred = inputs - jnp.mean(inputs, axis=-1, keepdims=True)
    variance = jnp.mean(centred * centred, axis=-1, keepdims=True)
    return centred * lax.rsqrt(variance + epsilon) * norm_gain


def modulate(inputs, norm_gain, shift_vector, scale_vector):
    return layer_norm(inputs, norm_gain) * (1.0 + scale_vector) + shift_vector


def rotary_tables(positions, head_width):
    halfway = head_width // 2
    inverse = jnp.exp(-math.log(10000.0) * jnp.arange(halfway, dtype=jnp.float32) / halfway)
    angles = positions.astype(jnp.float32)[:, None] * inverse[None, :]
    angles = jnp.concatenate([angles, angles], axis=1)
    return (jnp.cos(angles), jnp.sin(angles))


def rotate(head_rows, cosine, sine):
    halfway = head_rows.shape[-1] // 2
    turned = jnp.concatenate([-head_rows[..., halfway:], head_rows[..., :halfway]], axis=-1)
    return head_rows * cosine[:, None, :] + turned * sine[:, None, :]


def time_embedding(timestep, embed_width):
    halfway = embed_width // 2
    rates = jnp.exp(-math.log(10000.0) * jnp.arange(halfway, dtype=jnp.float32) / halfway)
    angles = timestep[0].astype(jnp.float32) * rates
    return jnp.concatenate([jnp.cos(angles), jnp.sin(angles)])


def block_length(total_rows, other_count):
    pieces = total_rows // other_count
    widest = 1 << max(0, (2048 // other_count).bit_length() - 1)
    size = other_count * math.gcd(pieces, widest)
    return size


def over_blocks(running, row_arrays, other_count, advance):
    total_rows = row_arrays[0].shape[0]
    block_size = block_length(total_rows, other_count)

    def one_turn(block_index, current):
        block_start = block_index * block_size
        blocks = tuple(
            (lax.dynamic_slice_in_dim(array, block_start, block_size, 0) for array in row_arrays)
        )
        return advance(current, blocks)

    return lax.fori_loop(0, total_rows // block_size, one_turn, running)


def forward_update(running, queries, key_block, value_block, score_scale):
    highest_seen, totals, weighted = running
    scores = (
        jnp.einsum("qhd,khd->hqk", queries, key_block, preferred_element_type=jnp.float32)
        * score_scale
    )
    new_highest = jnp.maximum(highest_seen, jnp.max(scores, axis=-1))
    factor = jnp.exp(highest_seen - new_highest)
    weights = jnp.exp(scores - new_highest[:, :, None])
    totals = totals * factor + jnp.sum(weights, axis=-1)
    weighted = weighted * factor.T[:, :, None] + jnp.einsum(
        "hqk,khd->qhd",
        weights.astype(jnp.bfloat16),
        value_block,
        preferred_element_type=jnp.float32,
    )
    return (new_highest, totals, weighted)


def query_update(
    query_grad, queries, mixed_grad, logsum, delta, key_block, value_block, score_scale
):
    scores = (
        jnp.einsum("qhd,khd->hqk", queries, key_block, preferred_element_type=jnp.float32)
        * score_scale
    )
    probs = jnp.exp(scores - logsum[:, :, None])
    prob_grad = jnp.einsum(
        "qhd,khd->hqk", mixed_grad, value_block, preferred_element_type=jnp.float32
    )
    score_grad = (probs * (prob_grad - delta[:, :, None])).astype(jnp.bfloat16)
    return query_grad + score_scale * jnp.einsum(
        "hqk,khd->qhd", score_grad, key_block, preferred_element_type=jnp.float32
    )


def key_update(
    running, query_block, grad_block, logsum_block, delta_block, own_keys, own_values, score_scale
):
    key_grad, value_grad = running
    scores = (
        jnp.einsum("qhd,khd->hqk", query_block, own_keys, preferred_element_type=jnp.float32)
        * score_scale
    )
    probs = jnp.exp(scores - logsum_block.T[:, :, None])
    value_grad = value_grad + jnp.einsum(
        "hqk,qhd->khd", probs.astype(jnp.bfloat16), grad_block, preferred_element_type=jnp.float32
    )
    prob_grad = jnp.einsum(
        "qhd,khd->hqk", grad_block, own_values, preferred_element_type=jnp.float32
    )
    score_grad = (probs * (prob_grad - delta_block.T[:, :, None])).astype(jnp.bfloat16)
    key_grad = key_grad + score_scale * jnp.einsum(
        "hqk,qhd->khd", score_grad, query_block, preferred_element_type=jnp.float32
    )
    return (key_grad, value_grad)


def to_heads(rows):
    return lax.all_to_all(rows, "tp", split_axis=1, concat_axis=0, tiled=True)


def to_rows(rows):
    return lax.all_to_all(rows, "tp", split_axis=0, concat_axis=1, tiled=True)


def per_device(
    tokens,
    cotangent,
    prefix_length,
    mask_flags,
    timestep,
    mask_embed,
    ln1_gain,
    ln2_gain,
    ada_weight,
    ada_bias,
    qkv_weight,
    out_weight,
    up_weight,
    up_bias,
    down_weight,
    down_bias,
):
    row_count = tokens.shape[0]
    model_width = tokens.shape[1]
    head_count = HEADS
    head_width = model_width // head_count
    score_scale = head_width ** (-0.5)
    positions = lax.axis_index(("seq", "tp")) * row_count + jnp.arange(row_count, dtype=jnp.int32)
    masked = ((positions >= prefix_length[0]) & (mask_flags == 1)).astype(jnp.float32)
    activation = jax.nn.silu(time_embedding(timestep, ada_weight.shape[0]))
    modulation = jnp.dot(
        activation, ada_weight.astype(jnp.float32), precision=highest
    ) + ada_bias.astype(jnp.float32)
    shift_one, scale_one, gate_one, shift_two, scale_two, gate_two = jnp.split(modulation, 6)
    cosine, sine = rotary_tables(positions, head_width)
    gain_one = ln1_gain.astype(jnp.float32)
    gain_two = ln2_gain.astype(jnp.float32)
    start = tokens.astype(jnp.float32) + masked[:, None] * mask_embed.astype(jnp.float32)[None, :]
    normed = modulate(start, gain_one, shift_one, scale_one).astype(jnp.bfloat16)
    projected = jnp.dot(normed, qkv_weight, preferred_element_type=jnp.float32)
    split_rows = projected.reshape(row_count, 3, head_count, head_width)
    queries, key_rows, value_rows = (
        to_heads(rows.reshape(row_count, model_width).astype(jnp.bfloat16))
        for rows in (
            rotate(split_rows[:, 0], cosine, sine),
            rotate(split_rows[:, 1], cosine, sine),
            split_rows[:, 2],
        )
    )
    group_size, group_width = queries.shape
    head_group = group_width // head_width
    queries = queries.reshape(group_size, head_group, head_width)
    every_key = lax.all_gather(key_rows, "seq", axis=0, tiled=True)
    every_value = lax.all_gather(value_rows, "seq", axis=0, tiled=True)
    initial = (
        jnp.full((head_group, group_size), floor_value, jnp.float32),
        jnp.zeros((head_group, group_size), jnp.float32),
        jnp.zeros((group_size, head_group, head_width), jnp.float32),
    )

    def advance(current, blocks):
        return forward_update(
            current,
            queries,
            blocks[0].reshape(-1, head_group, head_width),
            blocks[1].reshape(-1, head_group, head_width),
            score_scale,
        )

    running = over_blocks(
        initial,
        (every_key, every_value),
        group_size,
        advance,
    )
    highest_seen, totals, weighted = running
    logsum = highest_seen + jnp.log(totals)
    attended = weighted / totals.T[:, :, None]
    mixed = to_rows(attended.reshape(group_size, group_width).astype(jnp.bfloat16))
    branch = jnp.dot(mixed, out_weight, preferred_element_type=jnp.float32)
    middle = start + gate_one * branch
    normed_two = modulate(middle, gain_two, shift_two, scale_two).astype(jnp.bfloat16)
    group_rows = lax.all_gather(normed_two, "tp", axis=0, tiled=True)
    hidden = jnp.dot(group_rows, up_weight, preferred_element_type=jnp.float32) + up_bias.astype(
        jnp.float32
    )
    active = jax.nn.gelu(hidden).astype(jnp.bfloat16)
    result = lax.psum_scatter(
        jnp.dot(active, down_weight, preferred_element_type=jnp.float32).astype(jnp.bfloat16),
        "tp",
        scatter_dimension=0,
        tiled=True,
    ).astype(jnp.float32) + down_bias.astype(jnp.float32)
    output = (middle + gate_two * result).astype(jnp.bfloat16)
    upstream = cotangent.astype(jnp.float32)
    result_grad = (upstream * gate_two).astype(jnp.bfloat16)
    gate_two_grad = jnp.sum(upstream * result, axis=0)
    down_bias_grad = jnp.sum(result_grad.astype(jnp.float32), axis=0)
    group_grads = lax.all_gather(result_grad, "tp", axis=0, tiled=True)
    down_weight_grad = jnp.dot(active.T, group_grads, preferred_element_type=jnp.float32)
    active_grad = jnp.dot(group_grads, down_weight.T, preferred_element_type=jnp.float32)
    unused, gelu_back = jax.vjp(jax.nn.gelu, hidden)
    hidden_grad = gelu_back(active_grad)[0].astype(jnp.bfloat16)
    up_bias_grad = jnp.sum(hidden_grad.astype(jnp.float32), axis=0)
    up_weight_grad = jnp.dot(group_rows.T, hidden_grad, preferred_element_type=jnp.float32)
    normed_two_grad = lax.psum_scatter(
        jnp.dot(hidden_grad, up_weight.T, preferred_element_type=jnp.float32).astype(jnp.bfloat16),
        "tp",
        scatter_dimension=0,
        tiled=True,
    ).astype(jnp.float32)
    unused, second_back = jax.vjp(modulate, middle, gain_two, shift_two, scale_two)
    middle_part, gain_two_grad, shift_two_grad, scale_two_grad = second_back(normed_two_grad)
    middle_grad = middle_part + upstream
    gate_one_grad = jnp.sum(middle_grad * branch, axis=0)
    branch_grad = (middle_grad * gate_one).astype(jnp.bfloat16)
    out_weight_grad = jnp.dot(mixed.T, branch_grad, preferred_element_type=jnp.float32)
    mixed_grad = to_heads(
        jnp.dot(branch_grad, out_weight.T, preferred_element_type=jnp.float32).astype(jnp.bfloat16)
    ).reshape(group_size, head_group, head_width)
    delta_rows = jnp.sum(mixed_grad.astype(jnp.float32) * attended, axis=-1)
    delta = delta_rows.T
    initial_query = jnp.zeros((group_size, head_group, head_width), jnp.float32)

    def advance(grads_now, blocks):
        return query_update(
            grads_now,
            queries,
            mixed_grad,
            logsum,
            delta,
            blocks[0].reshape(-1, head_group, head_width),
            blocks[1].reshape(-1, head_group, head_width),
            score_scale,
        )

    query_grad = over_blocks(
        initial_query,
        (every_key, every_value),
        group_size,
        advance,
    )
    every_logsum, every_delta = (
        lax.all_gather(logsum.T, "seq", axis=0, tiled=True),
        lax.all_gather(delta_rows, "seq", axis=0, tiled=True),
    )
    own_keys = key_rows.reshape(group_size, head_group, head_width)
    own_values = value_rows.reshape(group_size, head_group, head_width)
    initial_keys = (
        jnp.zeros((group_size, head_group, head_width), jnp.float32),
        jnp.zeros((group_size, head_group, head_width), jnp.float32),
    )

    def advance(grads_now, blocks):
        return key_update(
            grads_now,
            blocks[0].reshape(-1, head_group, head_width),
            blocks[1].reshape(-1, head_group, head_width),
            blocks[2],
            blocks[3],
            own_keys,
            own_values,
            score_scale,
        )

    key_grad, value_grad = over_blocks(
        initial_keys,
        (
            lax.all_gather(queries.reshape(group_size, group_width), "seq", axis=0, tiled=True),
            lax.all_gather(mixed_grad.reshape(group_size, group_width), "seq", axis=0, tiled=True),
            every_logsum,
            every_delta,
        ),
        group_size,
        advance,
    )
    query_rows, key_part_rows, value_grad_rows = (
        to_rows(rows.reshape(group_size, group_width)).reshape(row_count, head_count, head_width)
        for rows in (query_grad, key_grad, value_grad)
    )
    unused, rotate_back = jax.vjp(lambda head_rows: rotate(head_rows, cosine, sine), query_rows)
    query_part = rotate_back(query_rows)[0].reshape(row_count, model_width)
    key_part = rotate_back(key_part_rows)[0].reshape(row_count, model_width)
    projected_grad = jnp.concatenate(
        [query_part, key_part, value_grad_rows.reshape(row_count, model_width)], axis=1
    ).astype(jnp.bfloat16)
    qkv_weight_grad = jnp.dot(normed.T, projected_grad, preferred_element_type=jnp.float32)
    normed_grad = jnp.dot(projected_grad, qkv_weight.T, preferred_element_type=jnp.float32)
    unused, first_back = jax.vjp(modulate, start, gain_one, shift_one, scale_one)
    start_part, gain_one_grad, shift_one_grad, scale_one_grad = first_back(normed_grad)
    start_grad = start_part + middle_grad
    embed_grad = jnp.sum(masked[:, None] * start_grad, axis=0)
    modulation_grad = jnp.concatenate(
        [
            shift_one_grad,
            scale_one_grad,
            gate_one_grad,
            shift_two_grad,
            scale_two_grad,
            gate_two_grad,
        ]
    )
    summed = lax.psum(
        (
            qkv_weight_grad,
            out_weight_grad,
            modulation_grad,
            gain_one_grad,
            gain_two_grad,
            down_bias_grad,
            embed_grad,
        ),
        ("seq", "tp"),
    )
    split_sums = lax.psum((up_weight_grad, up_bias_grad, down_weight_grad), "seq")
    return (
        output,
        start_grad,
        summed[6],
        summed[3],
        summed[4],
        activation[:, None] * summed[2][None, :],
        summed[2],
        summed[0],
        summed[1],
        split_sums[0],
        split_sums[1],
        split_sums[2],
        summed[5],
    )


ORDER = (
    "d1_dw d2_dw ln2b u1_dw",
    "d1_1 u2_dw res bgp",
    "d2_1 d1_2 L1 u1_1",
    "d2_2 d1_3 wo L2",
    "u1_2 o_1 d2_3 rel0",
    "L3a rel1 o_2 d1_4",
    "u1_3 L3b o_3 por1",
    "o_4 w1_a u2_1 por2",
    "w2_a o_5 w2_b d1_5",
    "resfin u2_2 u1_4 o_end",
    "w1_b og n1g w2_c",
    "d2_4 u1_5 u2_3 w2_d",
    "w1_c v1 u2_4 d2_5",
    "og2 d1_end w2_e w1_d",
    "og3 w2_end u2_5 v2",
    "v3 w1_e d2_end u1_end",
    "w1_end u2_end",
)
VMEM_LIMIT = 63 * 2**20
GROUPS = 4
CHIPS = 4
MESH = pl.DeviceIdType.MESH
f32, bf16 = jnp.float32, jnp.bfloat16


def dot(left, right, left_dim, right_dim):
    return lax.dot_general(
        left, right, (((left_dim,), (right_dim,)), ((), ())), preferred_element_type=f32
    )


def normalise(rows):
    centred = rows - jnp.mean(rows, axis=-1, keepdims=True)
    variance = jnp.mean(centred * centred, axis=-1, keepdims=True)
    spread = lax.rsqrt(variance + epsilon)
    return centred * spread, spread


def normalise_back(upstream, normal, spread):
    along = jnp.mean(upstream * normal, axis=-1, keepdims=True)
    return spread * (upstream - jnp.mean(upstream, axis=-1, keepdims=True) - normal * along)


def column_sum(rows):
    return jnp.sum(rows, axis=0, keepdims=True)


def row_of(ref, i, width):
    return ref[i * width : (i + 1) * width].astype(f32).reshape(1, width)


def activation_of(step, first, count, cond):
    halfway = cond // 2
    place = first + lax.broadcasted_iota(jnp.int32, (count, 1), 0)
    which = jnp.where(place < halfway, place, place - halfway).astype(f32)
    angles = step.astype(f32) * jnp.exp(-math.log(10000.0) * which / halfway)
    wave = jnp.where(place < halfway, jnp.cos(angles), jnp.sin(angles))
    return wave / (1.0 + jnp.exp(-wave))


def finish_kernel(
    per,
    head,
    timestep_ref,
    sums,
    output,
    input_grad,
    first,
    second,
    out_parts,
    up_parts,
    down_parts,
    o_out,
    o_in,
    o_embed,
    o_gain1,
    o_gain2,
    o_ada,
    o_ada_b,
    o_qkv,
    o_ow,
    o_up,
    o_up_b,
    o_down,
    o_down_b,
):
    n = pl.program_id(0)
    width = sums.shape[1]
    o_out[...] = output[...]
    o_in[...] = input_grad[...]
    o_up[...] = up_parts[...].astype(f32)
    o_down[...] = down_parts[...].astype(f32)
    wide = out_parts.shape[3]
    for m in range(2):
        o_ow[:, m * wide : (m + 1) * wide] = out_parts[0, m].astype(f32)
    count = o_ada.shape[0]
    act = activation_of(timestep_ref[0], n * count, count, count * 8)
    for i in range(6):
        o_ada[:, i * width : (i + 1) * width] = act * sums[8 + i : 9 + i, :]

    def piece(third, j):
        g, h = j // per, j % per
        source = first if h < 2 else second
        a = (4 + h % 2) * head if third == 0 else h % 2 * 2 * head + (third - 1) * head
        if h == 2 and third == 0:
            a = 2 * head
        return source[g, 0, :, a : a + head].astype(f32)

    for third in range(3):
        for j in range(0, GROUPS * per, 2):
            a = third * width + j * head
            o_qkv[:, a : a + 2 * head] = jnp.concatenate(
                [piece(third, j), piece(third, j + 1)], axis=1
            )

    @pl.when(n == 0)
    def _():
        for ref, i in ((o_embed, 0), (o_gain1, 1), (o_gain2, 2), (o_down_b, 3), (o_up_b, 4)):
            ref[...] = sums[i : i + 1, :].reshape(width)
        for i in range(6):
            o_ada_b[i * width : (i + 1) * width] = sums[8 + i : 9 + i, :].reshape(width)


def fused_kernel(
    tp_size,
    prefix_ref,
    timestep_ref,
    flags_ref,
    embed_ref,
    gain1_ref,
    gain2_ref,
    up_b_ref,
    down_b_ref,
    ada_b_ref,
    tokens_ref,
    cot_ref,
    cos_hbm,
    sin_hbm,
    ada_hbm,
    qkv_hbm,
    out_hbm,
    up_hbm,
    down_hbm,
    o_out,
    o_in,
    o_vec,
    o_qkv1,
    o_qkv2,
    o_ow,
    o_mlp,
    out_w,
    up_w,
    down_w,
    mod,
    start,
    normal1,
    spread1,
    normal2,
    spread2,
    branch,
    mcol,
    nl,
    qi,
    whm,
    cosb,
    sinb,
    kvall,
    qd,
    expd,
    tops,
    mrun,
    lrun,
    ot,
    lse,
    delta,
    mtb,
    mi,
    rg,
    ng,
    acts,
    hgs,
    ag,
    pn_own,
    pn_so,
    pn_si,
    pn_yo,
    pn_yi,
    bgg,
    mig,
    doi,
    dos,
    sbo,
    sbi,
    rso,
    rsi,
    rsx_out,
    rsx_in,
    dkv,
    pg1,
    pgi1,
    pg2,
    pgi2,
    dwb1,
    dws1,
    dwc1,
    dwr1,
    wg1,
    dwb2,
    dws2,
    dwc2,
    dwr2,
    wg2,
    wbuf,
    wsi,
    wz,
    wgt,
    og,
    mbuf,
    msi,
    mz,
    mgat,
    vec,
    vpl,
    vzs,
    vco,
    ss,
    rr,
    ls,
):
    rows, width = tokens_ref.shape
    head = width // HEADS
    per = HEADS // GROUPS
    gw = per * head
    line = GROUPS * rows
    shard = width // (2 * CHIPS)
    kv_at = [0, 2 * head, 6 * head]
    q_at = [4 * head, 8 * head]
    split = 6 * head
    s, t = lax.axis_index("seq"), lax.axis_index("tp")
    z, x, y, c = s // 2, s % 2, t // 2, t % 2
    sib = (s, t + 1 - 2 * c)
    chip = x * 2 + y
    p = chip * 2 + c

    def chip_of(k):
        return ((x + k // 2) % 2) * 2 + (y + k % 2) % 2

    def dev(k):
        return (z * 2 + (x + k // 2) % 2, ((y + k % 2) % 2) * 2 + c)

    def zdev(k):
        return (((z + k) % 4) * 2 + x, t)

    def zfrom(k):
        return (z + 4 - k) % 4

    names = {}

    def ids(name, count):
        if name not in names:
            names[name] = sum(n for _, n in names.values()), count
        return names[name][0]

    def remote(src, dst, i, to):
        return pltpu.make_async_remote_copy(
            src_ref=src,
            dst_ref=dst,
            send_sem=ss.at[i],
            recv_sem=rr.at[i],
            device_id=to,
            device_id_type=MESH,
        )

    pending = []

    def send(src, dst, i, to):
        copy = remote(src, dst, i, to)
        copy.start()
        pending.append(copy)
        return copy

    barrier = pltpu.get_barrier_semaphore()
    t_sib, t_y = y * 2 + 1 - c, (1 - y) * 2 + c
    t_ysib = (1 - y) * 2 + 1 - c
    ysib = (s, t_ysib)
    peers = [sib, ysib] + [dev(k) for k in (1, 2, 3)] + [zdev(k) for k in (1, 2, 3)]
    for peer in peers:
        pl.semaphore_signal(barrier, inc=1, device_id=peer, device_id_type=MESH)

    locals_ = []

    def local(src, dst, i):
        copy = pltpu.make_async_copy(src, dst, ls.at[i])
        copy.start()
        locals_.append(copy)
        return copy

    cond = ada_hbm.shape[0]
    ada = [
        local(ada_hbm.at[:, i * width : (i + 1) * width], msi.at[i * cond : (i + 1) * cond], 11 + i)
        for i in range(6)
    ]
    stage = [mbuf.at[0:width], mbuf.at[width : 2 * width], mgat.at[0:width]]
    raw = []
    for zb in range(GROUPS):
        block = (zb * 2 + x) * tp_size + t
        raw.append(local(cos_hbm.at[block], cosb.at[zb], zb))
        raw.append(local(sin_hbm.at[block], sinb.at[zb], 4 + zb))
    raw += [local(qkv_hbm.at[:, i * width : (i + 1) * width], stage[i], 8 + i) for i in range(3)]
    loads = zip((down_hbm, out_hbm, up_hbm), (down_w, out_w, up_w))
    weights = [local(src, dst, 17 + i) for i, (src, dst) in enumerate(loads)]
    act = activation_of(timestep_ref[0], 0, cond, cond)
    def modulate_rows(first, last):
        for i in range(first, last):
            ada[i].wait()
            part = msi[i * cond : (i + 1) * cond, :].astype(f32)
            mod[i : i + 1, :] = column_sum(part * act) + row_of(ada_b_ref, i, width)

    modulate_rows(0, 2)
    shift1, scale1 = mod[0:1, :], mod[1:2, :]
    embed, gain1, gain2, up_b, down_b = (
        row_of(ref, 0, width) for ref in (embed_ref, gain1_ref, gain2_ref, up_b_ref, down_b_ref)
    )
    place = (s * tp_size + t) * rows + lax.broadcasted_iota(jnp.int32, (1, rows), 1)
    chosen = jnp.where((place >= prefix_ref[0]) & (flags_ref[...].reshape(1, rows) == 1), 1.0, 0.0).astype(f32)
    mcol[...] = jnp.broadcast_to(chosen, (rows, rows)).T[:, 0:1]
    start[...] = tokens_ref[...].astype(f32) + mcol[...] * embed
    normal, spread = normalise(start[...])
    normal1[...] = normal
    spread1[...] = spread
    nl[z] = (normal * (gain1 * (1.0 + scale1)) + shift1).astype(bf16)

    pl.semaphore_wait(barrier, len(peers))

    def group_start(buffer, name):
        i = ids(name, 3)
        one = send(buffer.at[t], buffer.at[t], i, sib)
        two = send(buffer.at[t], buffer.at[t], i + 1, dev(1))
        return one, two, i + 2

    def group_pass(buffer, two, i):
        two.wait_recv()
        other = (1 - y) * 2 + c
        return send(buffer.at[other], buffer.at[other], i, sib)


    for copy in raw:
        copy.wait()
    lane = lax.broadcasted_iota(jnp.int32, (rows, 2 * head), 1)
    low_half = lane < head
    first = (lane % head) < head // 2
    half = head // 2

    def turn(tile, cosine, sine):
        ahead = jnp.where(first, -pltpu.roll(tile, 2 * head - half, 1), pltpu.roll(tile, half, 1))
        return tile * cosine + ahead * sine

    def turn_back(tile, cosine, sine):
        moved = tile * sine
        behind = jnp.where(first, pltpu.roll(moved, 2 * head - half, 1), -pltpu.roll(moved, half, 1))
        return tile * cosine + behind

    kvi = ids("kv", 12)
    scale = head ** (-0.5)
    cosine, sine = cosb[z], sinb[z]
    thirds = [dot(nl[z], ref[...], 1, 0) for ref in stage]

    def of_head(third, n):
        return thirds[third][:, n * head : (n + 1) * head]

    for g in range(GROUPS):
        for h in range(per):
            n = g * per + h
            tile = jnp.concatenate([of_head(1, n), of_head(2, n)], axis=1)
            rsx_out[h, g * rows : (g + 1) * rows, :] = jnp.where(
                low_half, turn(tile, cosine, sine), tile
            ).astype(bf16)
    here = pl.ds(z * rows, rows)

    def out_of(ref, g):
        return ref.at[:, pl.ds(g * rows, rows), :]

    zi = ids("kvz", 3)
    got_kv = []
    for k in (1, 2, 3):
        there = kvall.at[:, p, here, :]
        got_kv.append(send(out_of(rsx_out, (z + k) % 4), there, zi + k - 1, zdev(k)))
    kvall[:, p, here, :] = rsx_out[:, here, :]

    def over_plane(k):
        src = kvall.at[:, p, pl.ds(zfrom(k) * rows, rows), :]
        for kk in (1, 2, 3):
            send(src, src, kvi + (kk - 1) * 4 + k, dev(kk))

    over_plane(0)
    for g in range(GROUPS):
        n = g * per
        tile = turn(thirds[0][:, n * head : (n + 2) * head], cosine, sine) * scale
        rso[0, g * rows : (g + 1) * rows, :] = tile.astype(bf16)
        tile = jnp.concatenate([of_head(0, n + 2), jnp.zeros((rows, head), f32)], axis=1)
        rso[1, g * rows : (g + 1) * rows, :] = (turn(tile, cosine, sine) * scale).astype(bf16)
    qi[z] = rso[:, here, :]
    for g in range(GROUPS):
        for h in range(per):
            a = g * gw + h * head
            tile = [mbuf[width : 2 * width, a : a + head], mgat[0:width, a : a + head]]
            whm[g, :, kv_at[h] : kv_at[h] + 2 * head] = jnp.concatenate(tile, axis=1)
        a = g * gw
        whm[g, :, q_at[0] : q_at[0] + 2 * head] = mbuf[0:width, a : a + 2 * head]
        tile = [mbuf[0:width, a + 2 * head : a + 3 * head], jnp.zeros((width, head), bf16)]
        whm[g, :, q_at[1] : q_at[1] + 2 * head] = jnp.concatenate(tile, axis=1)

    modulate_rows(2, 6)
    gate1, shift2 = mod[2:3, :], mod[3:4, :]
    scale2, gate2 = mod[4:5, :], mod[5:6, :]
    rg[t] = (cot_ref[...].astype(f32) * gate2).astype(bf16)
    rg1, rg2, rgi = group_start(rg, "rg")
    for k in (1, 2, 3):
        got_kv[k - 1].wait_recv()
        over_plane(k)
    i = ids("q", 3)
    got_q = [send(out_of(rso, (z + k) % 4), qi.at[z], i + k - 1, zdev(k)) for k in (1, 2, 3)]
    kdi = ids("kvd", 4)
    remote(kvall.at[:, p], kvall.at[:, p], kdi, sib).start()
    for copy in got_q:
        copy.wait_recv()
    for zb in range(GROUPS):
        at = slice(zb * rows, (zb + 1) * rows)
        pair, last = qi[zb, 0].astype(f32), qi[zb, 1].astype(f32)
        qd[0, at, :] = jnp.where(low_half, pair, 0.0).astype(bf16)
        qd[1, at, :] = jnp.where(low_half, pltpu.roll(pair, head, 1), 0.0).astype(bf16)
        qd[2, at, :] = jnp.where(low_half, last, 0.0).astype(bf16)

    mrun[...] = jnp.full_like(mrun, floor_value)
    lrun[...] = jnp.zeros_like(lrun)
    ot[...] = jnp.zeros_like(ot)

    def forward(i, carry):
        k, away = i // 2, i % 2
        chunk = chip_of(k) * 2 + (c + away) % 2

        @pl.when((away == 0) & (k > 0))
        def _():
            for q in range(GROUPS):
                block = kvall.at[:, chunk, pl.ds(q * rows, rows), :]
                remote(block, block, kvi + (k - 1) * 4 + q, sib).wait_recv()
            remote(kvall.at[:, chunk], kvall.at[:, chunk], kdi + k, sib).start()

        @pl.when(away == 1)
        def _():
            remote(kvall.at[:, chunk], kvall.at[:, chunk], kdi + k, sib).wait_recv()

        scores = [dot(kvall[h, chunk], qd[h], 1, 1) for h in range(per)]
        for h in range(per):
            before = mrun[h]
            top = jnp.maximum(before, jnp.max(scores[h], axis=0, keepdims=True))
            weights = jnp.exp(scores[h] - top)
            factor = jnp.exp(before - top)
            rounded = weights.astype(bf16)
            expd[h, chunk] = rounded
            lrun[h] = lrun[h] * factor + column_sum(weights)
            mrun[h] = top
            tops[h, chunk] = top
            ot[h] = ot[h] * factor + dot(kvall[h, chunk], rounded, 0, 0)
        return carry

    lax.fori_loop(0, 2 * CHIPS, forward, 0)

    for h in range(per):
        ot[h] = ot[h] / lrun[h]
        lse[h] = mrun[h] + jnp.log(lrun[h])
        for zb in range(GROUPS):
            mtb[zb, h * head : (h + 1) * head, :] = ot[
                h, head : 2 * head, zb * rows : (zb + 1) * rows
            ].astype(bf16)
    i = ids("mix", 3)
    got_mix = [send(mtb.at[(z + k) % 4], mi.at[z], i + k - 1, zdev(k)) for k in (1, 2, 3)]
    mi[z] = mtb[z]
    rg3 = group_pass(rg, rg2, rgi)
    rg1.wait_recv()
    rg3.wait_recv()
    weights[0].wait()
    for tb in range(tp_size):
        ag[tb] = dot(rg[tb], down_w[...], 1, 1).astype(bf16)
    for copy in got_mix:
        copy.wait_recv()
    i = ids("nl", 3)
    got_nl = [send(nl.at[z], nl.at[z], i + k - 1, zdev(k)) for k in (1, 2, 3)]
    weights[1].wait()
    weights[2].wait()
    total = dot(mi[0], out_w[0:gw, :], 0, 0)
    for g in range(1, GROUPS):
        total = total + dot(mi[g], out_w[g * gw : (g + 1) * gw, :], 0, 0)
    branch[...] = total
    start[...] = start[...] + gate1 * total
    normal, spread = normalise(start[...])
    normal2[...] = normal
    spread2[...] = spread
    ng[t] = (normal * (gain2 * (1.0 + scale2)) + shift2).astype(bf16)
    piece = rows // 2
    halves = [pl.ds(n * piece, piece) for n in range(2)]

    def to_group(buffer, name):
        i = ids(name, 6)
        got = []
        for n, at in enumerate(halves):
            src = buffer.at[t, at]
            got.append((send(src, src, i + 3 * n, sib), send(src, src, i + 3 * n + 1, dev(1))))
        return got, i

    def pass_group(buffer, got, i, n):
        got[n][1].wait_recv()
        src = buffer.at[t_y, halves[n]]
        return send(src, src, i + 3 * n + 2, sib)

    got_ng, ngi = to_group(ng, "ng")
    inner, cubic = 0.7978845608028654, 0.044715

    def feed(tb, n):
        at = halves[n]
        hidden = dot(ng[tb, at], up_w[...], 1, 0) + up_b
        square = hidden * hidden
        bent = jnp.tanh(inner * hidden * (1.0 + cubic * square))
        share = 0.5 * (1.0 + bent)
        acts[tb, at] = (hidden * share).astype(bf16)
        slope = share + 0.5 * hidden * (1.0 - bent * bent) * (
            inner * (1.0 + 3.0 * cubic * square)
        )
        back = (ag[tb, at].astype(f32) * slope).astype(bf16)
        hgs[tb, at] = back
        return dot(back, up_w[...], 1, 1)

    def group_sum(m, term, name, n, one_ready, two_ready):
        i, at = ids(name, 3), halves[n]
        pn_own[m, at] = term(t, n)
        one_ready()
        pn_so[m, 0, at] = term(t_sib, n).astype(bf16)
        one = send(pn_so.at[m, 0, at], pn_si.at[m, 0, at], i, sib)
        two_ready()
        pn_so[m, 1, at] = term(t_ysib, n).astype(bf16)
        two = send(pn_so.at[m, 1, at], pn_si.at[m, 1, at], i + 1, sib)
        mine = term(t_y, n)
        two.wait_recv()
        pn_yo[m, at] = (mine + pn_si[m, 1, at].astype(f32)).astype(bf16)
        three = send(pn_yo.at[m, at], pn_yi.at[m, at], i + 2, dev(1))
        return one, three

    def group_total(m, parts):
        for one, three in parts:
            one.wait_recv()
            three.wait_recv()
        return pn_own[m] + pn_si[m, 0].astype(f32) + pn_yi[m].astype(f32)

    def nothing():
        pass

    back_parts = []
    for n in range(2):
        passed = []
        back_parts.append(
            group_sum(
                0,
                feed,
                f"pn{n}",
                n,
                got_ng[n][0].wait_recv,
                lambda: (
                    passed.append(pass_group(ng, got_ng, ngi, n)),
                    passed[0].wait_recv(),
                ),
            )
        )
    i = ids("mig", 3)
    to = ((t_sib, sib), (t_y, dev(1)), (t_ysib, ysib))
    got_mig = [send(mi.at[at], mig.at[t], i + n, where) for n, (at, where) in enumerate(to)]
    mig[t] = mi[t]
    half_rows = width // 2

    def exchange(buffer, incoming, parts, gathered, base, count, cols, name):
        near, own = count // 2, count // 2 // GROUPS
        i = ids(name, 8)
        src = buffer.at[pl.ds(base + (1 - x) * near, near), cols]
        got = send(src, incoming, i, dev(2))
        yield
        got.wait_recv()
        mine = buffer[pl.ds(base + x * near, near), cols].astype(f32) + incoming[...].astype(f32)
        incoming[...] = mine.astype(bf16)
        beside = ((z + 1 - 2 * (z % 2)) * 2 + x, t)
        got = []
        for n in range(2):
            src = incoming.at[pl.ds((n * 2 + 1 - z % 2) * own, own)]
            got.append(send(src, parts.at[n], i + 1 + n, beside))
        yield
        for n in range(2):
            got[n].wait_recv()
            src = incoming.at[pl.ds((n * 2 + z % 2) * own, own)]
            src[...] = (src[...].astype(f32) + parts[n].astype(f32)).astype(bf16)
        src = incoming.at[pl.ds(((z + 2) % 4) * own, own)]
        got = send(src, parts.at[2], i + 3, zdev(2))
        yield
        got.wait_recv()
        mine = incoming[pl.ds(z * own, own), :].astype(f32) + parts[2].astype(f32)

        def place(d):
            return gathered.at[pl.ds(base + x * near + d * own, own), cols]

        src = place(z)
        src[...] = mine.astype(bf16)
        got = send(src, src, i + 4, zdev(2))
        yield
        got.wait_recv()
        got = [send(place(d), place(d), i + 5 + n, beside) for n, d in enumerate((z, (z + 2) % 4))]
        yield
        for copy in got:
            copy.wait_recv()
        src = gathered.at[pl.ds(base + x * near, near), cols]
        got = send(src, src, i + 7, dev(2))
        yield
        got.wait_recv()
        yield

    wide = width // 2
    paths = {}

    def weight_piece(name, m, n, left, right):
        cols = pl.ds(n * wide, wide)
        upper = right[:, :, n * wide : (n + 1) * wide].reshape(line, wide)
        grad = dot(left[...].reshape(line, width), upper, 0, 0)
        mbuf[m * width : (m + 1) * width, n * wide : (n + 1) * wide] = grad.astype(bf16)
        incoming = msi.at[pl.ds(m * half_rows, half_rows), cols]
        parts = mz.at[m, :, :, cols]
        paths[name] = exchange(mbuf, incoming, parts, mgat, m * width, width, cols, name)
        next(paths[name])

    sbx = ids("sb", 12)
    rsi_at = ids("rs", 9)
    dq = ot
    kept = {}

    def backward(i, carry):
        h, r = i // CHIPS, i % CHIPS
        away, upper = 1 - r // 2, 1 - r % 2
        last = h // (per - 1)
        ks = (2 * upper + 1, 2 * upper)
        chunks = [chip_of(k) * 2 + (c + away) % 2 for k in ks]
        factors = [jnp.exp(tops[h, chunk] - lse[h]) for chunk in chunks]
        scaled = [(dos[h].astype(f32) * factor).astype(bf16) for factor in factors]
        prob_grads = [dot(kvall[h, chunk], d, 1, 0) for chunk, d in zip(chunks, scaled)]
        value_parts = [dot(expd[h, chunk], d, 1, 1) for chunk, d in zip(chunks, scaled)]
        parts = []
        for n, chunk in enumerate(chunks):
            weight = expd[h, chunk].astype(f32)
            score_grad = (weight * (prob_grads[n] - delta[h] * factors[n])).astype(bf16)
            dq[h] = dq[h] + dot(kvall[h, chunk], score_grad, 0, 0)
            parts.append(dot(score_grad, qd[h], 1, 0) + value_parts[n])
        overs = [remote(sbo.at[k], sbi.at[h, k], sbx + h * CHIPS + k, sib) for k in ks]

        @pl.when((away == 1) & (h > 0))
        def _():
            for k in ks:
                remote(sbo.at[k], sbi.at[h, k], sbx + (h - 1) * CHIPS + k, sib).wait_send()

        @pl.when(away == 1)
        def _():
            for n, k in enumerate(ks):
                sbo[k] = parts[n].astype(bf16)
                overs[n].start()

        @pl.when((away == 0) & (h > 0))
        def _():
            i = rsi_at + (h - 1) * 3 + upper
            remote(rso.at[upper], rsi.at[h, upper], i, sib).wait_send()

        @pl.when(away == 0)
        def _():
            overs[0].wait_recv()
            rso[upper] = (parts[0] + sbi[h, ks[0]].astype(f32)).astype(bf16)
            i = rsi_at + h * 3 + upper
            remote(rso.at[upper], rsi.at[h, upper], i, dev(1 + 2 * upper * last)).start()
            overs[1].wait_recv()
            both = parts[1] + sbi[h, ks[1]].astype(f32)

            @pl.when(upper == 0)
            def _():
                dkv[h] = both

            @pl.when(upper == 1)
            def _():
                rsx_out[h] = both.astype(bf16)

            @pl.when((upper == 1) & (last == 1))
            def _():
                remote(rsx_out.at[h], rsx_in.at[h], rsi_at + h * 3 + 2, dev(2)).start()

        return carry

    def backward_from(first, last):
        lax.fori_loop(first, last, backward, 0)

    def relay(h):
        remote(rso.at[1], rsi.at[h, 1], rsi_at + h * 3 + 1, sib).wait_recv()
        rsx_out[h] = (rsx_out[h].astype(f32) + rsi[h, 1].astype(f32)).astype(bf16)
        return send(rsx_out.at[h], rsx_in.at[h], rsi_at + h * 3 + 2, dev(2))

    def keys_back(h, out, b):
        remote(rso.at[0], rsi.at[h, 0], rsi_at + h * 3, sib).wait_recv()
        across[h].wait_recv()
        total = dkv[h] + (rsi[h, 0].astype(f32) + rsx_in[h].astype(f32))
        if h == per - 1:
            remote(rso.at[1], rsi.at[h, 1], rsi_at + h * 3 + 1, sib).wait_recv()
            total = total + rsi[h, 1].astype(f32)
        for zb in range(GROUPS):
            tile = total[zb * rows : (zb + 1) * rows, :]
            back = jnp.where(low_half, turn_back(tile, cosb[zb], sinb[zb]), tile)
            out[zb, :, b : b + 2 * head] = back.astype(bf16)

    def queries_back(one, two, out, b):
        flat = jnp.concatenate([one, two], axis=0).T * scale
        for zb in range(GROUPS):
            tile = flat[zb * rows : (zb + 1) * rows, :]
            out[zb, :, b : b + 2 * head] = turn_back(tile, cosb[zb], sinb[zb]).astype(bf16)

    def scatter_rows(out, into, name):
        i = ids(name, 3)
        got = [send(out.at[(z + k) % 4], into.at[z], i + k - 1, zdev(k)) for k in (1, 2, 3)]
        into[z] = out[z]
        return got

    def projection(out, mine, other, summed, incoming, gathered, name):
        grad = dot(nl[...].reshape(line, width), out[...].reshape(line, out.shape[2]), 0, 0)
        for n in range(2 * CHIPS):
            mine[n % 2, n // 2] = grad[n * shard : (n + 1) * shard, :].astype(bf16)
        i = ids(name, 13)
        got = send(mine.at[1 - c], other, i, sib)
        yield
        got.wait_recv()
        summed[...] = (mine[c].astype(f32) + other[...].astype(f32)).astype(bf16)
        got = [send(summed.at[chip_of(k)], incoming.at[k - 1], i + k, dev(k)) for k in (1, 2, 3)]
        yield
        for copy in got:
            copy.wait_recv()
        whole = summed[chip].astype(f32)
        for k in range(3):
            whole = whole + incoming[k].astype(f32)
        gathered[z, chip, c] = whole.astype(bf16)
        src = gathered.at[z, chip, c]
        got = [send(src, src, i + 3 + k, zdev(k)) for k in (1, 2, 3)]
        yield
        for copy in got:
            copy.wait_recv()
        src = gathered.at[:, chip, c]
        over_y = send(src, src, i + 7, dev(1))
        over_x = send(src, src, i + 8, dev(2))
        last = [send(src, src, i + 9, sib)]
        yield
        over_x.wait_recv()
        src = gathered.at[:, chip_of(2), c]
        both = send(src, src, i + 10, dev(1))
        last.append(send(src, src, i + 11, sib))
        yield
        over_y.wait_recv()
        src = gathered.at[:, chip_of(1), c]
        last.append(send(src, src, i + 12, sib))
        both.wait_recv()
        src = gathered.at[:, chip_of(3), c]
        last.append(send(src, src, ids(name + "x", 1), sib))
        yield
        for copy in last:
            copy.wait_recv()
        yield

    across = {}
    copies = []

    def write(src, dst):
        copies.append(pltpu.make_async_copy(src, dst, ls.at[len(copies)]))
        copies[-1].start()

    def second_norm_back():
        n2g = group_total(0, back_parts)
        sent = got_kv + got_q + got_mix
        for copy in sent:
            copy.wait_send()
        pending[:] = [copy for copy in pending if not any(copy is other for other in sent)]
        normal = normal2[...]
        middle = normalise_back(n2g * (gain2 * (1.0 + scale2)), normal, spread2[...])
        middle = middle + cot_ref[...].astype(f32)
        bgg[t] = (middle * gate1).astype(bf16)
        for g in range(GROUPS):
            mtb[g] = dot(out_w[g * gw : (g + 1) * gw, :], bgg[t], 1, 1).astype(bf16)
        i = ids("do", 3)
        kept["do"] = [send(mtb.at[(z + k) % 4], doi.at[z], i + k - 1, zdev(k)) for k in (1, 2, 3)]
        kept["bg"] = group_start(bgg, "bg")
        doi[z] = mtb[z]
        normal2[...] = middle
        vec[3:4, :] = column_sum(middle * branch[...])
        vec[4:5, :] = column_sum(n2g)
        vec[5:6, :] = column_sum(n2g * normal)

    def result_term(tb, n):
        return dot(acts[tb, halves[n]], down_w[...], 1, 0)

    def result_start():
        kept["res"] = [
            group_sum(1, result_term, f"res{n}", n, nothing, nothing) for n in range(2)
        ]
        vec[8:9, :] = column_sum(hgs[...].reshape(line, width).astype(f32))
        vec[9:16, :] = jnp.zeros((7, width), f32)
        vec[7:8, :] = column_sum(rg[t].astype(f32))

    def result_end():
        result = group_total(1, kept["res"]) + down_b
        o_out[...] = (start[...] + gate2 * result).astype(bf16)
        vec[6:7, :] = column_sum(cot_ref[...].astype(f32) * result)

    def branch_pass():
        one, two, i = kept["bg"]
        kept["bg3"] = group_pass(bgg, two, i)

    def out_weight_grad():
        kept["bg"][0].wait_recv()
        kept["bg3"].wait_recv()
        for copy in got_mig:
            copy.wait_recv()
        grad = dot(mig[0], bgg[0], 1, 0)
        for n in range(1, tp_size):
            grad = grad + dot(mig[n], bgg[n], 1, 0)
        wbuf[0:gw, :] = grad[:, 0:wide].astype(bf16)
        wbuf[gw : 2 * gw, :] = grad[:, wide:width].astype(bf16)
        paths["o"] = exchange(wbuf, wsi, wz, wgt, 0, 2 * gw, pl.ds(0, wide), "wo")
        next(paths["o"])

    def backward_first():
        for copy in kept["do"]:
            copy.wait_recv()
        for h in range(per):
            dos[h, 0:head, :] = jnp.zeros((head, line), bf16)
            for zb in range(GROUPS):
                dos[h, head : 2 * head, zb * rows : (zb + 1) * rows] = doi[
                    zb, h * head : (h + 1) * head, :
                ]
            delta[h] = column_sum(
                dos[h, head : 2 * head, :].astype(f32) * ot[h, head : 2 * head, :]
            )
        dq[...] = jnp.zeros_like(dq)
        backward_from(0, 4)

    def backward_last():
        backward_from(10, 12)
        across[2] = remote(rsx_out.at[per - 1], rsx_in.at[per - 1], rsi_at + per * 3 - 1, dev(2))
        pending.append(across[2])

    def relay_of(h):
        across[h] = relay(h)

    kept["nl"] = got_nl

    def portion_one():
        for copy in kept.pop("nl", []):
            copy.wait_recv()
        keys_back(0, pg1, kv_at[0])
        keys_back(1, pg1, kv_at[1])
        queries_back(dq[0, 0:head, :], dq[1, 0:head, :], pg1, q_at[0])
        kept["pg1"] = scatter_rows(pg1, pgi1, "pg1")
        paths["w1"] = projection(pg1, dwb1, dws1, dwc1, dwr1, wg1, "w1")
        next(paths["w1"])

    def portion_two():
        for copy in kept.pop("nl", []):
            copy.wait_recv()
        keys_back(2, pg2, kv_at[2] - split)
        queries_back(dq[2, 0:head, :], jnp.zeros((head, line), f32), pg2, q_at[1] - split)
        kept["pg2"] = scatter_rows(pg2, pgi2, "pg2")
        paths["w2"] = projection(pg2, dwb2, dws2, dwc2, dwr2, wg2, "w2")
        next(paths["w2"])

    def first_norm_back():
        for copy in kept["pg1"]:
            copy.wait_recv()
        n1g = dot(pgi1[0], whm[0, :, 0:split], 1, 1)
        for g in range(1, GROUPS):
            n1g = n1g + dot(pgi1[g], whm[g, :, 0:split], 1, 1)
        for copy in kept["pg2"]:
            copy.wait_recv()
        for g in range(GROUPS):
            n1g = n1g + dot(pgi2[g], whm[g, :, split : split + 4 * head], 1, 1)
        normal = normal1[...]
        vec[1:2, :] = column_sum(n1g)
        vec[2:3, :] = column_sum(n1g * normal)
        grad = normalise_back(n1g * (gain1 * (1.0 + scale1)), normal, spread1[...])
        grad = grad + normal2[...]
        o_in[...] = grad
        vec[0:1, :] = column_sum(grad * mcol[...])
        vpl[chip] = vec[...]
        i = ids("vp", 3)
        kept["vp"] = [send(vec, vpl.at[chip], i + k - 1, dev(k)) for k in (1, 2, 3)]

    def vectors_plane():
        for copy in kept["vp"]:
            copy.wait_recv()
        vzs[z, 0:8] = (vpl[0, 0:8] + vpl[1, 0:8]) + (vpl[2, 0:8] + vpl[3, 0:8])
        vzs[z, 8:16] = vpl[y, 8:16] + vpl[2 + y, 8:16]
        i = ids("vz", 3)
        kept["vz"] = [send(vzs.at[z], vzs.at[z], i + k - 1, zdev(k)) for k in (1, 2, 3)]

    def vectors_line():
        for copy in kept["vz"]:
            copy.wait_recv()
        vco[c] = (vzs[0] + vzs[1]) + (vzs[2] + vzs[3])
        kept["vc"] = send(vco.at[c], vco.at[c], ids("vc", 1), sib)

    def vectors_end():
        kept["vc"].wait_recv()
        sums = vco[0] + vco[1]
        o_vec[0:1, :] = sums[0:1, :]
        o_vec[1:2, :] = sums[2:3, :] * (1.0 + scale1)
        o_vec[2:3, :] = sums[5:6, :] * (1.0 + scale2)
        o_vec[3:4, :] = sums[7:8, :]
        o_vec[4:5, :] = vco[c, 8:9, :]
        o_vec[5:8, :] = jnp.zeros((3, width), f32)
        o_vec[8:9, :] = sums[1:2, :]
        o_vec[9:10, :] = sums[2:3, :] * gain1
        o_vec[10:11, :] = sums[3:4, :]
        o_vec[11:12, :] = sums[4:5, :]
        o_vec[12:13, :] = sums[5:6, :] * gain2
        o_vec[13:14, :] = sums[6:7, :]
        o_vec[14:16, :] = jnp.zeros((2, width), f32)

    def out_start():
        og[t] = wgt[...]
        kept["og"] = group_start(og, "og")

    def out_pass():
        one, two, i = kept["og"]
        kept["og3"] = group_pass(og, two, i)

    def out_end():
        kept["og"][0].wait_recv()
        kept["og3"].wait_recv()
        write(og, o_ow)

    finished = []

    def step_of(path, last):
        def run():
            next(paths[path])
            if not last:
                return
            if path == "w1":
                write(wg1, o_qkv1)
            elif path == "w2":
                write(wg2, o_qkv2)
            elif path != "o":
                finished.append(path[0])
                if finished.count(path[0]) == 2:
                    at = pl.ds(0 if path[0] == "u" else width, width)
                    write(mgat.at[at], o_mlp.at[at])

        return run

    steps = {
        "d1_dw": lambda: weight_piece("d1", 1, 0, acts, rg),
        "d2_dw": lambda: weight_piece("d2", 1, 1, acts, rg),
        "u1_dw": lambda: weight_piece("u1", 0, 0, ng, hgs),
        "u2_dw": lambda: weight_piece("u2", 0, 1, ng, hgs),
        "ln2b": second_norm_back,
        "res": result_start,
        "resfin": result_end,
        "bgp": branch_pass,
        "wo": out_weight_grad,
        "L1": backward_first,
        "L2": lambda: backward_from(4, 8),
        "L3a": lambda: backward_from(8, 10),
        "L3b": backward_last,
        "rel0": lambda: relay_of(0),
        "rel1": lambda: relay_of(1),
        "por1": portion_one,
        "por2": portion_two,
        "n1g": first_norm_back,
        "v1": vectors_plane,
        "v2": vectors_line,
        "v3": vectors_end,
        "og": out_start,
        "og2": out_pass,
        "og3": out_end,
    }
    for path in ("d1", "d2", "u1", "u2", "o"):
        for part in ("1", "2", "3", "4", "5", "end"):
            steps[path + "_" + part] = step_of(path, part == "end")
    for path in ("w1", "w2"):
        for part in ("a", "b", "c", "d", "e", "end"):
            steps[path + "_" + part] = step_of(path, part == "end")
    for batch in ORDER:
        for name in batch.split():
            steps[name]()
    for copy in pending:
        copy.wait_send()
    for k in range(CHIPS):
        remote(kvall.at[:, 0], kvall.at[:, 0], kdi + k, sib).wait_send()

    def drain(i, carry):
        remote(sbo.at[i], sbi.at[0, 0], sbx + (per - 1) * CHIPS + i, sib).wait_send()
        return carry

    lax.fori_loop(0, CHIPS, drain, 0)

    def drain(i, carry):
        remote(rso.at[i], rsi.at[0, 0], rsi_at + (per - 1) * 3 + i, sib).wait_send()
        return carry

    lax.fori_loop(0, 2, drain, 0)
    for copy in copies:
        copy.wait()


def rope_constants(length, rows, head):
    half = head // 2
    inverse = np.exp(np.float32(-math.log(10000.0)) * np.arange(half, dtype=np.float32) / half)
    angles = np.arange(length, dtype=np.float32)[:, None] * inverse.astype(np.float32)[None, :]
    angles = np.tile(angles, (1, 4)).astype(np.float64)
    shape = (length // rows, rows, 2 * head)
    return (
        jnp.asarray(np.cos(angles).astype(np.float32).reshape(shape)),
        jnp.asarray(np.sin(angles).astype(np.float32).reshape(shape)),
    )


def fused_device(
    seq_size,
    tp_size,
    tokens,
    cotangent,
    prefix_length,
    mask_flags,
    timestep,
    mask_embed,
    ln1_gain,
    ln2_gain,
    ada_weight,
    ada_bias,
    qkv_weight,
    out_weight,
    up_weight,
    up_bias,
    down_weight,
    down_bias,
):
    rows, width = tokens.shape
    head = width // HEADS
    per = HEADS // GROUPS
    gw = per * head
    line = GROUPS * rows
    packed = (per * 2 + 4) * head
    shard = width // (2 * CHIPS)
    cond = ada_weight.shape[0]
    cosine, sine = rope_constants(rows * seq_size * tp_size, rows, head)
    V = pltpu.VMEM
    vmem = pl.BlockSpec(memory_space=pltpu.VMEM)
    hbm = pl.BlockSpec(memory_space=pl.ANY)
    parts = (6 * head, 4 * head)
    outs = pl.pallas_call(
        functools.partial(fused_kernel, tp_size),
        out_shape=[
            jax.ShapeDtypeStruct((rows, width), bf16),
            jax.ShapeDtypeStruct((rows, width), f32),
            jax.ShapeDtypeStruct((16, width), f32),
            jax.ShapeDtypeStruct((GROUPS, CHIPS, 2, shard, parts[0]), bf16),
            jax.ShapeDtypeStruct((GROUPS, CHIPS, 2, shard, parts[1]), bf16),
            jax.ShapeDtypeStruct((tp_size, 2 * gw, width // 2), bf16),
            jax.ShapeDtypeStruct((2 * width, width), bf16),
        ],
        in_specs=[pl.BlockSpec(memory_space=pltpu.SMEM)] * 2
        + [vmem] * 9
        + [hbm] * 7,
        out_specs=[vmem] * 3 + [hbm] * 4,
        scratch_shapes=[
            V((width, width), bf16),
            V((width, width), bf16),
            V((width, width), bf16),
            V((8, width), f32),
            V((rows, width), f32),
            V((rows, width), f32),
            V((rows, 1), f32),
            V((rows, width), f32),
            V((rows, 1), f32),
            V((rows, width), f32),
            V((rows, 1), f32),
            V((GROUPS, rows, width), bf16),
            V((GROUPS, 2, rows, 2 * head), bf16),
            V((GROUPS, width, packed), bf16),
            V((GROUPS, rows, 2 * head), f32),
            V((GROUPS, rows, 2 * head), f32),
            V((per, 2 * CHIPS, line, 2 * head), bf16),
            V((per, line, 2 * head), bf16),
            V((per, 2 * CHIPS, line, line), bf16),
            V((per, 2 * CHIPS, 1, line), f32),
            V((per, 1, line), f32),
            V((per, 1, line), f32),
            V((per, 2 * head, line), f32),
            V((per, 1, line), f32),
            V((per, 1, line), f32),
            V((GROUPS, gw, rows), bf16),
            V((GROUPS, gw, rows), bf16),
            V((tp_size, rows, width), bf16),
            V((tp_size, rows, width), bf16),
            V((tp_size, rows, width), bf16),
            V((tp_size, rows, width), bf16),
            V((tp_size, rows, width), bf16),
            V((2, rows, width), f32),
            V((2, 2, rows, width), bf16),
            V((2, 2, rows, width), bf16),
            V((2, rows, width), bf16),
            V((2, rows, width), bf16),
            V((tp_size, rows, width), bf16),
            V((tp_size, gw, rows), bf16),
            V((GROUPS, gw, rows), bf16),
            V((per, 2 * head, line), bf16),
            V((CHIPS, line, 2 * head), bf16),
            V((per, CHIPS, line, 2 * head), bf16),
            V((2, line, 2 * head), bf16),
            V((per, 2, line, 2 * head), bf16),
            V((per, line, 2 * head), bf16),
            V((per, line, 2 * head), bf16),
            V((per, line, 2 * head), f32),
        ]
        + [V((GROUPS, rows, n), bf16) for n in parts for _ in range(2)]
        + [
            V(shape, bf16)
            for n in parts
            for shape in (
                (2, CHIPS, shard, n),
                (CHIPS, shard, n),
                (CHIPS, shard, n),
                (3, shard, n),
                (GROUPS, CHIPS, 2, shard, n),
            )
        ]
        + [
            V((2 * gw, width // 2), bf16),
            V((gw, width // 2), bf16),
            V((3, gw // GROUPS, width // 2), bf16),
            V((2 * gw, width // 2), bf16),
            V((tp_size, 2 * gw, width // 2), bf16),
            V((2 * width, width), bf16),
            V((width, width), bf16),
            V((2, 3, shard, width), bf16),
            V((2 * width, width), bf16),
            V((16, width), f32),
            V((CHIPS, 16, width), f32),
            V((GROUPS, 16, width), f32),
            V((2, 16, width), f32),
            pltpu.SemaphoreType.DMA((192,)),
            pltpu.SemaphoreType.DMA((192,)),
            pltpu.SemaphoreType.DMA((20,)),
        ],
        compiler_params=pltpu.CompilerParams(
            collective_id=0, has_side_effects=True, vmem_limit_bytes=VMEM_LIMIT
        ),
    )(
        prefix_length,
        timestep,
        mask_flags,
        mask_embed,
        ln1_gain,
        ln2_gain,
        up_bias,
        down_bias,
        ada_bias,
        tokens,
        cotangent,
        cosine,
        sine,
        ada_weight,
        qkv_weight,
        out_weight,
        up_weight,
        down_weight,
    )
    output, input_grad, sums, first, second, out_parts, mlp_parts = outs
    steps = 2 * CHIPS
    vector = jax.ShapeDtypeStruct((width,), f32)
    whole = pl.BlockSpec((width,), lambda n: (0,))

    def some(*shape):
        return jax.ShapeDtypeStruct(shape, f32)

    def rows_of(count, columns, skip=0):
        return pl.BlockSpec((count, columns), lambda n: (n + skip, 0))

    return pl.pallas_call(
        functools.partial(finish_kernel, per, head),
        grid=(steps,),
        out_shape=[
            jax.ShapeDtypeStruct((rows, width), bf16),
            some(rows, width),
            vector,
            vector,
            vector,
            some(cond, 6 * width),
            some(6 * width),
            some(width, 3 * width),
            some(width, width),
            some(width, width),
            vector,
            some(width, width),
            vector,
        ],
        in_specs=[
            pl.BlockSpec(memory_space=pltpu.SMEM),
            pl.BlockSpec((16, width), lambda n: (0, 0)),
            rows_of(rows // steps, width),
            rows_of(rows // steps, width),
            pl.BlockSpec((GROUPS, 1, shard, parts[0]), lambda n: (0, n, 0, 0)),
            pl.BlockSpec((GROUPS, 1, shard, parts[1]), lambda n: (0, n, 0, 0)),
            pl.BlockSpec((1, 2, shard, width // 2), lambda n: (n // 2, 0, n % 2, 0)),
            rows_of(shard, width),
            rows_of(shard, width, steps),
        ],
        out_specs=[
            rows_of(rows // steps, width),
            rows_of(rows // steps, width),
            whole,
            whole,
            whole,
            rows_of(cond // steps, 6 * width),
            pl.BlockSpec((6 * width,), lambda n: (0,)),
            rows_of(shard, 3 * width),
            rows_of(shard, width),
            rows_of(shard, width),
            whole,
            rows_of(shard, width),
            whole,
        ],
    )(
        timestep,
        sums,
        output,
        input_grad,
        first.reshape(GROUPS, steps, shard, parts[0]),
        second.reshape(GROUPS, steps, shard, parts[1]),
        out_parts.reshape(tp_size, 2, gw, width // 2),
        mlp_parts,
        mlp_parts,
    )


def solution(mesh):
    seq_size, tp_size = mesh.shape["seq"], mesh.shape["tp"]
    small = seq_size == 2 * GROUPS and tp_size == CHIPS
    in_specs = (
        P(("seq", "tp"), None),
        P(("seq", "tp"), None),
        P(),
        P(("seq", "tp")),
        P(),
        P(),
        P(),
        P(),
        P(),
        P(),
        P(),
        P(),
        P(None, "tp"),
        P("tp"),
        P("tp", None),
        P(),
    )
    out_specs = (
        P(("seq", "tp"), None),
        P(("seq", "tp"), None),
        P(),
        P(),
        P(),
        P(),
        P(),
        P(),
        P(),
        P(None, "tp"),
        P("tp"),
        P("tp", None),
        P(),
    )
    return jax.shard_map(
        functools.partial(fused_device, seq_size, tp_size) if small else per_device,
        mesh=mesh, in_specs=in_specs, out_specs=out_specs, check_vma=False
    )
```
